32 devices in a mesh: rows: 8 (over y, x, core), seq: 4 (over z).
Axes of the slice: x: 2, y: 2, z: 4, core: 2. Of those that a mesh axis runs over, the one named last changes fastest.
Arguments:
- block_input: bfloat16 [24, 512, 512], P('rows', 'seq'), may hold values from -6 to 6
- cotangent: bfloat16 [24, 512, 512], P('rows', 'seq'), may hold values from -6 to 6
- gain_attn: float32 [512], replicated, may hold values from 0.5 to 1.5
- w_query: bfloat16 [512, 512], replicated, may hold values from -0.0625 to 0.0625
- w_key: bfloat16 [512, 512], replicated, may hold values from -0.25 to 0.25
- w_value: bfloat16 [512, 512], replicated, may hold values from -0.25 to 0.25
- w_out: bfloat16 [512, 512], replicated, may hold values from -1 to 1
- gain_mlp: float32 [512], replicated, may hold values from 0.5 to 1.5
- w_inner: bfloat16 [512, 2048], replicated, may hold values from -0.25 to 0.25
- outer_weight: bfloat16 [2048, 512], replicated, may hold values from -0.125 to 0.125
- bias_table: float32 [32, 8], replicated, may hold values from -6 to 6
- lengths: int32 [24, 4], P('rows'), may hold values from 1 to 385, 512 in all within a row
- observed: int32 [24, 512], P('rows', 'seq'), may hold values 0 or 1
Outputs:
- block_output: bfloat16 [24, 512, 512], P('rows', 'seq')
- input_grad: bfloat16 [24, 512, 512], P('rows', 'seq')
- grad_gain_attn: float32 [512], replicated
- grad_query: float32 [512, 512], replicated
- grad_key: float32 [512, 512], replicated
- grad_value: float32 [512, 512], replicated
- grad_out: float32 [512, 512], replicated
- grad_gain_mlp: float32 [512], replicated
- grad_inner: float32 [512, 2048], replicated
- grad_outer: float32 [2048, 512], replicated
- grad_table: float32 [32, 8], replicated
The draws below stay inside these ranges and needn't reach their ends.
Inputs may be any that keep to these rules, and one draw needn't show every extreme that they name: The 4 lengths of a row sum to 512; the largest of each row is 385.
All inputs are finite; a program needn't handle non-finite values. No bound on the sum of `observed` on one device may be relied on, other than what follows from the above.
Results may differ from the reference program's by a relative error of at most 0.014.
Values may be sent and summed in bfloat16 or wider, within the bound.
No kernel may reach another device: no remote copies, remote signals or barrier semaphores. Data moves between devices by JAX's collectives and lax.ppermute only.
A program may use at most 128 MiB of HBM per device.

```python
import math
import jax
import jax.numpy as jnp
import numpy as np
from jax import lax

D = 512
FF = 2048
H = 8
HD = 64
BUCKETS = 32
PACKED_LENGTH = 512
SEGS = 4
ROWS = 24
MOST = 385


def touch_ends(values, key, smallest, high):
    index_at = [jax.random.randint(jax.random.fold_in(key, axis), (), 0, length) for axis, length in enumerate(values.shape)]
    main_axis = values.shape.index(max(values.shape))
    neighbour = index_at[:main_axis] + [(index_at[main_axis] + 1) % values.shape[main_axis]] + index_at[main_axis + 1:]
    return values.at[tuple(index_at)].set(smallest).at[tuple(neighbour)].set(high)


def level_of(rng, shape, shards, least, top_value):
    loudness = 1.0
    for axis_at, blocks in shards:
        heights = jax.random.uniform(jax.random.fold_in(jax.random.fold_in(rng, 6), axis_at), (blocks,), jnp.float32, least / len(shards), top_value / len(shards))
        loudness = loudness * jnp.repeat(jnp.exp(heights), shape[axis_at] // blocks).reshape((-1,) + (1,) * (len(shape) - 1 - axis_at))
    return loudness


def split_up(number_of, total, reach, lean):
    weights = [(1 << 20) // math.isqrt(standing ** lean) + 1 for standing in range(2, number_of + 1)]
    surplus, counts = total - reach - (number_of - 1), [1] * (number_of - 1)
    while surplus > 0:
        free = [i for i in range(number_of - 1) if counts[i] < reach]
        whole, budget = sum([weights[i] for i in free]), surplus
        for i in free:
            more = min(reach - counts[i], max(1, budget * weights[i] // whole), surplus)
            counts[i] = counts[i] + more
            surplus = surplus - more
    return np.array([reach] + counts)


def uneven_parts(stream_key, amount, total, most, lean):
    if amount == 2:
        one = jax.random.randint(stream_key, (), max(1, total - most), min(most, total - 1) + 1)
        return jnp.stack([one, total - one])
    sizes = jnp.asarray(split_up(amount, total, most, lean), jnp.int32)
    twos = (amount - 1) // 2
    donor, taker = sizes[1:1 + 2 * twos:2], sizes[2:2 + 2 * twos:2]
    margin = jnp.minimum(donor - 1, most - taker)
    shifted = jax.random.randint(jax.random.fold_in(stream_key, 1), (twos,), 0, 1 << 20) % (margin + 1)
    sizes = sizes.at[1:1 + 2 * twos:2].set(donor - shifted).at[2:2 + 2 * twos:2].set(taker + shifted)
    return sizes[jax.random.permutation(jax.random.fold_in(stream_key, 2), amount)]


def centred(stream_key, dims, spread, most, shards=(), held_as=jnp.bfloat16):
    array = spread * jax.random.normal(stream_key, dims, jnp.float32)
    if shards:
        array = array * level_of(stream_key, dims, shards, -0.22, 0.18)
    return jnp.clip(array, -most, most).astype(held_as)


def setup_inputs(seed: int = 0) -> dict:
    splits = jax.random.split(jax.random.key(seed), 14)
    return {
        "block_input": centred(splits[0], (ROWS, PACKED_LENGTH, D), 1.0, 6.0, ((0, 8), (1, 4))),
        "cotangent": centred(splits[1], (ROWS, PACKED_LENGTH, D), 1.0, 6.0, ((0, 8), (1, 4))),
        "gain_attn": jnp.clip(1.0 + 0.1 * jax.random.normal(splits[2], (D,), jnp.float32), 0.5, 1.5),
        "w_query": centred(splits[3], (D, D), (16 * D) ** -0.5, 0.0625),
        "w_key": centred(splits[4], (D, D), D ** -0.5, 0.25),
        "w_value": centred(splits[5], (D, D), D ** -0.5, 0.25),
        "w_out": centred(splits[6], (D, D), (D // 16) ** -0.5, 1.0),
        "gain_mlp": jnp.clip(1.0 + 0.1 * jax.random.normal(splits[7], (D,), jnp.float32), 0.5, 1.5),
        "w_inner": centred(splits[8], (D, FF), D ** -0.5, 0.25),
        "outer_weight": centred(splits[9], (FF, D), FF ** -0.5, 0.125),
        "bias_table": centred(splits[10], (BUCKETS, H), 1.0, 6.0, (), jnp.float32),
        "lengths": jax.vmap(lambda own: uneven_parts(own, SEGS, PACKED_LENGTH, MOST, 1))(jax.random.split(splits[11], ROWS)).reshape((ROWS, SEGS)).astype(jnp.int32),
        "observed": touch_ends((jax.random.randint(splits[12], (ROWS, PACKED_LENGTH), 0, 8) < 7).astype(jnp.int32), jax.random.fold_in(splits[12], 1), 0, 1),
    }


EPSILON = 1e-06
BUCKET_EDGES = (12, 16, 23, 32, 46, 64, 91)
EXACT_MATMUL = lax.Precision.HIGHEST

@jax.custom_vjp
def low(v):
    return lax.optimization_barrier(v.astype(jnp.bfloat16)).astype(jnp.float32)

@jax.custom_vjp
def low_back(v):
    return v

def low_keep(v):
    return (low(v), None)

def low_pass(kept, grad):
    return (grad,)

def back_keep(v):
    return (v, None)

def back_low(kept, grad):
    return (low(grad),)
low.defvjp(low_keep, low_pass)
low_back.defvjp(back_keep, back_low)

def bucket_of(relative):
    distance = jnp.abs(relative)
    beyond = jnp.full(distance.shape, 8, jnp.int32)
    for edge_value in BUCKET_EDGES:
        beyond = beyond + (distance >= edge_value).astype(jnp.int32)
    near = jnp.where(distance < 8, distance, beyond)
    return jnp.where(relative > 0, 16, 0).astype(jnp.int32) + near

def segment_ids(lengths, total_len):
    segment_ends = jnp.cumsum(lengths, -1).astype(jnp.int32)
    places = jnp.arange(total_len, dtype=jnp.int32)
    return lax.optimization_barrier(jnp.sum((segment_ends[..., None, :] <= places[:, None]).astype(jnp.int32), -1))

def project(left_side, right_side):
    return jnp.einsum('rtd,de->rte', left_side, right_side, precision=EXACT_MATMUL)

def norm_apply(values, gain):
    inv_rms = lax.rsqrt(lax.optimization_barrier(jnp.mean(values * values, -1, keepdims=True)) + EPSILON)
    return values * inv_rms * gain

def encoder_layer(block_f, gain_attn, w_query, w_key, w_value, w_out, gain_mlp, w_inner, outer_weight, bucket_bias_lookup, lengths, observed):
    row_count = block_f.shape[0]
    normed = low(norm_apply(block_f, gain_attn))
    queries = low_back(low(project(normed, w_query))).reshape(row_count, PACKED_LENGTH, H, HD)
    keys = low_back(low(project(normed, w_key))).reshape(row_count, PACKED_LENGTH, H, HD)
    values = low_back(low(project(normed, w_value))).reshape(row_count, PACKED_LENGTH, H, HD)
    scores = jnp.einsum('rqhe,rkhe->rhqk', queries, keys, precision=EXACT_MATMUL)
    places = jnp.arange(PACKED_LENGTH, dtype=jnp.int32)
    buckets = bucket_of(places[None, :] - places[:, None])
    relative_position_bias = jnp.transpose(bucket_bias_lookup[buckets], (2, 0, 1))
    segments = segment_ids(lengths, PACKED_LENGTH)
    allowed = (segments[:, :, None] == segments[:, None, :]) & ((observed[:, None, :] == 1) | (places[:, None] == places[None, :])[None])
    scores = jnp.where(allowed[:, None], low_back(scores + relative_position_bias[None]), -1000000000.0)
    row_top = lax.optimization_barrier(jnp.max(scores, -1, keepdims=True))
    exponent = jnp.exp(scores - row_top)
    weights_soft = exponent / lax.optimization_barrier(jnp.sum(exponent, -1, keepdims=True))
    combined_head_outputs = jnp.einsum('rhqk,rkhe->rqhe', low(weights_soft), values, precision=EXACT_MATMUL).reshape(row_count, PACKED_LENGTH, D)
    attended = low_back(low(combined_head_outputs))
    middle = block_f + low_back(project(attended, w_out))
    normed_mlp = low(norm_apply(middle, gain_mlp))
    inner_pre = low_back(project(normed_mlp, w_inner))
    active = low(jax.nn.gelu(inner_pre, approximate=True))
    return middle + project(active, outer_weight)

def reference(block_input, cotangent, gain_attn, w_query, w_key, w_value, w_out, gain_mlp, w_inner, outer_weight, bias_table, lengths, observed):
    weights = (gain_attn.astype(jnp.float32), w_query.astype(jnp.float32), w_key.astype(jnp.float32), w_value.astype(jnp.float32), w_out.astype(jnp.float32), gain_mlp.astype(jnp.float32), w_inner.astype(jnp.float32), outer_weight.astype(jnp.float32), bias_table.astype(jnp.float32))
    groups = ROWS // 8
    blocks = block_input.astype(jnp.float32).reshape(groups, 8, PACKED_LENGTH, D)
    tangents = cotangent.astype(jnp.float32).reshape(groups, 8, PACKED_LENGTH, D)
    length_groups = lengths.reshape(groups, 8, SEGS)
    mask_groups = observed.reshape(groups, 8, PACKED_LENGTH)

    def advance(totals, items):
        block_now, tangent, length_rows, mask_rows = items

        def forward(block_arg, *params):
            return encoder_layer(block_arg, *params, length_rows, mask_rows)
        output, pullback = jax.vjp(forward, block_now, *weights)
        gradients = pullback(tangent)
        summed = tuple((running + addend for running, addend in zip(totals, gradients[1:])))
        return (summed, (output.astype(jnp.bfloat16), gradients[0].astype(jnp.bfloat16)))
    zero_grads = tuple((jnp.zeros_like(weight_now) for weight_now in weights))
    totals, outputs = lax.scan(advance, zero_grads, (blocks, tangents, length_groups, mask_groups))
    return (outputs[0].reshape(ROWS, PACKED_LENGTH, D), outputs[1].reshape(ROWS, PACKED_LENGTH, D), totals[0], totals[1], totals[2], totals[3], totals[4], totals[5], totals[6], totals[7], totals[8])
```

```python
import functools

import jax
import jax.numpy as jnp
from jax import lax
from jax.experimental import pallas as pl
from jax.experimental.pallas import tpu as pltpu
from jax.sharding import PartitionSpec as P

D = 512
FF = 2048
H = 8
HD = 64
PAIRS = H // 2
BUCKETS = 32
PACKED_LENGTH = 512
EPSILON = 1e-06
BUCKET_EDGES = (12, 16, 23, 32, 46, 64, 91)
SPAN = 2 * PACKED_LENGTH
CHUNKS = 32
HALF = CHUNKS // 2
OUTER_ROWS = FF // CHUNKS
SMALL_ROWS = D // CHUNKS
FF_TILE = 512
MASKED = -1000000000.0
VMEM_LIMIT = 30 * 1024 * 1024
F32 = jnp.float32
BF16 = jnp.bfloat16


def dot(left, right, contract=(1, 0), precision=None):
    return lax.dot_general(
        left,
        right,
        (((contract[0],), (contract[1],)), ((), ())),
        preferred_element_type=F32,
        precision=precision,
    )


def xor_pairs(size, bit):
    return [(i, i ^ bit) for i in range(size)]


def bucket_of(relative):
    distance = jnp.abs(relative)
    beyond = jnp.full(distance.shape, 8, jnp.int32)
    for edge_value in BUCKET_EDGES:
        beyond = beyond + (distance >= edge_value).astype(jnp.int32)
    near = jnp.where(distance < 8, distance, beyond)
    return jnp.where(relative > 0, 16, 0).astype(jnp.int32) + near


def bucket_rows(shape, bucket_axis):
    place_axis = 1 - bucket_axis
    relative = lax.broadcasted_iota(jnp.int32, shape, place_axis) - PACKED_LENGTH
    return (bucket_of(relative) == lax.broadcasted_iota(jnp.int32, shape, bucket_axis)).astype(F32)


def split_heads(pair):
    lane = lax.broadcasted_iota(jnp.int32, pair.shape, 1)
    zero = jnp.zeros_like(pair)
    return jnp.concatenate(
        [jnp.where(lane < HD, pair, zero), jnp.where(lane >= HD, pair, zero)], axis=0
    )


def join_heads(stacked):
    half = stacked.shape[0] // 2
    lane = lax.broadcasted_iota(jnp.int32, (half, stacked.shape[1]), 1)
    return jnp.where(lane < HD, stacked[:half], stacked[half:])


def bias_kernel(place_ref, table_ref, bias_ref, line_ref, *, here, seq):
    line_ref[...] = dot(
        table_ref[...], bucket_rows((BUCKETS, SPAN), 0), (0, 0), lax.Precision.HIGHEST
    )
    me = place_ref[0]
    for block in range(seq):
        offset = ((me ^ block) - me) * here + PACKED_LENGTH - here
        window = line_ref[:, pl.ds(pl.multiple_of(offset, 128), 2 * here)]
        for head in range(H):
            spread = jnp.broadcast_to(window[head : head + 1], (here, 2 * here))
            skewed = pltpu.roll(spread, here, 1, stride=1, stride_axis=0)
            row = (head % 2) * here
            bias_ref[head // 2, row : row + here, block * here : (block + 1) * here] = skewed[
                :, :here
            ]


def attention_kernel(
    place_ref,
    lengths_ref,
    x0_ref,
    x1_ref,
    x2_ref,
    x3_ref,
    seen_ref,
    gain_ref,
    wq_ref,
    wk_ref,
    wv_ref,
    w_out_ref,
    gain_mlp_ref,
    bias_ref,
    *refs,
    row,
    here,
    seq,
):
    (
        normed_mlp_ref,
        attended_ref,
        middle_ref,
        mixed_ref,
        normed_ref,
        q_ref,
        k_ref,
        v_ref,
        p_ref,
    ) = refs[-9:]
    me = place_ref[0]
    own_x = x0_ref[0].astype(F32)
    x = jnp.concatenate(
        [own_x] + [ref[...].astype(F32) for ref in (x1_ref, x2_ref, x3_ref)], axis=0
    )
    inv = lax.rsqrt(jnp.mean(x * x, -1, keepdims=True) + EPSILON)
    normed = (x * inv * gain_ref[...]).astype(BF16)
    normed_ref[0] = normed
    q = dot(normed[:here], wq_ref[...]).astype(BF16)
    k = dot(normed, wk_ref[...]).astype(BF16)
    v = dot(normed, wv_ref[...]).astype(BF16)
    q_ref[0] = q
    k_ref[0] = k
    v_ref[0] = v
    ends = [lengths_ref[row, 0]]
    for part in range(1, lengths_ref.shape[1]):
        ends.append(ends[-1] + lengths_ref[row, part])

    def segment(place):
        total = jnp.zeros(place.shape, jnp.int32)
        for end in ends:
            total = total + (end <= place).astype(jnp.int32)
        return total

    query_place = me * here + lax.broadcasted_iota(jnp.int32, (here, 1), 0)
    lane = lax.broadcasted_iota(jnp.int32, (1, here), 1)
    key_place = jnp.concatenate([(me ^ block) * here + lane for block in range(seq)], axis=1)
    seen = jnp.concatenate([seen_ref[0, block : block + 1] for block in range(seq)], axis=1)
    key_segment = jnp.where(seen == 1, segment(key_place), -1)
    allowed = (segment(query_place) == key_segment) | (query_place == key_place)
    allowed = jnp.concatenate([allowed.astype(jnp.int32)] * 2, axis=0) == 1
    attended = []
    for pair in range(PAIRS):
        lanes = slice(pair * 2 * HD, (pair + 1) * 2 * HD)
        scores = dot(split_heads(q[:, lanes]), k[:, lanes], (1, 1)) + bias_ref[pair]
        scores = jnp.where(allowed, scores, MASKED)
        exponent = jnp.exp(scores - jnp.max(scores, -1, keepdims=True))
        share = 1.0 / jnp.sum(exponent, -1, keepdims=True)
        probs = (exponent * share).astype(BF16)
        p_ref[0, pair] = probs
        mixed = join_heads(dot(probs, v[:, lanes]))
        mixed_ref[0, :, lanes] = mixed
        attended.append(mixed.astype(BF16))
    attended = jnp.concatenate(attended, axis=1)
    attended_ref[0] = attended
    middle = own_x + dot(attended, w_out_ref[...])
    middle_ref[0] = middle
    inv = lax.rsqrt(jnp.mean(middle * middle, -1, keepdims=True) + EPSILON)
    normed_mlp_ref[...] = (middle * inv * gain_mlp_ref[...]).astype(BF16)


def gelu_both(u):
    scale = 0.7978845608028654
    square = u * u
    t = jnp.tanh(u * (scale + (scale * 0.044715) * square))
    half_up = 0.5 + 0.5 * t
    slope = half_up + (0.5 * u) * (1.0 - t * t) * (scale + (3.0 * 0.044715 * scale) * square)
    return u * half_up, slope


def mlp_kernel(half_ref, nm_ref, g_ref, w_inner_ref, w_outer_ref, *refs, deal, prior):
    if deal:
        label_ref = half_ref
        old_nm = refs[:prior]
        old_active = refs[prior : 2 * prior]
        old_grad = refs[2 * prior : 3 * prior]
        old_g = refs[3 * prior]
        total_in, back_in = refs[3 * prior + 1 : 3 * prior + 3]
        total_ref, back_ref, parts_ref = refs[-3:]
    else:
        total_ref, back_ref, active_ref, grad_ref = refs[-4:]
    step = pl.program_id(0)
    normed = nm_ref[...]
    g = g_ref[0]
    w_inner = w_inner_ref[...]
    w_outer = w_outer_ref[...]
    active_f, slope = gelu_both(dot(normed, w_inner))
    active = active_f.astype(BF16)
    grad_act = (dot(g, w_outer, (1, 1)) * slope).astype(BF16)

    @pl.when(step == 0)
    def _():
        if deal:
            total_ref[...] = total_in[...]
            back_ref[...] = back_in[...]
        else:
            total_ref[...] = jnp.zeros_like(total_ref)
            back_ref[...] = jnp.zeros_like(back_ref)

    total_ref[0] += dot(active, w_outer)
    back_ref[0] += dot(grad_act, w_inner, (1, 1))
    if not deal:
        active_ref[...] = active
        grad_ref[...] = grad_act
        return
    all_active = jnp.concatenate([ref[...] for ref in old_active] + [active], axis=0)
    all_grad = jnp.concatenate([ref[...] for ref in old_grad] + [grad_act], axis=0)
    all_normed = jnp.concatenate([ref[...] for ref in old_nm] + [normed], axis=0)
    all_g = jnp.concatenate([old_g[i] for i in range(prior)] + [g], axis=0)
    outer = dot(all_active, all_g, (0, 0)).astype(BF16)
    inner = dot(all_grad, all_normed, (0, 0)).astype(BF16)
    label = label_ref[1]
    for part in range(FF_TILE // OUTER_ROWS):
        slot = (step * (FF_TILE // OUTER_ROWS) + part) ^ label
        rows = slice(part * OUTER_ROWS, (part + 1) * OUTER_ROWS)
        parts_ref[slot, :OUTER_ROWS] = outer[rows]
        parts_ref[slot, OUTER_ROWS:] = inner[rows]


def back_kernel(
    place_ref,
    code_ref,
    g_ref,
    total_ref,
    back_ref,
    middle_ref,
    attended_ref,
    mixed_ref,
    normed_ref,
    q_ref,
    k_ref,
    v_ref,
    p_ref,
    gain_mlp_ref,
    w_out_ref,
    wq_ref,
    wk_ref,
    wv_ref,
    pin_ref,
    block_output_ref,
    grad_middle_ref,
    dx_keep_ref,
    dx_send_ref,
    keep_ref,
    send_ref,
    table_ref,
    gain_grad_ref,
    gain_mlp_grad_ref,
    table_sum_ref,
    line_ref,
    go_ref,
    gq_ref,
    gk_ref,
    gv_ref,
    stage_ref,
    *,
    here,
    seq,
):
    step = pl.program_id(0)

    @pl.when(step == 0)
    def _():
        for ref in (table_sum_ref, go_ref, gq_ref, gk_ref, gv_ref, gain_mlp_grad_ref):
            ref[...] = jnp.zeros_like(ref)

    middle = middle_ref[0]
    back = back_ref[0]
    block_output_ref[0] = (middle + total_ref[0]).astype(BF16)
    inv = lax.rsqrt(jnp.mean(middle * middle, -1, keepdims=True) + EPSILON)
    gain_mlp_grad_ref[...] += jnp.sum(back * middle * inv, axis=0, keepdims=True)
    scaled = back * gain_mlp_ref[...]
    grad_middle = (
        g_ref[0].astype(F32)
        + inv * scaled
        - middle * (inv * inv * inv) * jnp.mean(scaled * middle, -1, keepdims=True)
    )
    grad_middle_ref[0] = grad_middle
    branch = grad_middle.astype(BF16)
    ga = dot(branch, w_out_ref[...], (1, 1)).astype(BF16)
    go_ref[...] += dot(attended_ref[0], branch, (0, 0))
    q = q_ref[0]
    k = k_ref[0]
    v = v_ref[0]
    normed = normed_ref[0]
    dq, dkt, dvt = [], [], []
    for pair in range(PAIRS):
        lanes = slice(pair * 2 * HD, (pair + 1) * 2 * HD)
        ga_split = split_heads(ga[:, lanes])
        q_split = split_heads(q[:, lanes])
        mixed = mixed_ref[0, :, lanes]
        probs = p_ref[0, pair]
        delta = jnp.sum(
            ga_split.astype(F32) * jnp.concatenate([mixed, mixed], axis=0), -1, keepdims=True
        )
        grad_probs = dot(ga_split, v[:, lanes], (1, 1))
        grad_scores_f = probs.astype(F32) * (grad_probs - delta)
        table_sum_ref[pair] += grad_scores_f
        grad_scores = grad_scores_f.astype(BF16)
        dq.append(join_heads(dot(grad_scores, k[:, lanes])).astype(BF16))
        dkt.append(dot(q_split, grad_scores, (0, 0)).astype(BF16))
        dvt.append(dot(ga_split, probs, (0, 0)).astype(BF16))
    dq = jnp.concatenate(dq, axis=1)
    dkt = jnp.concatenate(dkt, axis=0)
    dvt = jnp.concatenate(dvt, axis=0)
    dxt = dot(wk_ref[...], dkt) + dot(wv_ref[...], dvt)
    own = dxt[:, :here] + dot(wq_ref[...], dq, (1, 1))
    dx_keep_ref[0, 0] = own.astype(BF16)
    for block in range(1, seq):
        target = dx_send_ref if block % 2 else dx_keep_ref
        target[block // 2, 0] = dxt[:, block * here : (block + 1) * here].astype(BF16)
    gq_ref[...] += dot(normed[:here], dq, (0, 0))
    gk_ref[...] += dot(dkt, normed)
    gv_ref[...] += dot(dvt, normed)

    @pl.when(step == pl.num_programs(0) - 1)
    def _():
        me = place_ref[0]
        line_ref[...] = jnp.zeros_like(line_ref)
        for block in range(seq):
            offset = ((me ^ block) - me) * here + PACKED_LENGTH - here
            window = pl.ds(pl.multiple_of(offset, 128), 2 * here)
            for head in range(H):
                row = (head % 2) * here
                tile = table_sum_ref[
                    head // 2, row : row + here, block * here : (block + 1) * here
                ]
                total = jnp.zeros((8, 2 * here), F32)
                empty = jnp.zeros((8, here), F32)
                for group in range(here // 8):
                    wide = jnp.concatenate([tile[group * 8 : group * 8 + 8], empty], axis=1)
                    total = total + pltpu.roll(wide, here - 8 * group, 1)
                line_ref[head * 8 : head * 8 + 8, window] += total
        lines = line_ref[...]
        sub = lax.broadcasted_iota(jnp.int32, lines.shape, 0)
        for bit in (1, 2, 4):
            lines = jnp.where((sub & bit) != 0, pltpu.roll(lines, SPAN - bit, 1), lines)
        by_head = jnp.concatenate(
            [jnp.sum(lines[h * 8 : h * 8 + 8], axis=0, keepdims=True) for h in range(H)], axis=0
        )
        table_ref[...] = dot(
            by_head, bucket_rows((SPAN, 128), 1), (1, 0), lax.Precision.HIGHEST
        )
        gk = gk_ref[...].T
        gv = gv_ref[...].T
        gq = gq_ref[...]
        gain = (
            wq_ref[...].astype(F32) * gq
            + wk_ref[...].astype(F32) * gk
            + wv_ref[...].astype(F32) * gv
        )
        gain_grad_ref[...] = dot(
            jnp.ones((8, D), F32), gain, (1, 1), lax.Precision.HIGHEST
        )
        core, label, other = code_ref[0], code_ref[1], code_ref[2]
        for index, grad in enumerate((go_ref[...], gq, gk, gv)):
            stage_ref[...] = grad
            rows = slice(index * SMALL_ROWS, (index + 1) * SMALL_ROWS)
            for slot in range(HALF):
                for target, chunk in (
                    (keep_ref, core * HALF + (slot ^ label)),
                    (send_ref, (1 - core) * HALF + (slot ^ other)),
                ):
                    first = pl.multiple_of(chunk * SMALL_ROWS, SMALL_ROWS)
                    target[slot, rows] = stage_ref[pl.ds(first, SMALL_ROWS), :].astype(BF16)


def pick(code_ref, low_ref, high_ref, chunk, use):
    core, label, other = code_ref[0], code_ref[1], code_ref[2]

    @pl.when(core == chunk[0])
    def _():
        use(low_ref, chunk[1] ^ label)

    @pl.when(core != chunk[0])
    def _():
        use(high_ref, chunk[1] ^ other)


def finish_mlp_kernel(code_ref, low_ref, high_ref, outer_ref, inner_ref, stage_ref):
    step = pl.program_id(0)
    per_step = FF_TILE // OUTER_ROWS
    for part in range(per_step):
        chunk = step * per_step + part
        rows = slice(part * OUTER_ROWS, (part + 1) * OUTER_ROWS)

        def use(ref, slot):
            outer_ref[rows, :] = ref[slot, :OUTER_ROWS].astype(F32)
            stage_ref[rows, :] = ref[slot, OUTER_ROWS:].astype(F32)

        pick(code_ref, low_ref, high_ref, (chunk // HALF, chunk % HALF), use)
    inner_ref[...] = stage_ref[...].T


def finish_attention_kernel(code_ref, low_ref, high_ref, *out_refs):
    half = pl.program_id(0)
    for part in range(HALF):
        rows = slice(part * SMALL_ROWS, (part + 1) * SMALL_ROWS)

        def use(ref, slot):
            for index, out_ref in enumerate(out_refs):
                out_ref[rows, :] = ref[
                    slot, index * SMALL_ROWS : (index + 1) * SMALL_ROWS
                ].astype(F32)

        pick(code_ref, low_ref, high_ref, (half, part), use)


def post_kernel(a_ref, b_ref, x_ref, grad_middle_ref, gain_ref, out_ref):
    back = (a_ref[0].astype(F32) + b_ref[0].astype(F32)).T
    x = x_ref[0].astype(F32)
    inv = lax.rsqrt(jnp.mean(x * x, -1, keepdims=True) + EPSILON)
    scaled = back * gain_ref[...]
    grad = inv * scaled - x * (inv * inv * inv) * jnp.mean(scaled * x, -1, keepdims=True)
    out_ref[0] = (grad_middle_ref[0] + grad).astype(BF16)


ANYWHERE = pl.BlockSpec(memory_space=pl.ANY)


def whole(shape):
    return pl.BlockSpec(shape, lambda *_: (0,) * len(shape))


def by_row(shape):
    return pl.BlockSpec((1,) + shape[1:], lambda i, *_: (i,) + (0,) * (len(shape) - 1))


def one_row(shape, row):
    return pl.BlockSpec((1,) + shape[1:], lambda *_: (row,) + (0,) * (len(shape) - 1))


def shaped(shape, dtype):
    return jax.ShapeDtypeStruct(shape, dtype)


def call(
    kernel,
    grid,
    prefetch,
    inputs,
    in_specs,
    outs,
    out_specs,
    scratch=(),
    flops=0,
    name=None,
    aliases=None,
):
    moved = sum(a.size * a.dtype.itemsize for a in inputs)
    moved += sum(o.size * o.dtype.itemsize for o in outs)
    return pl.pallas_call(
        kernel,
        out_shape=outs,
        grid_spec=pltpu.PrefetchScalarGridSpec(
            num_scalar_prefetch=len(prefetch),
            grid=grid,
            in_specs=in_specs,
            out_specs=out_specs,
            scratch_shapes=list(scratch),
        ),
        compiler_params=pltpu.CompilerParams(
            dimension_semantics=("arbitrary",) * len(grid), vmem_limit_bytes=VMEM_LIMIT
        ),
        cost_estimate=pl.CostEstimate(flops=flops, bytes_accessed=moved, transcendentals=0),
        input_output_aliases=aliases or {},
        name=name,
    )(*prefetch, *inputs)


def add(*parts):
    total = parts[0].astype(F32)
    for part in parts[1:]:
        total = total + part.astype(F32)
    return total


def make_body(rows, seq):
    both = ("rows", "seq")
    further = [1 << i for i in range(3, rows.bit_length() - 1)]

    def swap_rows(array, bit):
        return lax.ppermute(array, "rows", [(i, i ^ bit) for i in range(rows)])

    def swap_seq(array, bit):
        return lax.ppermute(array, "seq", [(i, i ^ bit) for i in range(seq)])

    def swap_step(array, step):
        def partner(r, z):
            first, second = ((0, 2), (0, 4)), ((1, 1), (1, 2))
            if r & 1:
                first, second = first[::-1], second[::-1]
            axis, bit = (first + second)[step]
            return (r, z ^ bit) if axis else (r ^ bit, z)

        pairs = []
        for r in range(rows):
            for z in range(seq):
                to_r, to_z = partner(r, z)
                pairs.append((r * seq + z, to_r * seq + to_z))
        return lax.ppermute(array, both, pairs)

    def codes():
        r, z = lax.axis_index("rows"), lax.axis_index("seq")
        core = r & 1
        b1, b2, z0, z1 = (r >> 1) & 1, (r >> 2) & 1, z & 1, (z >> 1) & 1
        even = b1 * 8 + b2 * 4 + z0 * 2 + z1
        odd = b2 * 8 + b1 * 4 + z1 * 2 + z0
        label = jnp.where(core == 0, even, odd)
        other = jnp.where(core == 0, odd, even)
        return jnp.stack([core, label, other]).astype(jnp.int32)

    def reduce_scatter(keep, arrived, hold=None):
        parts = [keep, arrived]
        size = keep.shape[0]
        outgoing = []
        for step in range(4):
            size //= 2
            send = add(*[part[size : 2 * size] for part in parts]).astype(BF16)
            outgoing.append(send)
            parts = [part[:size] for part in parts]
            parts.append(swap_step(send, step))
            if hold is not None and step == 0:
                parts[-1] = hold(send, parts[-1])
        total = add(*parts)
        for bit in further:
            total = total + swap_rows(total, bit)
        return total.astype(BF16)

    def all_gather(held):
        for step in (3, 2, 1, 0):
            held = jnp.concatenate([held, swap_step(held, step)])
        return held, swap_rows(held, 1)

    def body(
        block_input,
        cotangent,
        gain_attn,
        w_query,
        w_key,
        w_value,
        w_out,
        gain_mlp,
        w_inner,
        outer_weight,
        bias_table,
        lengths,
        observed,
    ):
        count, here = block_input.shape[0], block_input.shape[1]
        tokens = count * here
        last = count - 1
        place = lax.axis_index("seq").astype(jnp.int32).reshape(1)
        code = codes()
        gain_attn_row = gain_attn.reshape(1, D)
        gain_mlp_row = gain_mlp.reshape(1, D)

        mine = [block_input[row] for row in range(count)]
        x2 = [swap_seq(x, 2) for x in mine]
        x1 = [swap_seq(x, 1) for x in mine]
        seen = jnp.stack([observed] + [swap_seq(observed, j) for j in range(1, seq)], axis=1)
        x3 = [swap_seq(x, 1) for x in x2]

        stacked = (PAIRS, 2 * here, PACKED_LENGTH)
        bias = call(
            functools.partial(bias_kernel, here=here, seq=seq),
            (1,),
            (place,),
            (bias_table,),
            [whole(bias_table.shape)],
            [shaped(stacked, F32)],
            [whole(stacked)],
            [pltpu.VMEM((H, SPAN), F32)],
            name="bias",
        )[0]

        one = (here, D)
        own = (count, here, D)
        full = (count, PACKED_LENGTH, D)
        p_shape = (count,) + stacked
        square = whole((D, D))
        line = whole((1, D))

        kept = []
        sums = []
        normed_mlp, actives, grad_acts = [], [], []
        kept_shapes = [
            shaped(own, BF16),
            shaped(own, F32),
            shaped(own, F32),
            shaped(full, BF16),
            shaped(own, BF16),
            shaped(full, BF16),
            shaped(full, BF16),
            shaped(p_shape, BF16),
        ]
        sum_shapes = [shaped(own, F32)] * 2
        for row in range(count):
            inputs = [
                block_input,
                x1[row],
                x2[row],
                x3[row],
                seen,
                gain_attn_row,
                w_query,
                w_key,
                w_value,
                w_out,
                gain_mlp_row,
                bias,
            ]
            specs = [one_row(own, row)] + [whole(one)] * 3 + [one_row(seen.shape, row), line]
            specs += [square] * 4 + [line, whole(stacked)]
            first = len(inputs) + 2
            nm, *kept = call(
                functools.partial(attention_kernel, row=row, here=here, seq=seq),
                (1,),
                (place, lengths),
                inputs + kept,
                specs + [ANYWHERE] * len(kept),
                [shaped(one, BF16)] + kept_shapes,
                [whole(one)] + [one_row(s.shape, row) for s in kept_shapes],
                flops=8 * here * D * PACKED_LENGTH,
                name="attention",
                aliases={first + i: 1 + i for i in range(len(kept))},
            )
            normed_mlp.append(nm)
            if row == last:
                break
            sums_in = sums
            first = 4 + 1
            *sums, active, grad_act = call(
                functools.partial(mlp_kernel, deal=False, prior=0),
                (FF // FF_TILE,),
                (code,),
                [nm, cotangent, w_inner, outer_weight] + sums_in,
                [
                    whole(one),
                    one_row(own, row),
                    pl.BlockSpec((D, FF_TILE), lambda i, *_: (0, i)),
                    pl.BlockSpec((FF_TILE, D), lambda i, *_: (i, 0)),
                ]
                + [ANYWHERE] * len(sums_in),
                sum_shapes + [shaped((here, FF), BF16)] * 2,
                [one_row(own, row)] * 2
                + [pl.BlockSpec((here, FF_TILE), lambda i, *_: (0, i))] * 2,
                flops=8 * here * D * FF,
                name="mlp",
                aliases={first + i: i for i in range(len(sums_in))},
            )
            actives.append(active)
            grad_acts.append(grad_act)

        steps = FF // FF_TILE // 2
        part_shape = (HALF, 2 * OUTER_ROWS, D)

        def mlp_last(sums, own_half):
            which = code[0] if own_half else 1 - code[0]
            info = jnp.stack([which * steps, code[1] if own_half else code[2]])
            hidden = pl.BlockSpec((here, FF_TILE), lambda i, n: (0, n[0] + i))
            inputs = [normed_mlp[last], cotangent, w_inner, outer_weight]
            specs = [
                whole(one),
                one_row(own, last),
                pl.BlockSpec((D, FF_TILE), lambda i, n: (0, n[0] + i)),
                pl.BlockSpec((FF_TILE, D), lambda i, n: (n[0] + i, 0)),
            ]
            inputs += normed_mlp[:last] + actives + grad_acts + [cotangent]
            specs += [whole(one)] * last + [hidden] * (2 * last) + [whole(own)]
            first = len(inputs) + 1
            return call(
                functools.partial(mlp_kernel, deal=True, prior=last),
                (steps,),
                (info,),
                inputs + sums,
                specs + [one_row(own, last)] * 2,
                sum_shapes + [shaped(part_shape, BF16)],
                [one_row(own, last)] * 2 + [whole(part_shape)],
                flops=10 * here * D * FF,
                name="mlp_last",
                aliases={first: 0, first + 1: 1},
            )

        sums = [s.at[last].set(0.0) for s in sums]
        *sums, mlp_send = mlp_last(sums, False)
        mlp_arrived = swap_rows(mlp_send, 1)
        *sums, mlp_keep = mlp_last(sums, True)

        small_half = (HALF, 4 * SMALL_ROWS, D)
        dx_half = (seq // 2, count, D, here)
        dx_spec = pl.BlockSpec((seq // 2, 1, D, here), lambda i, *_: (0, i, 0, 0))
        results = []

        def back_call(pin, arrived):
            results.extend(
                call(
                    functools.partial(back_kernel, here=here, seq=seq),
                    (count,),
                    (place, code),
                    (cotangent, *sums, kept[1], kept[0], *kept[2:], gain_mlp_row, w_out)
                    + (w_query, w_key, w_value, pin),
                    [by_row(own)] * 6
                    + [by_row(full), by_row(own), by_row(full), by_row(full), by_row(p_shape)]
                    + [line]
                    + [square] * 4
                    + [ANYWHERE],
                    [shaped(own, BF16), shaped(own, F32)]
                    + [shaped(dx_half, BF16)] * 2
                    + [shaped(small_half, BF16)] * 2
                    + [shaped((H, 128), F32), shaped((8, D), F32), shaped((1, D), F32)],
                    [by_row(own)] * 2
                    + [dx_spec] * 2
                    + [whole(small_half)] * 2
                    + [whole((H, 128)), whole((8, D)), line],
                    [
                        pltpu.VMEM(stacked, F32),
                        pltpu.VMEM((8 * H, SPAN), F32),
                        pltpu.VMEM((D, D), F32),
                        pltpu.VMEM((D, D), F32),
                        pltpu.VMEM((D, D), F32),
                        pltpu.VMEM((D, D), F32),
                        pltpu.VMEM((D, D), F32),
                    ],
                    flops=20 * tokens * D * PACKED_LENGTH,
                    name="attention_back",
                )
            )
            return lax.optimization_barrier((arrived, results[6]))[0]

        mlp_part = reduce_scatter(mlp_keep, mlp_arrived, back_call)
        (
            block_output,
            grad_middle,
            dx_keep,
            dx_send,
            small_keep,
            small_send,
            table,
            gain_part,
            gain_mlp_part,
        ) = results

        half_sum = add(dx_keep, swap_seq(dx_send, 1)).astype(BF16)
        arrived = swap_seq(half_sum[1], 2)
        dx_shape = (count, D, here)
        input_grad = call(
            post_kernel,
            (count,),
            (),
            (half_sum[0], arrived, block_input, grad_middle, gain_attn_row),
            [by_row(dx_shape)] * 2 + [by_row(own)] * 2 + [line],
            [shaped(own, BF16)],
            [by_row(own)],
            name="post",
        )[0]

        small_part = reduce_scatter(small_keep, swap_rows(small_send, 1))
        mlp_low, mlp_high = all_gather(mlp_part)
        grad_outer, grad_inner = call(
            finish_mlp_kernel,
            (FF // FF_TILE,),
            (code,),
            (mlp_low, mlp_high),
            [whole(part_shape)] * 2,
            [shaped((FF, D), F32), shaped((D, FF), F32)],
            [
                pl.BlockSpec((FF_TILE, D), lambda i, *_: (i, 0)),
                pl.BlockSpec((D, FF_TILE), lambda i, *_: (0, i)),
            ],
            [pltpu.VMEM((FF_TILE, D), F32)],
            name="finish_mlp",
        )
        small_low, small_high = all_gather(small_part)
        grad_out, grad_query, grad_key, grad_value = call(
            finish_attention_kernel,
            (2,),
            (code,),
            (small_low, small_high),
            [whole(small_half)] * 2,
            [shaped((D, D), F32)] * 4,
            [pl.BlockSpec((D // 2, D), lambda i, *_: (i, 0))] * 4,
            name="finish_attention",
        )

        small = jnp.concatenate(
            [gain_part[:1] / gain_attn_row, gain_mlp_part, table.reshape(2, D)], axis=0
        )
        for bit in [1 << i for i in range(rows.bit_length() - 1)]:
            small = small + swap_rows(small, bit)
        for bit in [1 << i for i in range(seq.bit_length() - 1)]:
            small = small + swap_seq(small, bit)

        return (
            block_output,
            input_grad,
            small[0],
            grad_query,
            grad_key,
            grad_value,
            grad_out,
            small[1],
            grad_inner,
            grad_outer,
            small[2:].reshape(H, 128)[:, :BUCKETS].T,
        )

    return body


def solution(mesh):
    split = P("rows", "seq", None)
    placed = (split, split) + (P(),) * 9 + (P("rows", None), P("rows", "seq"))
    return jax.shard_map(
        make_body(mesh.shape["rows"], mesh.shape["seq"]),
        mesh=mesh,
        in_specs=placed,
        out_specs=(split, split) + (P(),) * 9,
        check_vma=False,
    )
```

```python
import functools
import math

import jax
import jax.numpy as jnp
from jax import lax
from jax.experimental import pallas as pl
from jax.experimental.pallas import tpu as pltpu
from jax.sharding import PartitionSpec as P

D = 512
FF = 2048
H = 8
HD = 64
PAIRS = H // 2
BUCKETS = 32
PACKED_LENGTH = 512
EPSILON = 1e-06
BUCKET_EDGES = (12, 16, 23, 32, 46, 64, 91)
SPAN = 2 * PACKED_LENGTH
CHUNKS = 32
HALF = CHUNKS // 2
OUTER_ROWS = FF // CHUNKS
SMALL_ROWS = D // CHUNKS
FF_TILE = 512
MASKED = -1000000000.0
MIB = 1024 * 1024
F32 = jnp.float32
BF16 = jnp.bfloat16


def dot(left, right, contract=(1, 0), precision=None):
    return lax.dot_general(
        left,
        right,
        (((contract[0],), (contract[1],)), ((), ())),
        preferred_element_type=F32,
        precision=precision,
    )


def xor_pairs(size, bit):
    return [(i, i ^ bit) for i in range(size)]


def bucket_of(relative):
    distance = jnp.abs(relative)
    beyond = jnp.full(distance.shape, 8, jnp.int32)
    for edge_value in BUCKET_EDGES:
        beyond = beyond + (distance >= edge_value).astype(jnp.int32)
    near = jnp.where(distance < 8, distance, beyond)
    return jnp.where(relative > 0, 16, 0).astype(jnp.int32) + near


def bucket_rows(shape, bucket_axis):
    place_axis = 1 - bucket_axis
    relative = lax.broadcasted_iota(jnp.int32, shape, place_axis) - PACKED_LENGTH
    return (bucket_of(relative) == lax.broadcasted_iota(jnp.int32, shape, bucket_axis)).astype(F32)


def split_heads(pair):
    lane = lax.broadcasted_iota(jnp.int32, pair.shape, 1)
    zero = jnp.zeros_like(pair)
    return jnp.concatenate(
        [jnp.where(lane < HD, pair, zero), jnp.where(lane >= HD, pair, zero)], axis=0
    )


def join_heads(stacked):
    half = stacked.shape[0] // 2
    lane = lax.broadcasted_iota(jnp.int32, (half, stacked.shape[1]), 1)
    return jnp.where(lane < HD, stacked[:half], stacked[half:])


def prepare_kernel(place_ref, table_ref, *refs, here, seq):
    count = (len(refs) - 3) // 2
    sources, bias_ref, targets = refs[:count], refs[count], refs[count + 1 : 2 * count + 1]
    line_ref, sems = refs[2 * count + 1 :]
    copies = [
        pltpu.make_async_copy(source, target, sems.at[i])
        for i, (source, target) in enumerate(zip(sources, targets))
    ]
    for copy in copies:
        copy.start()
    line_ref[...] = dot(
        table_ref[...], bucket_rows((BUCKETS, SPAN), 0), (0, 0), lax.Precision.HIGHEST
    )
    me = place_ref[0]
    for block in range(seq):
        offset = ((me ^ block) - me) * here + PACKED_LENGTH - here
        window = line_ref[:, pl.ds(pl.multiple_of(offset, 128), 2 * here)]
        for head in range(H):
            spread = jnp.broadcast_to(window[head : head + 1], (here, 2 * here))
            skewed = pltpu.roll(spread, here, 1, stride=1, stride_axis=0)
            row = (head % 2) * here
            bias_ref[head // 2, row : row + here, block * here : (block + 1) * here] = skewed[
                :, :here
            ]
    for copy in copies:
        copy.wait()


def attention_kernel(
    place_ref,
    lengths_ref,
    x0_ref,
    x1_ref,
    x2_ref,
    x3_ref,
    seen0_ref,
    seen1_ref,
    seen2_ref,
    seen3_ref,
    gain_ref,
    wq_ref,
    wk_ref,
    wv_ref,
    w_out_ref,
    gain_mlp_ref,
    bias_ref,
    normed_mlp_ref,
    attended_ref,
    middle_ref,
    mixed_ref,
    normed_ref,
    q_ref,
    k_ref,
    v_ref,
    p_ref,
    *,
    row,
    here,
    seq,
):
    me = place_ref[0]
    own_x = x0_ref[0].astype(F32)
    x = jnp.concatenate(
        [own_x] + [ref.astype(F32) for ref in (x1_ref[0], x2_ref[0], x3_ref[...])], axis=0
    )
    inv = lax.rsqrt(jnp.mean(x * x, -1, keepdims=True) + EPSILON)
    normed = (x * inv * gain_ref[...]).astype(BF16)
    normed_ref[...] = normed
    q = dot(normed[:here], wq_ref[...]).astype(BF16)
    k = dot(normed, wk_ref[...]).astype(BF16)
    v = dot(normed, wv_ref[...]).astype(BF16)
    q_ref[...] = q
    k_ref[...] = k
    v_ref[...] = v
    ends = [lengths_ref[row, 0]]
    for part in range(1, lengths_ref.shape[1]):
        ends.append(ends[-1] + lengths_ref[row, part])

    def segment(place):
        total = jnp.zeros(place.shape, jnp.int32)
        for end in ends:
            total = total + (end <= place).astype(jnp.int32)
        return total

    query_place = me * here + lax.broadcasted_iota(jnp.int32, (here, 1), 0)
    lane = lax.broadcasted_iota(jnp.int32, (1, here), 1)
    key_place = jnp.concatenate([(me ^ block) * here + lane for block in range(seq)], axis=1)
    seen = jnp.concatenate(
        [ref[row : row + 1] for ref in (seen0_ref, seen1_ref, seen2_ref, seen3_ref)], axis=1
    )
    key_segment = jnp.where(seen == 1, segment(key_place), -1)
    allowed = (segment(query_place) == key_segment) | (query_place == key_place)
    allowed = jnp.concatenate([allowed.astype(jnp.int32)] * 2, axis=0) == 1
    attended = []
    for pair in range(PAIRS):
        lanes = slice(pair * 2 * HD, (pair + 1) * 2 * HD)
        scores = dot(split_heads(q[:, lanes]), k[:, lanes], (1, 1)) + bias_ref[pair]
        scores = jnp.where(allowed, scores, MASKED)
        exponent = jnp.exp(scores - jnp.max(scores, -1, keepdims=True))
        share = 1.0 / jnp.sum(exponent, -1, keepdims=True)
        probs = (exponent * share).astype(BF16)
        p_ref[pair] = probs
        mixed = join_heads(dot(probs, v[:, lanes]))
        mixed_ref[:, lanes] = mixed
        attended.append(mixed.astype(BF16))
    attended = jnp.concatenate(attended, axis=1)
    attended_ref[...] = attended
    middle = own_x + dot(attended, w_out_ref[...])
    middle_ref[...] = middle
    inv = lax.rsqrt(jnp.mean(middle * middle, -1, keepdims=True) + EPSILON)
    normed_mlp_ref[...] = (middle * inv * gain_mlp_ref[...]).astype(BF16)


def gelu_both(u):
    scale = 0.7978845608028654
    square = u * u
    t = jnp.tanh(u * (scale + (scale * 0.044715) * square))
    half_up = 0.5 + 0.5 * t
    slope = half_up + (0.5 * u) * (1.0 - t * t) * (scale + (3.0 * 0.044715 * scale) * square)
    return u * half_up, slope


def mlp_kernel(code_ref, *refs, rows, own_half):
    nm_refs = refs[:rows]
    g_ref, w_inner_ref, w_outer_ref, total_ref, back_ref, parts_ref = refs[rows:]
    step = pl.program_id(0)
    core = code_ref[0]
    which = core if own_half else 1 - core
    label = code_ref[1] if own_half else code_ref[2]
    first = pl.multiple_of((which * pl.num_programs(0) + step) * FF_TILE, FF_TILE)
    normed = jnp.concatenate([ref[...] for ref in nm_refs], axis=0)
    g = g_ref[...].reshape(normed.shape)
    w_inner = w_inner_ref[:, pl.ds(first, FF_TILE)]
    w_outer = w_outer_ref[pl.ds(first, FF_TILE), :]
    active_f, slope = gelu_both(dot(normed, w_inner))
    active = active_f.astype(BF16)
    grad_act = (dot(g, w_outer, (1, 1)) * slope).astype(BF16)

    @pl.when(step == 0)
    def _():
        total_ref[...] = jnp.zeros_like(total_ref)
        back_ref[...] = jnp.zeros_like(back_ref)

    total_ref[...] += dot(active, w_outer)
    back_ref[...] += dot(grad_act, w_inner, (1, 1))
    outer = dot(active, g, (0, 0)).astype(BF16)
    inner = dot(grad_act, normed, (0, 0)).astype(BF16)
    for part in range(FF_TILE // OUTER_ROWS):
        slot = (step * (FF_TILE // OUTER_ROWS) + part) ^ label
        rows = slice(part * OUTER_ROWS, (part + 1) * OUTER_ROWS)
        parts_ref[slot, :OUTER_ROWS] = outer[rows]
        parts_ref[slot, OUTER_ROWS:] = inner[rows]


def back_kernel(place_ref, code_ref, *refs, rows, here, seq):
    per_row = 9
    row_refs = [refs[i * per_row : (i + 1) * per_row] for i in range(rows)]
    refs = refs[rows * per_row :]
    (
        g_ref,
        total_a_ref,
        total_b_ref,
        back_a_ref,
        back_b_ref,
        gain_attn_ref,
        gain_mlp_ref,
        w_out_ref,
        wq_ref,
        wk_ref,
        wv_ref,
        pin_ref,
        block_output_ref,
        grad_middle_ref,
        dx_keep_ref,
        dx_send_ref,
        keep_ref,
        send_ref,
        rider_ref,
        table_sum_ref,
        line_ref,
        go_ref,
        gq_ref,
        gk_ref,
        gv_ref,
    ) = refs
    gain_mlp_grad = jnp.zeros((1, D), F32)
    for index in range(rows):
        _, attended_ref, middle_ref, mixed_ref, normed_ref, q_ref, k_ref, v_ref, p_ref = row_refs[
            index
        ]
        tokens = slice(index * here, (index + 1) * here)
        middle = middle_ref[...]
        back = back_a_ref[tokens] + back_b_ref[tokens]
        block_output_ref[index] = (middle + total_a_ref[tokens] + total_b_ref[tokens]).astype(BF16)
        inv = lax.rsqrt(jnp.mean(middle * middle, -1, keepdims=True) + EPSILON)
        gain_mlp_grad = gain_mlp_grad + jnp.sum(back * middle * inv, axis=0, keepdims=True)
        scaled = back * gain_mlp_ref[...]
        grad_middle = (
            g_ref[index].astype(F32)
            + inv * scaled
            - middle * (inv * inv * inv) * jnp.mean(scaled * middle, -1, keepdims=True)
        )
        grad_middle_ref[index] = grad_middle
        branch = grad_middle.astype(BF16)
        ga = dot(branch, w_out_ref[...], (1, 1)).astype(BF16)

        def accumulate(ref, value):
            if index == 0:
                ref[...] = value
            else:
                ref[...] += value

        accumulate(go_ref, dot(attended_ref[...], branch, (0, 0)))
        q = q_ref[...]
        k = k_ref[...]
        v = v_ref[...]
        normed = normed_ref[...]
        dq, dkt, dvt = [], [], []
        for pair in range(PAIRS):
            lanes = slice(pair * 2 * HD, (pair + 1) * 2 * HD)
            ga_split = split_heads(ga[:, lanes])
            q_split = split_heads(q[:, lanes])
            mixed = mixed_ref[:, lanes]
            probs = p_ref[pair]
            delta = jnp.sum(
                ga_split.astype(F32) * jnp.concatenate([mixed, mixed], axis=0), -1, keepdims=True
            )
            grad_probs = dot(ga_split, v[:, lanes], (1, 1))
            grad_scores_f = probs.astype(F32) * (grad_probs - delta)
            accumulate(table_sum_ref.at[pair], grad_scores_f)
            grad_scores = grad_scores_f.astype(BF16)
            dq.append(join_heads(dot(grad_scores, k[:, lanes])).astype(BF16))
            dkt.append(dot(q_split, grad_scores, (0, 0)).astype(BF16))
            dvt.append(dot(ga_split, probs, (0, 0)).astype(BF16))
        dq = jnp.concatenate(dq, axis=1)
        dkt = jnp.concatenate(dkt, axis=0)
        dvt = jnp.concatenate(dvt, axis=0)
        dxt = dot(wk_ref[...], dkt) + dot(wv_ref[...], dvt)
        own = dxt[:, :here] + dot(wq_ref[...], dq, (1, 1))
        pieces = [own] + [dxt[:, block * here : (block + 1) * here] for block in range(1, seq)]
        pieces = [piece.astype(BF16) for piece in pieces]
        dx_keep_ref[0, index] = pieces[0]
        dx_send_ref[1, index] = pieces[3]

        @pl.when(code_ref[0] == 0)
        def _():
            dx_keep_ref[1, index] = pieces[2]
            dx_send_ref[0, index] = pieces[1]

        @pl.when(code_ref[0] == 1)
        def _():
            dx_keep_ref[1, index] = pieces[1]
            dx_send_ref[0, index] = pieces[2]

        accumulate(gq_ref, dot(normed[:here], dq, (0, 0)))
        accumulate(gk_ref, dot(dkt, normed))
        accumulate(gv_ref, dot(dvt, normed))

    me = place_ref[0]
    line_ref[...] = jnp.zeros_like(line_ref)
    for block in range(seq):
        offset = ((me ^ block) - me) * here + PACKED_LENGTH - here
        window = pl.ds(pl.multiple_of(offset, 128), 2 * here)
        for head in range(H):
            row = (head % 2) * here
            tile = table_sum_ref[head // 2, row : row + here, block * here : (block + 1) * here]
            total = jnp.zeros((8, 2 * here), F32)
            empty = jnp.zeros((8, here), F32)
            for group in range(here // 8):
                wide = jnp.concatenate([tile[group * 8 : group * 8 + 8], empty], axis=1)
                total = total + pltpu.roll(wide, here - 8 * group, 1)
            line_ref[head * 8 : head * 8 + 8, window] += total
    lines = line_ref[...]
    sub = lax.broadcasted_iota(jnp.int32, lines.shape, 0)
    for bit in (1, 2, 4):
        lines = jnp.where((sub & bit) != 0, pltpu.roll(lines, SPAN - bit, 1), lines)
    by_head = jnp.concatenate(
        [jnp.sum(lines[h * 8 : h * 8 + 8], axis=0, keepdims=True) for h in range(H)], axis=0
    )
    table = dot(by_head, bucket_rows((SPAN, 128), 1), (1, 0), lax.Precision.HIGHEST)
    gk_ref[...] = gk_ref[...].T
    gv_ref[...] = gv_ref[...].T
    gain = (
        wq_ref[...].astype(F32) * gq_ref[...]
        + wk_ref[...].astype(F32) * gk_ref[...]
        + wv_ref[...].astype(F32) * gv_ref[...]
    )
    gain_grad = dot(jnp.ones((8, D), F32), gain, (1, 1), lax.Precision.HIGHEST)
    rider = jnp.concatenate(
        [
            jnp.concatenate([table, jnp.zeros((8, D - 128), F32)], axis=1),
            gain_grad[:1] / gain_attn_ref[...],
            gain_mlp_grad,
            jnp.zeros((6, D), F32),
        ],
        axis=0,
    )
    rider_ref[...] = rider
    high = rider.astype(BF16)
    base = HALF * 4 * SMALL_ROWS
    send_ref[base : base + 16, :] = high
    send_ref[base + 16 : base + 32, :] = (rider - high.astype(F32)).astype(BF16)
    core, label, other = code_ref[0], code_ref[1], code_ref[2]
    for index, grad_ref in enumerate((go_ref, gq_ref, gk_ref, gv_ref)):
        for slot in range(HALF):
            chunk = core * HALF + (slot ^ label)
            first = pl.multiple_of(chunk * SMALL_ROWS, SMALL_ROWS)
            rows_to = slice(index * SMALL_ROWS, (index + 1) * SMALL_ROWS)
            keep_ref[slot, rows_to] = grad_ref[pl.ds(first, SMALL_ROWS), :].astype(BF16)
            chunk = (1 - core) * HALF + (slot ^ other)
            first = pl.multiple_of(chunk * SMALL_ROWS, SMALL_ROWS)
            start = (slot * 4 + index) * SMALL_ROWS
            send_ref[start : start + SMALL_ROWS, :] = grad_ref[
                pl.ds(first, SMALL_ROWS), :
            ].astype(BF16)


def pick(code_ref, low_ref, high_ref, chunk, use):
    core, label, other = code_ref[0], code_ref[1], code_ref[2]

    @pl.when(core == chunk[0])
    def _():
        use(low_ref, chunk[1] ^ label)

    @pl.when(core != chunk[0])
    def _():
        use(high_ref, chunk[1] ^ other)


def finish_mlp_kernel(code_ref, low_ref, high_ref, outer_ref, inner_ref, stage_ref):
    step = pl.program_id(0)
    per_step = FF_TILE // OUTER_ROWS
    for part in range(per_step):
        chunk = step * per_step + part
        rows = slice(part * OUTER_ROWS, (part + 1) * OUTER_ROWS)

        def use(ref, slot):
            outer_ref[rows, :] = ref[slot, :OUTER_ROWS].astype(F32)
            stage_ref[rows, :] = ref[slot, OUTER_ROWS:].astype(F32)

        pick(code_ref, low_ref, high_ref, (chunk // HALF, chunk % HALF), use)
    inner_ref[...] = stage_ref[...].T


def finish_attention_kernel(code_ref, low_ref, high_ref, *out_refs):
    half = pl.program_id(0)
    for part in range(HALF):
        rows = slice(part * SMALL_ROWS, (part + 1) * SMALL_ROWS)

        def use(ref, slot):
            for index, out_ref in enumerate(out_refs):
                out_ref[rows, :] = ref[
                    slot, index * SMALL_ROWS : (index + 1) * SMALL_ROWS
                ].astype(F32)

        pick(code_ref, low_ref, high_ref, (half, part), use)


def post_kernel(a_ref, b_ref, x_ref, grad_middle_ref, gain_ref, out_ref):
    back = (a_ref[0].astype(F32) + b_ref[0].astype(F32)).T
    x = x_ref[0].astype(F32)
    inv = lax.rsqrt(jnp.mean(x * x, -1, keepdims=True) + EPSILON)
    scaled = back * gain_ref[...]
    grad = inv * scaled - x * (inv * inv * inv) * jnp.mean(scaled * x, -1, keepdims=True)
    out_ref[0] = (grad_middle_ref[0] + grad).astype(BF16)


ANYWHERE = pl.BlockSpec(memory_space=pl.ANY)


def whole(shape):
    return pl.BlockSpec(shape, lambda *_: (0,) * len(shape))


def by_row(shape):
    return pl.BlockSpec((1,) + shape[1:], lambda i, *_: (i,) + (0,) * (len(shape) - 1))


def one_row(shape, row):
    return pl.BlockSpec((1,) + shape[1:], lambda *_: (row,) + (0,) * (len(shape) - 1))


def shaped(shape, dtype):
    return jax.ShapeDtypeStruct(shape, dtype)


def call(
    kernel,
    grid,
    prefetch,
    inputs,
    in_specs,
    outs,
    out_specs,
    scratch=(),
    flops=0,
    name=None,
    aliases=None,
    vmem=16,
):
    moved = sum(a.size * a.dtype.itemsize for a in inputs)
    moved += sum(math.prod(o.shape) * o.dtype.itemsize for o in outs)
    return pl.pallas_call(
        kernel,
        out_shape=outs,
        grid_spec=pltpu.PrefetchScalarGridSpec(
            num_scalar_prefetch=len(prefetch),
            grid=grid,
            in_specs=in_specs,
            out_specs=out_specs,
            scratch_shapes=list(scratch),
        ),
        compiler_params=pltpu.CompilerParams(
            dimension_semantics=("arbitrary",) * len(grid), vmem_limit_bytes=vmem * MIB
        ),
        cost_estimate=pl.CostEstimate(flops=flops, bytes_accessed=moved, transcendentals=0),
        input_output_aliases=aliases or {},
        name=name,
    )(*prefetch, *inputs)


def add(*parts):
    total = parts[0].astype(F32)
    for part in parts[1:]:
        total = total + part.astype(F32)
    return total


def make_body(rows, seq):
    both = ("rows", "seq")
    further = [1 << i for i in range(3, rows.bit_length() - 1)]

    def swap_rows(array, bit):
        return lax.ppermute(array, "rows", [(i, i ^ bit) for i in range(rows)])

    def swap_seq(array, bit):
        return lax.ppermute(array, "seq", [(i, i ^ bit) for i in range(seq)])

    def swap_step(array, step):
        def partner(r, z):
            first, second = ((0, 2), (0, 4)), ((1, 1), (1, 2))
            if r & 1:
                first, second = first[::-1], second[::-1]
            axis, bit = (first + second)[step]
            return (r, z ^ bit) if axis else (r ^ bit, z)

        pairs = []
        for r in range(rows):
            for z in range(seq):
                to_r, to_z = partner(r, z)
                pairs.append((r * seq + z, to_r * seq + to_z))
        return lax.ppermute(array, both, pairs)

    def codes():
        r, z = lax.axis_index("rows"), lax.axis_index("seq")
        core = r & 1
        b1, b2, z0, z1 = (r >> 1) & 1, (r >> 2) & 1, z & 1, (z >> 1) & 1
        even = b1 * 8 + b2 * 4 + z0 * 2 + z1
        odd = b2 * 8 + b1 * 4 + z1 * 2 + z0
        label = jnp.where(core == 0, even, odd)
        other = jnp.where(core == 0, odd, even)
        return jnp.stack([core, label, other]).astype(jnp.int32)

    def after(array, *earlier):
        return lax.optimization_barrier((array, *earlier))[0]

    def halves(rider):
        high = rider.astype(BF16)
        return [high, (rider - high.astype(F32)).astype(BF16)]

    class Reduction:
        def __init__(self, wire, shape, rider=None):
            self.rider = rider
            self.parts = [None]
            self.step = 0
            self.arrived = (swap_rows(wire, 1), *shape[:2])

        def send(self, outgoing):
            slots, rows_each = outgoing.shape[:2]
            if self.rider is not None:
                flat = outgoing.reshape(slots * rows_each, D)
                outgoing = jnp.concatenate([flat] + halves(self.rider), axis=0)
            self.arrived = (swap_step(outgoing, self.step), slots, rows_each)
            self.step += 1

        def receive(self, *earlier):
            array, slots, rows_each = self.arrived
            array = after(array, *earlier)
            if self.rider is not None:
                size = slots * rows_each
                extra = array[size:].astype(F32)
                self.rider = self.rider + extra[:16] + extra[16:]
                array = array[:size].reshape(slots, rows_each, D)
            self.parts.append(array)

        def halve(self, *earlier):
            self.receive(*earlier)
            size = self.parts[0].shape[0] // 2
            outgoing = add(*[part[size:] for part in self.parts]).astype(BF16)
            self.parts = [part[:size] for part in self.parts]
            self.send(outgoing)
            return outgoing

        def total(self, *earlier):
            self.receive(*earlier)
            total = add(*self.parts)
            for bit in further:
                total = total + swap_rows(total, bit)
                if self.rider is not None:
                    self.rider = self.rider + swap_rows(self.rider, bit)
            self.held = total.astype(BF16)
            self.arrived = swap_step(self.held, 3)
            self.step = 2
            return self.held

        def double(self, *earlier):
            self.held = jnp.concatenate([self.held, after(self.arrived, *earlier)])
            if self.step >= 0:
                self.arrived = swap_step(self.held, self.step)
            else:
                self.arrived = swap_rows(self.held, 1)
            self.step -= 1
            return self.held

    def body(
        block_input,
        cotangent,
        gain_attn,
        w_query,
        w_key,
        w_value,
        w_out,
        gain_mlp,
        w_inner,
        outer_weight,
        bias_table,
        lengths,
        observed,
    ):
        count, here = block_input.shape[0], block_input.shape[1]
        tokens = count * here
        last = count - 1
        place = lax.axis_index("seq").astype(jnp.int32).reshape(1)
        code = codes()
        gain_attn_row = gain_attn.reshape(1, D)
        gain_mlp_row = gain_mlp.reshape(1, D)

        def in_hbm(array):
            return pltpu.with_memory_space_constraint(array, pltpu.HBM)

        stacked = (PAIRS, 2 * here, PACKED_LENGTH)
        one = (here, D)
        own = (count, here, D)
        full = (PACKED_LENGTH, D)
        square = whole((D, D))
        line = whole((1, D))

        x2 = swap_seq(block_input, 2)
        x1 = swap_seq(block_input, 1)
        seen = [observed] + [swap_seq(observed, j) for j in range(1, seq)]
        resident = (w_query, w_key, w_value, w_out, w_inner, outer_weight, cotangent)
        bias, *resident = call(
            functools.partial(prepare_kernel, here=here, seq=seq),
            (1,),
            (place,),
            (bias_table, *[in_hbm(array) for array in resident]),
            [whole(bias_table.shape)] + [ANYWHERE] * len(resident),
            [pltpu.VMEM(stacked, F32)]
            + [pltpu.VMEM(array.shape, array.dtype) for array in resident],
            [whole(stacked)] + [whole(array.shape) for array in resident],
            [pltpu.VMEM((H, SPAN), F32), pltpu.SemaphoreType.DMA((len(resident),))],
            name="prepare",
            vmem=4,
        )
        w_query, w_key, w_value, w_out, w_inner, outer_weight, cotangent = resident
        x2 = after(x2, bias)
        x3 = [swap_seq(x2[row], 1) for row in range(count)]

        kept = []
        kept_shapes = [
            pltpu.VMEM(one, BF16),
            pltpu.VMEM(one, BF16),
            pltpu.VMEM(one, F32),
            pltpu.VMEM(one, F32),
            pltpu.VMEM(full, BF16),
            pltpu.VMEM(one, BF16),
            pltpu.VMEM(full, BF16),
            pltpu.VMEM(full, BF16),
            pltpu.VMEM(stacked, BF16),
        ]
        for row in range(count):
            kept.append(
                call(
                    functools.partial(attention_kernel, row=row, here=here, seq=seq),
                    (1,),
                    (place, lengths),
                    [block_input, in_hbm(x1), in_hbm(x2), in_hbm(x3[row]), *seen]
                    + [gain_attn_row, w_query, w_key, w_value, w_out, gain_mlp_row, bias],
                    [one_row(own, row)] * 3
                    + [whole(one)]
                    + [whole(observed.shape)] * seq
                    + [line]
                    + [square] * 4
                    + [line, whole(stacked)],
                    kept_shapes,
                    [whole(shape.shape) for shape in kept_shapes],
                    flops=8 * here * D * PACKED_LENGTH,
                    name="attention",
                    vmem=12,
                )
            )
        normed_mlp = [part[0] for part in kept]

        flat = (tokens, D)
        steps = FF // FF_TILE // 2
        part_shape = (HALF, 2 * OUTER_ROWS, D)

        def mlp_part(own_half, nm):
            return call(
                functools.partial(mlp_kernel, rows=count, own_half=own_half),
                (steps,),
                (code,),
                (*nm, cotangent, w_inner, outer_weight),
                [whole(one)] * count + [whole(own), whole((D, FF)), whole((FF, D))],
                [pltpu.VMEM(flat, F32)] * 2 + [pltpu.HBM(part_shape, BF16)],
                [whole(flat)] * 2 + [whole(part_shape)],
                flops=6 * tokens * D * FF,
                name="mlp",
                vmem=20,
            )

        total_a, back_a, mlp_send = mlp_part(False, normed_mlp)
        mlp = Reduction(mlp_send, part_shape)
        nm = [after(normed_mlp[0], total_a)] + normed_mlp[1:]
        total_b, back_b, mlp_keep = mlp_part(True, nm)

        small_half = (HALF, 4 * SMALL_ROWS, D)
        small_wire = (HALF * 4 * SMALL_ROWS + 32, D)
        dx_half = (seq // 2, count, D, here)
        mlp.parts[0] = mlp_keep
        first_out = mlp.halve()
        (
            block_output,
            grad_middle,
            dx_keep,
            dx_send,
            small_keep,
            small_send,
            rider,
        ) = call(
            functools.partial(back_kernel, rows=count, here=here, seq=seq),
            (1,),
            (place, code),
            [array for part in kept for array in part]
            + [cotangent, total_a, total_b, back_a, back_b, gain_attn_row, gain_mlp_row]
            + [w_out, w_query, w_key, w_value, in_hbm(first_out)],
            [whole(shape.shape) for part in kept for shape in kept_shapes]
            + [whole(own)]
            + [whole(flat)] * 4
            + [line] * 2
            + [square] * 4
            + [ANYWHERE],
            [shaped(own, BF16), shaped(own, F32)]
            + [shaped(dx_half, BF16)] * 2
            + [shaped(small_half, BF16), shaped(small_wire, BF16), shaped((16, D), F32)],
            [whole(own)] * 2
            + [whole(dx_half)] * 2
            + [whole(small_half), whole(small_wire), whole((16, D))],
            [
                pltpu.VMEM(stacked, F32),
                pltpu.VMEM((8 * H, SPAN), F32),
                pltpu.VMEM((D, D), F32),
                pltpu.VMEM((D, D), F32),
                pltpu.VMEM((D, D), F32),
                pltpu.VMEM((D, D), F32),
            ],
            flops=20 * tokens * D * PACKED_LENGTH,
            name="attention_back",
            vmem=24,
        )
        small = Reduction(small_send, small_half, rider)
        small.parts[0] = small_keep
        dx_arrived = swap_step(dx_send, 2)
        done = mlp.halve(rider)
        done = small.halve(done)
        done = mlp.halve(done)
        done = small.halve(done)
        done = mlp.halve(done)
        done = small.halve(done)
        done = mlp.total(done)
        done = small.halve(done)
        done = mlp.double(done)
        done = small.total(done)
        done = mlp.double(done)
        done = small.double(done)
        done = small.double(done)
        done = mlp.double(done)
        half_sum = add(dx_keep, after(dx_arrived, done)).astype(BF16)
        dx_last = swap_step(half_sum[1], 3)
        done = small.double(half_sum)
        done = mlp.double(done)
        done = small.double(done)
        dx_shape = (count, D, here)
        input_grad = call(
            post_kernel,
            (count,),
            (),
            (half_sum[0], after(dx_last, done), block_input, grad_middle, gain_attn_row),
            [by_row(dx_shape)] * 2 + [by_row(own)] * 2 + [line],
            [shaped(own, BF16)],
            [by_row(own)],
            name="post",
        )[0]
        done = input_grad
        grad_outer, grad_inner = call(
            finish_mlp_kernel,
            (FF // FF_TILE,),
            (code,),
            (mlp.held, after(mlp.arrived, done)),
            [whole(part_shape)] * 2,
            [shaped((FF, D), F32), shaped((D, FF), F32)],
            [
                pl.BlockSpec((FF_TILE, D), lambda i, *_: (i, 0)),
                pl.BlockSpec((D, FF_TILE), lambda i, *_: (0, i)),
            ],
            [pltpu.VMEM((FF_TILE, D), F32)],
            name="finish_mlp",
        )
        grad_out, grad_query, grad_key, grad_value = call(
            finish_attention_kernel,
            (2,),
            (code,),
            (small.held, small.arrived),
            [whole(small_half)] * 2,
            [shaped((D, D), F32)] * 4,
            [pl.BlockSpec((D // 2, D), lambda i, *_: (i, 0))] * 4,
            name="finish_attention",
        )

        return (
            block_output,
            input_grad,
            small.rider[8],
            grad_query,
            grad_key,
            grad_value,
            grad_out,
            small.rider[9],
            grad_inner,
            grad_outer,
            small.rider[:H, :BUCKETS].T,
        )

    return body


def solution(mesh):
    split = P("rows", "seq", None)
    placed = (split, split) + (P(),) * 9 + (P("rows", None), P("rows", "seq"))
    return jax.shard_map(
        make_body(mesh.shape["rows"], mesh.shape["seq"]),
        mesh=mesh,
        in_specs=placed,
        out_specs=(split, split) + (P(),) * 9,
        check_vma=False,
    )
```

```python
import functools
import math

import jax
import jax.numpy as jnp
from jax import lax
from jax.experimental import pallas as pl
from jax.experimental.pallas import tpu as pltpu
from jax.sharding import PartitionSpec as P

D = 512
FF = 2048
H = 8
HD = 64
PAIRS = H // 2
BUCKETS = 32
PACKED_LENGTH = 512
EPSILON = 1e-06
BUCKET_EDGES = (12, 16, 23, 32, 46, 64, 91)
SPAN = 2 * PACKED_LENGTH
CHUNKS = 32
HALF = CHUNKS // 2
OUTER_ROWS = FF // CHUNKS
SMALL_ROWS = D // CHUNKS
FF_TILE = 512
MASKED = -1000000000.0
MIB = 1024 * 1024
F32 = jnp.float32
BF16 = jnp.bfloat16


SMALL_HALVINGS = 3
BEFORE_ROW = 2
ORDER = (
    "outer",
    "inner",
    "dx_start",
    "small_start",
    "small",
    "outer",
    "inner",
    "small",
    "outer",
    "inner",
    "small",
    "outer",
    "inner",
    "small",
    "outer",
    "inner",
    "small",
    "dx",
    "outer",
    "inner",
    "small",
    "finish_outer",
    "small",
    "finish_inner",
    "post",
    "small",
)


def dot(left, right, contract=(1, 0), precision=None):
    return lax.dot_general(
        left,
        right,
        (((contract[0],), (contract[1],)), ((), ())),
        preferred_element_type=F32,
        precision=precision,
    )


def xor_pairs(size, bit):
    return [(i, i ^ bit) for i in range(size)]


def bucket_of(relative):
    distance = jnp.abs(relative)
    beyond = jnp.full(distance.shape, 8, jnp.int32)
    for edge_value in BUCKET_EDGES:
        beyond = beyond + (distance >= edge_value).astype(jnp.int32)
    near = jnp.where(distance < 8, distance, beyond)
    return jnp.where(relative > 0, 16, 0).astype(jnp.int32) + near


def bucket_rows(shape, bucket_axis):
    place_axis = 1 - bucket_axis
    relative = lax.broadcasted_iota(jnp.int32, shape, place_axis) - PACKED_LENGTH
    return (bucket_of(relative) == lax.broadcasted_iota(jnp.int32, shape, bucket_axis)).astype(F32)


def split_heads(pair):
    lane = lax.broadcasted_iota(jnp.int32, pair.shape, 1)
    zero = jnp.zeros_like(pair)
    return jnp.concatenate(
        [jnp.where(lane < HD, pair, zero), jnp.where(lane >= HD, pair, zero)], axis=0
    )


def join_heads(stacked):
    half = stacked.shape[0] // 2
    lane = lax.broadcasted_iota(jnp.int32, (half, stacked.shape[1]), 1)
    return jnp.where(lane < HD, stacked[:half], stacked[half:])


def pack_kernel(x_ref, seen_ref, wire_ref, first_ref, *row_refs, here):
    count = x_ref.shape[0]
    flags = seen_ref[...].astype(F32)
    flags = jnp.concatenate([flags, jnp.zeros((16 - count, here), F32)], axis=0)
    tail = jnp.concatenate([flags, jnp.zeros((16, D - here), F32)], axis=1).astype(BF16)
    for row in range(count):
        wire_ref[row * here : (row + 1) * here] = x_ref[row]
        if row:
            row_refs[row - 1][...] = x_ref[row]
    wire_ref[count * here :] = tail
    first_ref[:here] = x_ref[0]
    first_ref[here:] = tail


def prepare_kernel(place_ref, table_ref, *refs, here, seq):
    count = (len(refs) - 3) // 2
    sources, bias_ref, targets = refs[:count], refs[count], refs[count + 1 : 2 * count + 1]
    line_ref, sems = refs[2 * count + 1 :]
    copies = [
        pltpu.make_async_copy(source, target, sems.at[i])
        for i, (source, target) in enumerate(zip(sources, targets))
    ]
    for copy in copies:
        copy.start()
    line_ref[...] = dot(
        table_ref[...], bucket_rows((BUCKETS, SPAN), 0), (0, 0), lax.Precision.HIGHEST
    )
    me = place_ref[0]
    for block in range(seq):
        offset = ((me ^ block) - me) * here + PACKED_LENGTH - here
        window = line_ref[:, pl.ds(pl.multiple_of(offset, 128), 2 * here)]
        for head in range(H):
            spread = jnp.broadcast_to(window[head : head + 1], (here, 2 * here))
            skewed = pltpu.roll(spread, here, 1, stride=1, stride_axis=0)
            row = (head % 2) * here
            bias_ref[head // 2, row : row + here, block * here : (block + 1) * here] = skewed[
                :, :here
            ]
    for copy in copies:
        copy.wait()


def attention_kernel(
    place_ref,
    lengths_ref,
    x0_ref,
    x1_ref,
    x2_ref,
    x3_ref,
    seen_ref,
    x1_tail_ref,
    x2_tail_ref,
    x3_tail_ref,
    gain_ref,
    gain_mlp_ref,
    bias_ref,
    wq_ref,
    wk_ref,
    wv_ref,
    w_out_ref,
    *refs,
    row,
    here,
    seq,
):
    (
        normed_mlp_ref,
        attended_ref,
        middle_ref,
        mixed_ref,
        normed_ref,
        q_ref,
        k_ref,
        v_ref,
        p_ref,
    ) = refs[-9:]
    me = place_ref[0]
    own_x = x0_ref[0].astype(F32)
    x = jnp.concatenate(
        [own_x] + [ref.astype(F32) for ref in (x1_ref[...], x2_ref[...], x3_ref[...])], axis=0
    )
    inv = lax.rsqrt(jnp.mean(x * x, -1, keepdims=True) + EPSILON)
    normed = (x * inv * gain_ref[...]).astype(BF16)
    normed_ref[...] = normed
    q = dot(normed[:here], wq_ref[...]).astype(BF16)
    k = dot(normed, wk_ref[...]).astype(BF16)
    v = dot(normed, wv_ref[...]).astype(BF16)
    q_ref[...] = q
    k_ref[...] = k
    v_ref[...] = v
    ends = [lengths_ref[row, 0]]
    for part in range(1, lengths_ref.shape[1]):
        ends.append(ends[-1] + lengths_ref[row, part])

    def segment(place):
        total = jnp.zeros(place.shape, jnp.int32)
        for end in ends:
            total = total + (end <= place).astype(jnp.int32)
        return total

    query_place = me * here + lax.broadcasted_iota(jnp.int32, (here, 1), 0)
    lane = lax.broadcasted_iota(jnp.int32, (1, here), 1)
    key_place = jnp.concatenate([(me ^ block) * here + lane for block in range(seq)], axis=1)
    seen = jnp.concatenate(
        [seen_ref[row : row + 1].astype(F32)]
        + [
            ref[...].astype(F32)[row : row + 1, :here]
            for ref in (x1_tail_ref, x2_tail_ref, x3_tail_ref)
        ],
        axis=1,
    )
    key_segment = jnp.where(seen == 1.0, segment(key_place), -1)
    allowed = (segment(query_place) == key_segment) | (query_place == key_place)
    allowed = jnp.concatenate([allowed.astype(jnp.int32)] * 2, axis=0) == 1
    attended = []
    for pair in range(PAIRS):
        lanes = slice(pair * 2 * HD, (pair + 1) * 2 * HD)
        scores = dot(split_heads(q[:, lanes]), k[:, lanes], (1, 1)) + bias_ref[pair]
        scores = jnp.where(allowed, scores, MASKED)
        exponent = jnp.exp(scores - jnp.max(scores, -1, keepdims=True))
        share = 1.0 / jnp.sum(exponent, -1, keepdims=True)
        probs = (exponent * share).astype(BF16)
        p_ref[pair] = probs
        mixed = join_heads(dot(probs, v[:, lanes]))
        mixed_ref[:, lanes] = mixed
        attended.append(mixed.astype(BF16))
    attended = jnp.concatenate(attended, axis=1)
    attended_ref[...] = attended
    middle = own_x + dot(attended, w_out_ref[...])
    middle_ref[...] = middle
    inv = lax.rsqrt(jnp.mean(middle * middle, -1, keepdims=True) + EPSILON)
    normed_mlp_ref[...] = (middle * inv * gain_mlp_ref[...]).astype(BF16)


def gelu_both(u):
    scale = 0.7978845608028654
    square = u * u
    t = jnp.tanh(u * (scale + (scale * 0.044715) * square))
    half_up = 0.5 + 0.5 * t
    slope = half_up + (0.5 * u) * (1.0 - t * t) * (scale + (3.0 * 0.044715 * scale) * square)
    return u * half_up, slope


def mlp_kernel(code_ref, *refs, rows, own_half):
    nm_refs = refs[:rows]
    g_ref, w_inner_ref, w_outer_ref, total_ref, back_ref, outer_ref, inner_ref = refs[rows:]
    step = pl.program_id(0)
    label = code_ref[1] if own_half else code_ref[2]
    normed = jnp.concatenate([ref[...] for ref in nm_refs], axis=0)
    g = g_ref[...].reshape(normed.shape)
    w_inner = w_inner_ref[...]
    w_outer = w_outer_ref[...]
    active_f, slope = gelu_both(dot(normed, w_inner))
    active = active_f.astype(BF16)
    grad_act = (dot(g, w_outer, (1, 1)) * slope).astype(BF16)

    @pl.when(step == 0)
    def _():
        total_ref[...] = jnp.zeros_like(total_ref)
        back_ref[...] = jnp.zeros_like(back_ref)

    total_ref[...] += dot(active, w_outer)
    back_ref[...] += dot(grad_act, w_inner, (1, 1))
    outer = dot(active, g, (0, 0)).astype(BF16)
    inner = dot(grad_act, normed, (0, 0)).astype(BF16)
    for part in range(FF_TILE // OUTER_ROWS):
        slot = (step * (FF_TILE // OUTER_ROWS) + part) ^ label
        rows = slice(part * OUTER_ROWS, (part + 1) * OUTER_ROWS)
        outer_ref[slot] = outer[rows]
        inner_ref[slot] = inner[rows]


def back_kernel(place_ref, code_ref, *refs, row, last, here, seq):
    _, attended_ref, middle_ref, mixed_ref, normed_ref, q_ref, k_ref, v_ref, p_ref = refs[:9]
    (
        g_ref,
        total_a_ref,
        total_b_ref,
        back_a_ref,
        back_b_ref,
        gain_mlp_ref,
        w_out_ref,
        wq_ref,
        wk_ref,
        wv_ref,
        _,
    ) = refs[9:20]
    refs = refs[20:]
    old = refs[:6] if row else None
    refs = refs[6:] if row else refs
    if last:
        gain_attn_ref = refs[0]
        refs = refs[1:]
    if row:
        refs = refs[1:]
    block_output_ref, grad_middle_ref, dx_keep_ref, dx_send_ref = refs[:4]
    if last:
        keep_ref, send_ref, rider_ref, line_ref = refs[4:8]
        sums = refs[8:14]
    else:
        sums = refs[4:10]

    def accumulate(which, value, part=None):
        if part is None:
            sums[which][...] = value + old[which][...] if row else value
        else:
            sums[which][part] = value + old[which][part] if row else value

    index = row
    tokens = slice(index * here, (index + 1) * here)
    middle = middle_ref[...]
    back = back_a_ref[tokens] + back_b_ref[tokens]
    block_output_ref[0] = (middle + total_a_ref[tokens] + total_b_ref[tokens]).astype(BF16)
    inv = lax.rsqrt(jnp.mean(middle * middle, -1, keepdims=True) + EPSILON)
    accumulate(5, jnp.sum(back * middle * inv, axis=0, keepdims=True))
    scaled = back * gain_mlp_ref[...]
    grad_middle = (
        g_ref[row].astype(F32)
        + inv * scaled
        - middle * (inv * inv * inv) * jnp.mean(scaled * middle, -1, keepdims=True)
    )
    grad_middle_ref[...] = grad_middle
    branch = grad_middle.astype(BF16)
    ga = dot(branch, w_out_ref[...], (1, 1)).astype(BF16)

    accumulate(0, dot(attended_ref[...], branch, (0, 0)))
    q = q_ref[...]
    k = k_ref[...]
    v = v_ref[...]
    normed = normed_ref[...]
    dq, dkt, dvt = [], [], []
    for pair in range(PAIRS):
        lanes = slice(pair * 2 * HD, (pair + 1) * 2 * HD)
        ga_split = split_heads(ga[:, lanes])
        q_split = split_heads(q[:, lanes])
        mixed = mixed_ref[:, lanes]
        probs = p_ref[pair]
        delta = jnp.sum(
            ga_split.astype(F32) * jnp.concatenate([mixed, mixed], axis=0), -1, keepdims=True
        )
        grad_probs = dot(ga_split, v[:, lanes], (1, 1))
        grad_scores_f = probs.astype(F32) * (grad_probs - delta)
        accumulate(4, grad_scores_f, pair)
        grad_scores = grad_scores_f.astype(BF16)
        dq.append(join_heads(dot(grad_scores, k[:, lanes])).astype(BF16))
        dkt.append(dot(q_split, grad_scores, (0, 0)).astype(BF16))
        dvt.append(dot(ga_split, probs, (0, 0)).astype(BF16))
    dq = jnp.concatenate(dq, axis=1)
    dkt = jnp.concatenate(dkt, axis=0)
    dvt = jnp.concatenate(dvt, axis=0)
    dxt = dot(wk_ref[...], dkt) + dot(wv_ref[...], dvt)
    own = dxt[:, :here] + dot(wq_ref[...], dq, (1, 1))
    pieces = [own] + [dxt[:, block * here : (block + 1) * here] for block in range(1, seq)]
    pieces = [piece.astype(BF16) for piece in pieces]
    dx_keep_ref[0] = pieces[0]
    dx_send_ref[1] = pieces[3]

    @pl.when(code_ref[0] == 0)
    def _():
        dx_keep_ref[1] = pieces[2]
        dx_send_ref[0] = pieces[1]

    @pl.when(code_ref[0] == 1)
    def _():
        dx_keep_ref[1] = pieces[1]
        dx_send_ref[0] = pieces[2]

    accumulate(1, dot(normed[:here], dq, (0, 0)))
    accumulate(2, dot(dkt, normed))
    accumulate(3, dot(dvt, normed))

    if not last:
        return
    me = place_ref[0]
    line_ref[...] = jnp.zeros_like(line_ref)
    for block in range(seq):
        offset = ((me ^ block) - me) * here + PACKED_LENGTH - here
        window = pl.ds(pl.multiple_of(offset, 128), 2 * here)
        for head in range(H):
            row = (head % 2) * here
            tile = sums[4][head // 2, row : row + here, block * here : (block + 1) * here]
            total = jnp.zeros((8, 2 * here), F32)
            empty = jnp.zeros((8, here), F32)
            for group in range(here // 8):
                wide = jnp.concatenate([tile[group * 8 : group * 8 + 8], empty], axis=1)
                total = total + pltpu.roll(wide, here - 8 * group, 1)
            line_ref[head * 8 : head * 8 + 8, window] += total
    lines = line_ref[...]
    sub = lax.broadcasted_iota(jnp.int32, lines.shape, 0)
    for bit in (1, 2, 4):
        lines = jnp.where((sub & bit) != 0, pltpu.roll(lines, SPAN - bit, 1), lines)
    by_head = jnp.concatenate(
        [jnp.sum(lines[h * 8 : h * 8 + 8], axis=0, keepdims=True) for h in range(H)], axis=0
    )
    table = dot(by_head, bucket_rows((SPAN, 128), 1), (1, 0), lax.Precision.HIGHEST)
    go_ref, gq_ref, gk_ref, gv_ref = sums[:4]
    gk_ref[...] = gk_ref[...].T
    gv_ref[...] = gv_ref[...].T
    gain = (
        wq_ref[...].astype(F32) * gq_ref[...]
        + wk_ref[...].astype(F32) * gk_ref[...]
        + wv_ref[...].astype(F32) * gv_ref[...]
    )
    gain_grad = dot(jnp.ones((8, D), F32), gain, (1, 1), lax.Precision.HIGHEST)
    rider = jnp.concatenate(
        [
            jnp.concatenate([table, jnp.zeros((8, D - 128), F32)], axis=1),
            gain_grad[:1] / gain_attn_ref[...],
            sums[5][...],
            jnp.zeros((6, D), F32),
        ],
        axis=0,
    )
    rider_ref[...] = rider
    high = rider.astype(BF16)
    base = HALF * 4 * SMALL_ROWS
    send_ref[base : base + 16, :] = high
    send_ref[base + 16 : base + 32, :] = (rider - high.astype(F32)).astype(BF16)
    core, label, other = code_ref[0], code_ref[1], code_ref[2]
    for index, grad_ref in enumerate((go_ref, gq_ref, gk_ref, gv_ref)):
        for slot in range(HALF):
            chunk = core * HALF + (slot ^ label)
            first = pl.multiple_of(chunk * SMALL_ROWS, SMALL_ROWS)
            rows_to = slice(index * SMALL_ROWS, (index + 1) * SMALL_ROWS)
            keep_ref[slot, rows_to] = grad_ref[pl.ds(first, SMALL_ROWS), :].astype(BF16)
            chunk = (1 - core) * HALF + (slot ^ other)
            first = pl.multiple_of(chunk * SMALL_ROWS, SMALL_ROWS)
            start = (slot * 4 + index) * SMALL_ROWS
            send_ref[start : start + SMALL_ROWS, :] = grad_ref[
                pl.ds(first, SMALL_ROWS), :
            ].astype(BF16)


def pick(code_ref, low_ref, high_ref, chunk, use):
    core, label, other = code_ref[0], code_ref[1], code_ref[2]

    @pl.when(core == chunk[0])
    def _():
        use(low_ref, chunk[1] ^ label)

    @pl.when(core != chunk[0])
    def _():
        use(high_ref, chunk[1] ^ other)


def finish_mlp_kernel(code_ref, low_ref, high_ref, out_ref, stage_ref, *, turned):
    step = pl.program_id(0)
    per_step = FF_TILE // OUTER_ROWS
    target = stage_ref if turned else out_ref
    for part in range(per_step):
        chunk = step * per_step + part
        rows = slice(part * OUTER_ROWS, (part + 1) * OUTER_ROWS)

        def use(ref, slot):
            target[rows, :] = ref[slot].astype(F32)

        pick(code_ref, low_ref, high_ref, (chunk // HALF, chunk % HALF), use)
    if turned:
        out_ref[...] = stage_ref[...].T


def finish_attention_kernel(code_ref, half_ref, *refs, own_half):
    out_refs = refs[-4:]
    label = code_ref[1] if own_half else code_ref[2]
    for part in range(HALF):
        rows = slice(part * SMALL_ROWS, (part + 1) * SMALL_ROWS)
        for index, out_ref in enumerate(out_refs):
            out_ref[rows, :] = half_ref[
                part ^ label, index * SMALL_ROWS : (index + 1) * SMALL_ROWS
            ].astype(F32)


def post_kernel(a_ref, b_ref, x_ref, gain_ref, *refs):
    grad_middle_refs, out_ref = refs[:-1], refs[-1]
    for row, grad_middle_ref in enumerate(grad_middle_refs):
        back = (a_ref[row].astype(F32) + b_ref[row].astype(F32)).T
        x = x_ref[row].astype(F32)
        inv = lax.rsqrt(jnp.mean(x * x, -1, keepdims=True) + EPSILON)
        scaled = back * gain_ref[...]
        grad = inv * scaled - x * (inv * inv * inv) * jnp.mean(scaled * x, -1, keepdims=True)
        out_ref[row] = (grad_middle_ref[...] + grad).astype(BF16)


ANYWHERE = pl.BlockSpec(memory_space=pl.ANY)


def whole(shape):
    return pl.BlockSpec(shape, lambda *_: (0,) * len(shape))


def by_row(shape):
    return pl.BlockSpec((1,) + shape[1:], lambda i, *_: (i,) + (0,) * (len(shape) - 1))


def one_row(shape, row):
    return pl.BlockSpec((1,) + shape[1:], lambda *_: (row,) + (0,) * (len(shape) - 1))


def shaped(shape, dtype):
    return jax.ShapeDtypeStruct(shape, dtype)


def call(
    kernel,
    grid,
    prefetch,
    inputs,
    in_specs,
    outs,
    out_specs,
    scratch=(),
    flops=0,
    name=None,
    aliases=None,
    vmem=16,
):
    return pl.pallas_call(
        kernel,
        out_shape=outs,
        grid_spec=pltpu.PrefetchScalarGridSpec(
            num_scalar_prefetch=len(prefetch),
            grid=grid,
            in_specs=in_specs,
            out_specs=out_specs,
            scratch_shapes=list(scratch),
        ),
        compiler_params=pltpu.CompilerParams(
            dimension_semantics=("arbitrary",) * len(grid), vmem_limit_bytes=vmem * MIB
        ),
        cost_estimate=pl.CostEstimate(flops=flops, bytes_accessed=flops // 256, transcendentals=0),
        input_output_aliases=aliases or {},
        name=name,
    )(*prefetch, *inputs)


def add(*parts):
    total = parts[0].astype(F32)
    for part in parts[1:]:
        total = total + part.astype(F32)
    return total


def make_body(rows, seq):
    both = ("rows", "seq")
    further = [1 << i for i in range(3, rows.bit_length() - 1)]

    def swap_rows(array, bit):
        return lax.ppermute(array, "rows", [(i, i ^ bit) for i in range(rows)])

    def swap_seq(array, bit):
        return lax.ppermute(array, "seq", [(i, i ^ bit) for i in range(seq)])

    def swap_step(array, step):
        def partner(r, z):
            first, second = ((0, 2), (0, 4)), ((1, 1), (1, 2))
            if r & 1:
                first, second = first[::-1], second[::-1]
            axis, bit = (first + second)[step]
            return (r, z ^ bit) if axis else (r ^ bit, z)

        pairs = []
        for r in range(rows):
            for z in range(seq):
                to_r, to_z = partner(r, z)
                pairs.append((r * seq + z, to_r * seq + to_z))
        return lax.ppermute(array, both, pairs)

    def codes():
        r, z = lax.axis_index("rows"), lax.axis_index("seq")
        core = r & 1
        b1, b2, z0, z1 = (r >> 1) & 1, (r >> 2) & 1, z & 1, (z >> 1) & 1
        even = b1 * 8 + b2 * 4 + z0 * 2 + z1
        odd = b2 * 8 + b1 * 4 + z1 * 2 + z0
        label = jnp.where(core == 0, even, odd)
        other = jnp.where(core == 0, odd, even)
        return jnp.stack([core, label, other]).astype(jnp.int32)

    def after(array, *earlier):
        return lax.optimization_barrier((array, *earlier))[0]

    def two_parts(rider):
        high = rider.astype(BF16)
        return [high, (rider - high.astype(F32)).astype(BF16)]

    class Reduction:
        def __init__(self, wire, shape, halvings, rider=None):
            self.rider = rider
            self.slots, self.rows_each = shape[:2]
            self.halvings = halvings
            self.step = 0
            self.spreading = False
            self.parts = [None]
            self.arrived = swap_rows(wire, 1)

        def send(self, outgoing):
            if self.rider is not None:
                flat = outgoing.reshape(-1, D)
                outgoing = jnp.concatenate([flat] + two_parts(self.rider), axis=0)
            self.slots = outgoing.shape[0] if self.rider is None else flat.shape[0] // self.rows_each
            self.arrived = swap_step(outgoing, self.step)
            self.step += 1

        def receive(self, earlier):
            array = after(self.arrived, *earlier)
            if self.rider is not None:
                size = self.slots * self.rows_each
                extra = array[size:].astype(F32)
                high, low = two_parts(self.rider)
                self.rider = (high.astype(F32) + low.astype(F32)) + (extra[:16] + extra[16:])
                array = array[:size].reshape(self.slots, self.rows_each, D)
            return array

        def advance(self, *earlier):
            if self.spreading:
                held = jnp.concatenate([self.held, after(self.arrived, *earlier)])
            else:
                self.parts.append(self.receive(earlier))
                if self.step < self.halvings:
                    size = self.parts[0].shape[0] // 2
                    outgoing = add(*[part[size:] for part in self.parts]).astype(BF16)
                    self.parts = [part[:size] for part in self.parts]
                    self.send(outgoing)
                    return outgoing
                held = add(*self.parts)
                if self.step < 4:
                    held = held.astype(BF16)
                    size = 8 >> self.step
                    order = [slot ^ size for slot in range(held.shape[0])]
                    self.parts = [held]
                    self.send(jnp.concatenate([held[slot : slot + 1] for slot in order]))
                    return held
                for bit in further:
                    held = held + swap_rows(held, bit)
                    if self.rider is not None:
                        self.rider = self.rider + swap_rows(self.rider, bit)
                held = held.astype(BF16)
                self.spreading = True
                self.step = self.halvings
            self.held = held
            self.step -= 1
            if self.step >= 0:
                self.arrived = swap_step(held, self.step)
            else:
                self.arrived = swap_rows(held, 1)
            return held

    def body(
        block_input,
        cotangent,
        gain_attn,
        w_query,
        w_key,
        w_value,
        w_out,
        gain_mlp,
        w_inner,
        outer_weight,
        bias_table,
        lengths,
        observed,
    ):
        count, here = block_input.shape[0], block_input.shape[1]
        tokens = count * here
        last = count - 1
        place = lax.axis_index("seq").astype(jnp.int32).reshape(1)
        code = codes()
        gain_attn_row = gain_attn.reshape(1, D)
        gain_mlp_row = gain_mlp.reshape(1, D)

        def in_hbm(array):
            return pltpu.with_memory_space_constraint(array, pltpu.HBM)

        stacked = (PAIRS, 2 * here, PACKED_LENGTH)
        one = (here, D)
        own = (count, here, D)
        full = (PACKED_LENGTH, D)
        square = whole((D, D))
        line = whole((1, D))

        wire, *x2 = call(
            functools.partial(pack_kernel, here=here),
            (1,),
            (),
            (block_input, observed),
            [whole(own), whole(observed.shape)],
            [shaped((tokens + 16, D), BF16), shaped((here + 16, D), BF16)]
            + [shaped(one, BF16)] * (count - 1),
            [whole((tokens + 16, D)), whole((here + 16, D))] + [whole(one)] * (count - 1),
            name="pack",
            vmem=8,
        )
        x2 = [swap_seq(x, 2) for x in x2]
        x1 = swap_seq(wire, 1)
        *x2, bias_table = lax.optimization_barrier((*x2, bias_table))
        x3 = [swap_seq(x, 1) for x in x2]
        resident = (w_query, w_key, w_value, w_out)
        resident = call(
            functools.partial(prepare_kernel, here=here, seq=seq),
            (1,),
            (place,),
            (bias_table, *[in_hbm(array) for array in resident]),
            [whole(bias_table.shape)] + [ANYWHERE] * len(resident),
            [pltpu.VMEM(stacked, F32)]
            + [pltpu.VMEM(array.shape, array.dtype) for array in resident],
            [whole(stacked)] + [whole(array.shape) for array in resident],
            [pltpu.VMEM((H, SPAN), F32), pltpu.SemaphoreType.DMA((len(resident),))],
            name="prepare",
            vmem=4,
        )
        kept = []
        kept_shapes = [
            pltpu.VMEM(one, BF16),
            pltpu.VMEM(one, BF16),
            pltpu.VMEM(one, F32),
            pltpu.VMEM(one, F32),
            pltpu.VMEM(full, BF16),
            pltpu.VMEM(one, BF16),
            pltpu.VMEM(full, BF16),
            pltpu.VMEM(full, BF16),
            pltpu.VMEM(stacked, BF16),
        ]
        for row in range(count):
            *resident, nm, attended, middle, mixed, normed, q, k, v, p = call(
                functools.partial(attention_kernel, row=row, here=here, seq=seq),
                (1,),
                (place, lengths),
                [block_input, x1, x2[row], x3[row], observed, x1, x2[0], x3[0]]
                + [gain_attn_row, gain_mlp_row, *resident],
                [
                    one_row(own, row),
                    pl.BlockSpec(one, lambda *_, row=row: (row, 0)),
                    whole(one),
                    whole(one),
                    whole(observed.shape),
                    pl.BlockSpec((16, D), lambda *_: (tokens // 16, 0)),
                    pl.BlockSpec((16, D), lambda *_: (here // 16, 0)),
                    pl.BlockSpec((16, D), lambda *_: (here // 16, 0)),
                ]
                + [line] * 2
                + [whole(stacked)]
                + [square] * 4,
                [pltpu.VMEM(array.shape, array.dtype) for array in resident] + kept_shapes,
                [ANYWHERE] * len(resident) + [whole(shape.shape) for shape in kept_shapes],
                flops=8 * here * D * PACKED_LENGTH,
                name="attention",
                vmem=12,
                aliases={12 + i: i for i in range(len(resident))},
            )
            kept.append((nm, attended, middle, mixed, normed, q, k, v, p))
        _, w_query, w_key, w_value, w_out = resident
        normed_mlp = [part[0] for part in kept]

        flat = (tokens, D)
        steps = FF // FF_TILE // 2
        part_shape = (HALF, OUTER_ROWS, D)

        def mlp_part(own_half, nm):
            def tile(i, code):
                return (code[0] if own_half else 1 - code[0]) * steps + i

            return call(
                functools.partial(mlp_kernel, rows=count, own_half=own_half),
                (steps,),
                (code,),
                [*nm, in_hbm(cotangent), in_hbm(w_inner), in_hbm(outer_weight)],
                [whole(one)] * count
                + [
                    whole(own),
                    pl.BlockSpec((D, FF_TILE), lambda i, n: (0, tile(i, n))),
                    pl.BlockSpec((FF_TILE, D), lambda i, n: (tile(i, n), 0)),
                ],
                [pltpu.VMEM(flat, F32)] * 2 + [pltpu.HBM(part_shape, BF16)] * 2,
                [whole(flat)] * 2 + [whole(part_shape)] * 2,
                flops=6 * tokens * D * FF,
                name="mlp",
                vmem=20,
            )

        total_a, back_a, outer_send, inner_send = mlp_part(False, normed_mlp)
        chains = {
            "outer": Reduction(outer_send, part_shape, 3),
            "inner": Reduction(inner_send, part_shape, 3),
        }
        nm = [after(normed_mlp[0], total_a)] + normed_mlp[1:]
        total_b, back_b, outer_keep, inner_keep = mlp_part(True, nm)
        chains["outer"].parts[0] = outer_keep
        chains["inner"].parts[0] = inner_keep

        small_half = (HALF, 4 * SMALL_ROWS, D)
        small_wire = (HALF * 4 * SMALL_ROWS + 32, D)
        done = chains["outer"].advance()
        done = chains["inner"].advance(done)
        dx_half = (seq // 2, D, here)
        sum_shapes = [pltpu.VMEM((D, D), F32)] * 4
        sum_shapes += [pltpu.VMEM(stacked, F32), pltpu.VMEM((1, D), F32)]
        sums, block_output = (), ()
        grad_middles, dx_keeps, dx_sends = [], [], []
        for row in range(count):
            end = row == count - 1
            inputs = [*kept[row], cotangent, total_a, total_b, back_a, back_b, gain_mlp_row]
            inputs += [w_out, w_query, w_key, w_value, done, *sums]
            specs = [whole(shape.shape) for shape in kept_shapes] + [whole(own)]
            specs += [whole(flat)] * 4 + [line] + [square] * 4 + [ANYWHERE]
            specs += [whole(shape.shape) for shape in sum_shapes[: len(sums)]]
            if end:
                inputs.append(gain_attn_row)
                specs.append(line)
            if row:
                inputs.append(block_output)
                specs.append(ANYWHERE)
            aliases = {len(inputs) + 1: 0} if row else {}
            outs = [pltpu.HBM(own, BF16), pltpu.HBM(one, F32)] + [shaped(dx_half, BF16)] * 2
            out_specs = [one_row(own, row), whole(one)] + [whole(dx_half)] * 2
            if end:
                outs += [shaped(small_half, BF16), shaped(small_wire, BF16), shaped((16, D), F32)]
                out_specs += [whole(small_half), whole(small_wire), whole((16, D))]
                scratch = [pltpu.VMEM((8 * H, SPAN), F32)]
                scratch += [pltpu.VMEM(shape.shape, shape.dtype) for shape in sum_shapes]
            else:
                outs += sum_shapes
                out_specs += [whole(shape.shape) for shape in sum_shapes]
                scratch = []
                if row:
                    aliases |= {22 + i: 4 + i for i in range(len(sums))}
            block_output, grad_middle, dx_keep, dx_send, *sums = call(
                functools.partial(back_kernel, row=row, last=end, here=here, seq=seq),
                (1,),
                (place, code),
                inputs,
                specs,
                outs,
                out_specs,
                scratch,
                flops=20 * here * D * PACKED_LENGTH,
                name="attention_back",
                vmem=24 if end else 14,
                aliases=aliases,
            )
            done = grad_middle
            if row == BEFORE_ROW - 1:
                done = chains["outer"].advance(done)
                done = chains["inner"].advance(done)
            grad_middles.append(grad_middle)
            dx_keeps.append(dx_keep)
            dx_sends.append(dx_send)
        small_keep, small_send, rider = sums
        dx_arrived = [swap_step(dx_send, 2) for dx_send in dx_sends[:-1]]
        for event in ORDER:
            if event in chains:
                done = chains[event].advance(done)
            elif event == "small_start":
                chains["small"] = Reduction(
                    after(small_send, done), small_half, SMALL_HALVINGS, rider
                )
                chains["small"].parts[0] = small_keep
            elif event == "dx_start":
                *dx_arrived, done = lax.optimization_barrier((*dx_arrived, done))
                dx_half = [
                    [add(x[i], y[i]).astype(BF16) for x, y in zip(dx_keeps, dx_arrived)]
                    for i in range(2)
                ]
                dx_arrived = swap_step(after(dx_sends[-1], dx_half[0][-1]), 2)
                done = dx_half[1][-1]
            elif event == "dx":
                dx_arrived = after(dx_arrived, done)
                half_kept, half_sent = [
                    jnp.stack(dx_half[i] + [add(dx_keeps[-1][i], dx_arrived[i]).astype(BF16)])
                    for i in range(2)
                ]
                dx_last = swap_step(half_sent, 3)
                done = half_sent
            elif event == "post":
                input_grad = call(
                    post_kernel,
                    (1,),
                    (),
                    (half_kept, after(dx_last, done), block_input, gain_attn_row, *grad_middles),
                    [whole(half_kept.shape)] * 2 + [whole(own), line] + [whole(one)] * count,
                    [shaped(own, BF16)],
                    [whole(own)],
                    name="post",
                )[0]
                done = input_grad
            elif event == "finish_outer":
                chain = chains["outer"]
                grad_outer = call(
                    functools.partial(finish_mlp_kernel, turned=False),
                    (FF // FF_TILE,),
                    (code,),
                    (chain.held, after(chain.arrived, done)),
                    [whole(part_shape)] * 2,
                    [shaped((FF, D), F32)],
                    [pl.BlockSpec((FF_TILE, D), lambda i, *_: (i, 0))],
                    [pltpu.VMEM((8, 128), F32)],
                    name="finish_outer",
                )[0]
                done = grad_outer
            elif event == "finish_inner":
                chain = chains["inner"]
                grad_inner = call(
                    functools.partial(finish_mlp_kernel, turned=True),
                    (FF // FF_TILE,),
                    (code,),
                    (chain.held, after(chain.arrived, done)),
                    [whole(part_shape)] * 2,
                    [shaped((D, FF), F32)],
                    [pl.BlockSpec((D, FF_TILE), lambda i, *_: (0, i))],
                    [pltpu.VMEM((FF_TILE, D), F32)],
                    name="finish_inner",
                )[0]
                done = grad_inner
        chain = chains["small"]
        grads = ()
        for own_half in (True, False):
            half = chain.held if own_half else after(chain.arrived, grads[0])

            def half_of(i, code):
                return (code[0] if own_half else 1 - code[0], 0)

            grads = call(
                functools.partial(finish_attention_kernel, own_half=own_half),
                (1,),
                (code,),
                (half, *grads),
                [whole(small_half)] + [ANYWHERE] * len(grads),
                [shaped((D, D), F32)] * 4,
                [pl.BlockSpec((D // 2, D), half_of)] * 4,
                name="finish_attention",
                aliases={2 + i: i for i in range(len(grads))},
            )
        grad_out, grad_query, grad_key, grad_value = grads
        rider = chain.rider

        return (
            block_output,
            input_grad,
            rider[8],
            grad_query,
            grad_key,
            grad_value,
            grad_out,
            rider[9],
            grad_inner,
            grad_outer,
            rider[:H, :BUCKETS].T,
        )

    return body


def solution(mesh):
    split = P("rows", "seq", None)
    placed = (split, split) + (P(),) * 9 + (P("rows", None), P("rows", "seq"))
    return jax.shard_map(
        make_body(mesh.shape["rows"], mesh.shape["seq"]),
        mesh=mesh,
        in_specs=placed,
        out_specs=(split, split) + (P(),) * 9,
        check_vma=False,
    )
```

```python
import functools
import math

import jax
import jax.numpy as jnp
from jax import lax
from jax.experimental import pallas as pl
from jax.experimental.pallas import tpu as pltpu
from jax.sharding import PartitionSpec as P

D = 512
FF = 2048
H = 8
HD = 64
PAIRS = H // 2
BUCKETS = 32
PACKED_LENGTH = 512
EPSILON = 1e-06
BUCKET_EDGES = (12, 16, 23, 32, 46, 64, 91)
SPAN = 2 * PACKED_LENGTH
CHUNKS = 32
HALF = CHUNKS // 2
OUTER_ROWS = FF // CHUNKS
SMALL_ROWS = D // CHUNKS
FF_TILE = 512
HALF_FF = FF // 2
MASKED = -1000000000.0
MIB = 1024 * 1024
F32 = jnp.float32
BF16 = jnp.bfloat16


SMALL_HALVINGS = 3
BEFORE_ROW = 2
EARLY = ("outer", "inner", )
ORDER = (
    "outer",
    "small_start",
    "rider",
    "inner",
    "outer",
    "small",
    "dx_first",
    "inner",
    "outer",
    "inner",
    "small",
    "small",
    "dx_start",
    "outer",
    "small",
    "inner",
    "outer",
    "inner",
    "small",
    "dx",
    "outer",
    "small",
    "small",
    "post",
    "inner",
    "finish_outer",
    "finish_inner",
    "small",
)


def dot(left, right, contract=(1, 0), precision=None):
    return lax.dot_general(
        left,
        right,
        (((contract[0],), (contract[1],)), ((), ())),
        preferred_element_type=F32,
        precision=precision,
    )


def xor_pairs(size, bit):
    return [(i, i ^ bit) for i in range(size)]


def bucket_of(relative):
    distance = jnp.abs(relative)
    beyond = jnp.full(distance.shape, 8, jnp.int32)
    for edge_value in BUCKET_EDGES:
        beyond = beyond + (distance >= edge_value).astype(jnp.int32)
    near = jnp.where(distance < 8, distance, beyond)
    return jnp.where(relative > 0, 16, 0).astype(jnp.int32) + near


def bucket_rows(shape, bucket_axis):
    place_axis = 1 - bucket_axis
    relative = lax.broadcasted_iota(jnp.int32, shape, place_axis) - PACKED_LENGTH
    return (bucket_of(relative) == lax.broadcasted_iota(jnp.int32, shape, bucket_axis)).astype(F32)


def split_heads(pair):
    lane = lax.broadcasted_iota(jnp.int32, pair.shape, 1)
    zero = jnp.zeros_like(pair)
    return jnp.concatenate(
        [jnp.where(lane < HD, pair, zero), jnp.where(lane >= HD, pair, zero)], axis=0
    )


def join_heads(stacked):
    half = stacked.shape[0] // 2
    lane = lax.broadcasted_iota(jnp.int32, (half, stacked.shape[1]), 1)
    return jnp.where(lane < HD, stacked[:half], stacked[half:])


def pack_kernel(x_ref, seen_ref, *out_refs, here, rows, tail):
    count = x_ref.shape[0]
    for out_ref, group in zip(out_refs, rows):
        for place, row in enumerate(group):
            out_ref[place * here : (place + 1) * here] = x_ref[row]
    if tail:
        flags = seen_ref[...].astype(F32)
        flags = jnp.concatenate([flags, jnp.zeros((16 - count, here), F32)], axis=0)
        flags = jnp.concatenate([flags, jnp.zeros((16, D - here), F32)], axis=1)
        out_refs[0][len(rows[0]) * here :] = flags.astype(BF16)


def split_kernel(wire_ref, *out_refs, here):
    for row, out_ref in enumerate(out_refs):
        out_ref[:here] = wire_ref[row * here : (row + 1) * here]
    out_refs[0][here:] = wire_ref[len(out_refs) * here :]


def prepare_kernel(place_ref, table_ref, *refs, here, seq):
    count = (len(refs) - 3) // 2
    sources, bias_ref, targets = refs[:count], refs[count], refs[count + 1 : 2 * count + 1]
    line_ref, sems = refs[2 * count + 1 :]
    copies = [
        pltpu.make_async_copy(source, target, sems.at[i])
        for i, (source, target) in enumerate(zip(sources, targets))
    ]
    for copy in copies:
        copy.start()
    line_ref[...] = dot(
        table_ref[...], bucket_rows((BUCKETS, SPAN), 0), (0, 0), lax.Precision.HIGHEST
    )
    me = place_ref[0]
    for block in range(seq):
        offset = ((me ^ block) - me) * here + PACKED_LENGTH - here
        window = line_ref[:, pl.ds(pl.multiple_of(offset, 128), 2 * here)]
        for head in range(H):
            spread = jnp.broadcast_to(window[head : head + 1], (here, 2 * here))
            skewed = pltpu.roll(spread, here, 1, stride=1, stride_axis=0)
            row = (head % 2) * here
            bias_ref[head // 2, row : row + here, block * here : (block + 1) * here] = skewed[
                :, :here
            ]
    for copy in copies:
        copy.wait()


def attention_kernel(
    place_ref,
    lengths_ref,
    code_ref,
    x0_ref,
    x1_ref,
    x2_ref,
    x3_ref,
    seen_ref,
    x1_tail_ref,
    x2_tail_ref,
    x3_tail_ref,
    gain_ref,
    gain_mlp_ref,
    bias_ref,
    wq_ref,
    wk_ref,
    wv_ref,
    w_out_ref,
    *refs,
    row,
    here,
    seq,
    fetch,
):
    if fetch:
        copies = [
            pltpu.make_async_copy(refs[i], refs[i - 4], refs[-1].at[i]) for i in range(3)
        ]
        for copy in copies:
            copy.start()
        refs = refs[:-4]
    (
        normed_mlp_ref,
        attended_ref,
        middle_ref,
        mixed_ref,
        normed_ref,
        q_ref,
        k_ref,
        v_ref,
        p_ref,
    ) = refs[-9:]
    me = place_ref[0]
    own_x = x0_ref[0].astype(F32)
    x = jnp.concatenate(
        [own_x] + [ref.astype(F32) for ref in (x1_ref[...], x2_ref[...], x3_ref[...])], axis=0
    )
    inv = lax.rsqrt(jnp.mean(x * x, -1, keepdims=True) + EPSILON)
    normed = (x * inv * gain_ref[...]).astype(BF16)
    normed_ref[...] = normed
    q = dot(normed[:here], wq_ref[...]).astype(BF16)
    k = dot(normed, wk_ref[...]).astype(BF16)
    v = dot(normed, wv_ref[...]).astype(BF16)
    q_ref[...] = q
    k_ref[...] = k
    v_ref[...] = v
    ends = [lengths_ref[row, 0]]
    for part in range(1, lengths_ref.shape[1]):
        ends.append(ends[-1] + lengths_ref[row, part])

    def segment(place):
        total = jnp.zeros(place.shape, jnp.int32)
        for end in ends:
            total = total + (end <= place).astype(jnp.int32)
        return total

    query_place = me * here + lax.broadcasted_iota(jnp.int32, (here, 1), 0)
    lane = lax.broadcasted_iota(jnp.int32, (1, here), 1)
    key_place = jnp.concatenate([(me ^ block) * here + lane for block in range(seq)], axis=1)
    seen = jnp.concatenate(
        [seen_ref[row : row + 1].astype(F32)]
        + [
            ref[...].astype(F32)[row : row + 1, :here]
            for ref in (x1_tail_ref, x2_tail_ref, x3_tail_ref)
        ],
        axis=1,
    )
    key_segment = jnp.where(seen == 1.0, segment(key_place), -1)
    allowed = (segment(query_place) == key_segment) | (query_place == key_place)
    allowed = jnp.concatenate([allowed.astype(jnp.int32)] * 2, axis=0) == 1
    attended = []
    for pair in range(PAIRS):
        lanes = slice(pair * 2 * HD, (pair + 1) * 2 * HD)
        scores = dot(split_heads(q[:, lanes]), k[:, lanes], (1, 1)) + bias_ref[pair]
        scores = jnp.where(allowed, scores, MASKED)
        exponent = jnp.exp(scores - jnp.max(scores, -1, keepdims=True))
        ones = jnp.ones((PACKED_LENGTH, 128), BF16)
        both = dot(exponent.astype(BF16), jnp.concatenate([v[:, lanes], ones], axis=1))
        share = 1.0 / both[:, 128:]
        mixed = join_heads(both[:, :128] * share)
        for first in range(0, PACKED_LENGTH, 128):
            part = slice(first, first + 128)
            p_ref[pair, :, part] = (exponent[:, part] * share).astype(BF16)
        mixed_ref[:, lanes] = mixed
        attended.append(mixed.astype(BF16))
    attended = jnp.concatenate(attended, axis=1)
    attended_ref[...] = attended
    middle = own_x + dot(attended, w_out_ref[...])
    middle_ref[...] = middle
    inv = lax.rsqrt(jnp.mean(middle * middle, -1, keepdims=True) + EPSILON)
    normed_mlp_ref[...] = (middle * inv * gain_mlp_ref[...]).astype(BF16)
    if fetch:
        for copy in copies:
            copy.wait()


def gelu_both(u):
    scale = 0.7978845608028654
    square = u * u
    t = jnp.tanh(u * (scale + (scale * 0.044715) * square))
    half_up = 0.5 + 0.5 * t
    slope = half_up + (0.5 * u) * (1.0 - t * t) * (scale + (3.0 * 0.044715 * scale) * square)
    return u * half_up, slope


def mlp_kernel(code_ref, *refs, rows, own_half):
    nm_refs = refs[:rows]
    g_ref, w_inner_ref, w_outer_ref = refs[rows : rows + 3]
    refs = refs[rows + 3 :]
    total_ref, back_ref, outer_ref, inner_ref = refs
    label = code_ref[1] if own_half else code_ref[2]
    normed = jnp.concatenate([ref[...] for ref in nm_refs], axis=0)
    g = g_ref[...].reshape(normed.shape)
    half = code_ref[0] if own_half else 1 - code_ref[0]
    hidden = pl.ds(pl.multiple_of(half * HALF_FF, HALF_FF), HALF_FF)
    w_inner = w_inner_ref[:, hidden]
    w_outer = w_outer_ref[hidden, :]
    active_f, slope = gelu_both(dot(normed, w_inner))
    active = active_f.astype(BF16)
    grad_act = (dot(g, w_outer, (1, 1)) * slope).astype(BF16)
    total_ref[...] = dot(active, w_outer)
    back_ref[...] = dot(grad_act, w_inner, (1, 1))
    outer = dot(active, g, (0, 0)).astype(BF16)
    inner = dot(grad_act, normed, (0, 0)).astype(BF16)
    for part in range(HALF):
        slot = part ^ label
        rows = slice(part * OUTER_ROWS, (part + 1) * OUTER_ROWS)
        outer_ref[slot] = outer[rows]
        inner_ref[slot] = inner[rows]


def back_kernel(place_ref, code_ref, *refs, row, last, here, seq):
    _, attended_ref, middle_ref, mixed_ref, normed_ref, q_ref, k_ref, v_ref, p_ref = refs[:9]
    (
        g_ref,
        total_a_ref,
        total_b_ref,
        back_a_ref,
        back_b_ref,
        gain_mlp_ref,
        w_out_ref,
        wq_ref,
        wk_ref,
        wv_ref,
        _,
    ) = refs[9:20]
    refs = refs[20:]
    old = refs[:6] if row else None
    refs = refs[6:] if row else refs
    if row:
        refs = refs[1:]
    block_output_ref, grad_middle_ref, dx_keep_ref, dx_send_ref = refs[:4]
    sums = refs[4:10]
    if last:
        keep_ref, send_ref = refs[10:12]

    def accumulate(which, value, part=None):
        if part is None:
            sums[which][...] = value + old[which][...] if row else value
        else:
            sums[which][part] = value + old[which][part] if row else value

    index = row
    tokens = slice(index * here, (index + 1) * here)
    middle = middle_ref[...]
    back = back_a_ref[tokens] + back_b_ref[tokens]
    block_output_ref[0] = (middle + total_a_ref[tokens] + total_b_ref[tokens]).astype(BF16)
    inv = lax.rsqrt(jnp.mean(middle * middle, -1, keepdims=True) + EPSILON)
    accumulate(5, jnp.sum(back * middle * inv, axis=0, keepdims=True))
    scaled = back * gain_mlp_ref[...]
    grad_middle = (
        g_ref[row].astype(F32)
        + inv * scaled
        - middle * (inv * inv * inv) * jnp.mean(scaled * middle, -1, keepdims=True)
    )
    grad_middle_ref[...] = grad_middle
    branch = grad_middle.astype(BF16)
    ga = dot(branch, w_out_ref[...], (1, 1)).astype(BF16)

    accumulate(0, dot(attended_ref[...], branch, (0, 0)))
    q = q_ref[...]
    k = k_ref[...]
    v = v_ref[...]
    normed = normed_ref[...]
    dq, dkt, dvt = [], [], []
    for pair in range(PAIRS):
        lanes = slice(pair * 2 * HD, (pair + 1) * 2 * HD)
        ga_split = split_heads(ga[:, lanes])
        q_split = split_heads(q[:, lanes])
        mixed = mixed_ref[:, lanes]
        probs = p_ref[pair]
        delta = jnp.sum(
            ga_split.astype(F32) * jnp.concatenate([mixed, mixed], axis=0), -1, keepdims=True
        )
        grad_probs = dot(ga_split, v[:, lanes], (1, 1))
        grad_scores_f = probs.astype(F32) * (grad_probs - delta)
        accumulate(4, grad_scores_f, pair)
        grad_scores = grad_scores_f.astype(BF16)
        dq.append(join_heads(dot(grad_scores, k[:, lanes])).astype(BF16))
        dkt.append(dot(q_split, grad_scores, (0, 0)).astype(BF16))
        dvt.append(dot(ga_split, probs, (0, 0)).astype(BF16))
    dq = jnp.concatenate(dq, axis=1)
    dkt = jnp.concatenate(dkt, axis=0)
    dvt = jnp.concatenate(dvt, axis=0)
    chunks = [slice(first, first + 128) for first in range(0, D, 128)]
    pieces = [[] for _ in range(seq)]
    for rows in chunks:
        dxt = dot(wk_ref[rows], dkt) + dot(wv_ref[rows], dvt)
        own = dxt[:, :here] + dot(wq_ref[rows], dq, (1, 1))
        pieces[0].append(own.astype(BF16))
        for block in range(1, seq):
            pieces[block].append(dxt[:, block * here : (block + 1) * here].astype(BF16))
    pieces = [jnp.concatenate(piece, axis=0) for piece in pieces]
    dx_keep_ref[0] = pieces[0]
    dx_send_ref[1] = pieces[3]

    @pl.when(code_ref[0] == 0)
    def _():
        dx_keep_ref[1] = pieces[2]
        dx_send_ref[0] = pieces[1]

    @pl.when(code_ref[0] == 1)
    def _():
        dx_keep_ref[1] = pieces[1]
        dx_send_ref[0] = pieces[2]

    accumulate(1, dot(normed[:here], dq, (0, 0)))
    for rows in chunks:
        accumulate(2, dot(dkt[rows], normed), rows)
        accumulate(3, dot(dvt[rows], normed), rows)

    if not last:
        return
    go_ref, gq_ref, gk_ref, gv_ref = sums[:4]
    gk_ref[...] = gk_ref[...].T
    gv_ref[...] = gv_ref[...].T
    core, label, other = code_ref[0], code_ref[1], code_ref[2]
    for index, grad_ref in enumerate((go_ref, gq_ref, gk_ref, gv_ref)):
        for slot in range(HALF):
            chunk = core * HALF + (slot ^ label)
            first = pl.multiple_of(chunk * SMALL_ROWS, SMALL_ROWS)
            rows_to = slice(index * SMALL_ROWS, (index + 1) * SMALL_ROWS)
            keep_ref[slot, rows_to] = grad_ref[pl.ds(first, SMALL_ROWS), :].astype(BF16)
            chunk = (1 - core) * HALF + (slot ^ other)
            first = pl.multiple_of(chunk * SMALL_ROWS, SMALL_ROWS)
            send_ref[slot, rows_to] = grad_ref[pl.ds(first, SMALL_ROWS), :].astype(BF16)


def rider_kernel(
    place_ref,
    gq_ref,
    gk_ref,
    gv_ref,
    table_sum_ref,
    gain_mlp_ref,
    gain_attn_ref,
    wq_ref,
    wk_ref,
    wv_ref,
    rider_ref,
    line_ref,
    *,
    here,
    seq,
):
    me = place_ref[0]
    line_ref[...] = jnp.zeros_like(line_ref)
    for block in range(seq):
        offset = ((me ^ block) - me) * here + PACKED_LENGTH - here
        window = pl.ds(pl.multiple_of(offset, 128), 2 * here)
        for head in range(H):
            row = (head % 2) * here
            tile = table_sum_ref[head // 2, row : row + here, block * here : (block + 1) * here]
            total = jnp.zeros((8, 2 * here), F32)
            empty = jnp.zeros((8, here), F32)
            for group in range(here // 8):
                wide = jnp.concatenate([tile[group * 8 : group * 8 + 8], empty], axis=1)
                total = total + pltpu.roll(wide, here - 8 * group, 1)
            line_ref[head * 8 : head * 8 + 8, window] += total
    lines = line_ref[...]
    sub = lax.broadcasted_iota(jnp.int32, lines.shape, 0)
    for bit in (1, 2, 4):
        lines = jnp.where((sub & bit) != 0, pltpu.roll(lines, SPAN - bit, 1), lines)
    by_head = jnp.concatenate(
        [jnp.sum(lines[h * 8 : h * 8 + 8], axis=0, keepdims=True) for h in range(H)], axis=0
    )
    table = dot(by_head, bucket_rows((SPAN, 128), 1), (1, 0), lax.Precision.HIGHEST)
    gain = (
        wq_ref[...].astype(F32) * gq_ref[...]
        + wk_ref[...].astype(F32) * gk_ref[...]
        + wv_ref[...].astype(F32) * gv_ref[...]
    )
    gain_grad = dot(jnp.ones((8, D), F32), gain, (1, 1), lax.Precision.HIGHEST)
    rider = jnp.concatenate(
        [
            jnp.concatenate([table, jnp.zeros((8, D - 128), F32)], axis=1),
            gain_grad[:1] / gain_attn_ref[...],
            gain_mlp_ref[...],
            jnp.zeros((6, D), F32),
        ],
        axis=0,
    )
    rider_ref[...] = rider


def pick(code_ref, low_ref, high_ref, chunk, use):
    core, label, other = code_ref[0], code_ref[1], code_ref[2]

    @pl.when(core == chunk[0])
    def _():
        use(low_ref, chunk[1] ^ label)

    @pl.when(core != chunk[0])
    def _():
        use(high_ref, chunk[1] ^ other)


def finish_mlp_kernel(code_ref, low_ref, high_ref, out_ref, stage_ref, *, turned):
    step = pl.program_id(0)
    per_step = FF_TILE // OUTER_ROWS
    target = stage_ref if turned else out_ref
    for part in range(per_step):
        chunk = step * per_step + part
        rows = slice(part * OUTER_ROWS, (part + 1) * OUTER_ROWS)

        def use(ref, slot):
            target[rows, :] = ref[slot].astype(F32)

        pick(code_ref, low_ref, high_ref, (chunk // HALF, chunk % HALF), use)
    if turned:
        out_ref[...] = stage_ref[...].T


def finish_attention_kernel(code_ref, half_ref, *refs, own_half):
    out_refs = refs[-4:]
    label = code_ref[1] if own_half else code_ref[2]
    for part in range(HALF):
        rows = slice(part * SMALL_ROWS, (part + 1) * SMALL_ROWS)
        for index, out_ref in enumerate(out_refs):
            out_ref[rows, :] = half_ref[
                part ^ label, index * SMALL_ROWS : (index + 1) * SMALL_ROWS
            ].astype(F32)


def post_kernel(a_ref, b_ref, x_ref, gain_ref, *refs):
    grad_middle_refs, out_ref = refs[:-1], refs[-1]
    for row, grad_middle_ref in enumerate(grad_middle_refs):
        back = (a_ref[row].astype(F32) + b_ref[row].astype(F32)).T
        x = x_ref[row].astype(F32)
        inv = lax.rsqrt(jnp.mean(x * x, -1, keepdims=True) + EPSILON)
        scaled = back * gain_ref[...]
        grad = inv * scaled - x * (inv * inv * inv) * jnp.mean(scaled * x, -1, keepdims=True)
        out_ref[row] = (grad_middle_ref[...] + grad).astype(BF16)


ANYWHERE = pl.BlockSpec(memory_space=pl.ANY)


def whole(shape):
    return pl.BlockSpec(shape, lambda *_: (0,) * len(shape))


def by_row(shape):
    return pl.BlockSpec((1,) + shape[1:], lambda i, *_: (i,) + (0,) * (len(shape) - 1))


def one_row(shape, row):
    return pl.BlockSpec((1,) + shape[1:], lambda *_: (row,) + (0,) * (len(shape) - 1))


def shaped(shape, dtype):
    return jax.ShapeDtypeStruct(shape, dtype)


def call(
    kernel,
    grid,
    prefetch,
    inputs,
    in_specs,
    outs,
    out_specs,
    scratch=(),
    flops=0,
    name=None,
    aliases=None,
    vmem=16,
):
    return pl.pallas_call(
        kernel,
        out_shape=outs,
        grid_spec=pltpu.PrefetchScalarGridSpec(
            num_scalar_prefetch=len(prefetch),
            grid=grid,
            in_specs=in_specs,
            out_specs=out_specs,
            scratch_shapes=list(scratch),
        ),
        compiler_params=pltpu.CompilerParams(
            dimension_semantics=("arbitrary",) * len(grid), vmem_limit_bytes=vmem * MIB
        ),
        cost_estimate=pl.CostEstimate(flops=flops, bytes_accessed=flops // 256, transcendentals=0),
        input_output_aliases=aliases or {},
        name=name,
    )(*prefetch, *inputs)


def add(*parts):
    total = parts[0].astype(F32)
    for part in parts[1:]:
        total = total + part.astype(F32)
    return total


def make_body(rows, seq):
    both = ("rows", "seq")
    further = [1 << i for i in range(3, rows.bit_length() - 1)]

    def swap_rows(array, bit):
        return lax.ppermute(array, "rows", [(i, i ^ bit) for i in range(rows)])

    def swap_seq(array, bit):
        return lax.ppermute(array, "seq", [(i, i ^ bit) for i in range(seq)])

    def swap_step(array, step):
        def partner(r, z):
            first, second = ((0, 2), (0, 4)), ((1, 1), (1, 2))
            if r & 1:
                first, second = first[::-1], second[::-1]
            axis, bit = (first + second)[step]
            return (r, z ^ bit) if axis else (r ^ bit, z)

        pairs = []
        for r in range(rows):
            for z in range(seq):
                to_r, to_z = partner(r, z)
                pairs.append((r * seq + z, to_r * seq + to_z))
        return lax.ppermute(array, both, pairs)

    def codes():
        r, z = lax.axis_index("rows"), lax.axis_index("seq")
        core = r & 1
        b1, b2, z0, z1 = (r >> 1) & 1, (r >> 2) & 1, z & 1, (z >> 1) & 1
        even = b1 * 8 + b2 * 4 + z0 * 2 + z1
        odd = b2 * 8 + b1 * 4 + z1 * 2 + z0
        label = jnp.where(core == 0, even, odd)
        other = jnp.where(core == 0, odd, even)
        return jnp.stack([core, label, other]).astype(jnp.int32)

    def after(array, *earlier):
        return lax.optimization_barrier((array, *earlier))[0]

    def two_parts(rider):
        high = rider.astype(BF16)
        return [high, (rider - high.astype(F32)).astype(BF16)]

    class Reduction:
        def __init__(self, wire, shape, halvings):
            self.rider = self.side = None
            self.slots, self.rows_each = shape[:2]
            self.halvings = halvings
            self.step = 0
            self.spreading = False
            self.parts = [None]
            self.arrived = swap_rows(wire, 1)

        def attach(self, rider):
            self.rider = rider
            self.side = swap_rows(jnp.concatenate(two_parts(rider), axis=0), 1)

        def send(self, outgoing):
            if self.rider is not None:
                flat = outgoing.reshape(-1, D)
                outgoing = jnp.concatenate([flat] + two_parts(self.rider), axis=0)
            self.slots = outgoing.shape[0] if self.rider is None else flat.shape[0] // self.rows_each
            self.arrived = swap_step(outgoing, self.step)
            self.step += 1

        def receive(self, earlier):
            array = after(self.arrived, *earlier)
            if self.rider is not None:
                size = self.slots * self.rows_each
                extra = (array[size:] if self.side is None else self.side).astype(F32)
                high, low = two_parts(self.rider)
                self.rider = (high.astype(F32) + low.astype(F32)) + (extra[:16] + extra[16:])
                if self.side is None:
                    array = array[:size].reshape(self.slots, self.rows_each, D)
                self.side = None
            return array

        def advance(self, *earlier):
            if self.spreading:
                held = jnp.concatenate([self.held, after(self.arrived, *earlier)])
            else:
                self.parts.append(self.receive(earlier))
                if self.step < self.halvings:
                    size = self.parts[0].shape[0] // 2
                    outgoing = add(*[part[size:] for part in self.parts]).astype(BF16)
                    self.parts = [part[:size] for part in self.parts]
                    self.send(outgoing)
                    return outgoing
                held = add(*self.parts)
                if self.step < 4:
                    held = held.astype(BF16)
                    size = 8 >> self.step
                    order = [slot ^ size for slot in range(held.shape[0])]
                    self.parts = [held]
                    self.send(jnp.concatenate([held[slot : slot + 1] for slot in order]))
                    return held
                for bit in further:
                    held = held + swap_rows(held, bit)
                    if self.rider is not None:
                        self.rider = self.rider + swap_rows(self.rider, bit)
                held = held.astype(BF16)
                self.spreading = True
                self.step = self.halvings
            self.held = held
            self.step -= 1
            if self.step >= 0:
                self.arrived = swap_step(held, self.step)
            else:
                self.arrived = swap_rows(held, 1)
            return held

    def body(
        block_input,
        cotangent,
        gain_attn,
        w_query,
        w_key,
        w_value,
        w_out,
        gain_mlp,
        w_inner,
        outer_weight,
        bias_table,
        lengths,
        observed,
    ):
        count, here = block_input.shape[0], block_input.shape[1]
        tokens = count * here
        last = count - 1
        place = lax.axis_index("seq").astype(jnp.int32).reshape(1)
        code = codes()
        gain_attn_row = gain_attn.reshape(1, D)
        gain_mlp_row = gain_mlp.reshape(1, D)

        def in_hbm(array):
            return pltpu.with_memory_space_constraint(array, pltpu.HBM)

        stacked = (PAIRS, 2 * here, PACKED_LENGTH)
        one = (here, D)
        own = (count, here, D)
        full = (PACKED_LENGTH, D)
        square = whole((D, D))
        line = whole((1, D))

        def pack(rows, tail, *pins):
            shapes = [(len(group) * here + (16 if tail and not i else 0), D) for i, group in enumerate(rows)]
            return call(
                functools.partial(pack_kernel, here=here, rows=rows, tail=tail),
                (1,),
                (),
                (in_hbm(block_input), in_hbm(after(observed, *pins))),
                [whole(own), whole(observed.shape)],
                [shaped(shape, BF16) for shape in shapes],
                [whole(shape) for shape in shapes],
                name="pack",
                vmem=8,
            )

        wire = pack([list(range(count))], True)[0]
        x2 = swap_seq(wire, 2)
        x1 = swap_seq(wire, 1)
        x2 = call(
            functools.partial(split_kernel, here=here),
            (1,),
            (),
            (x2,),
            [whole(wire.shape)],
            [shaped((here + 16, D), BF16)] + [shaped(one, BF16)] * (count - 1),
            [whole((here + 16, D))] + [whole(one)] * (count - 1),
            name="split",
            vmem=4,
        )
        *x2, bias_table = lax.optimization_barrier((*x2, bias_table))
        x3 = [swap_seq(x, 1) for x in x2]
        resident = (w_query, w_key, w_value, w_out)
        resident = call(
            functools.partial(prepare_kernel, here=here, seq=seq),
            (1,),
            (place,),
            (bias_table, *[in_hbm(array) for array in resident]),
            [whole(bias_table.shape)] + [ANYWHERE] * len(resident),
            [pltpu.VMEM(stacked, F32)]
            + [pltpu.VMEM(array.shape, array.dtype) for array in resident],
            [whole(stacked)] + [whole(array.shape) for array in resident],
            [pltpu.VMEM((H, SPAN), F32), pltpu.SemaphoreType.DMA((len(resident),))],
            name="prepare",
            vmem=4,
        )
        kept = []
        kept_shapes = [
            pltpu.VMEM(one, BF16),
            pltpu.VMEM(one, BF16),
            pltpu.VMEM(one, F32),
            pltpu.VMEM(one, F32),
            pltpu.VMEM(full, BF16),
            pltpu.VMEM(one, BF16),
            pltpu.VMEM(full, BF16),
            pltpu.VMEM(full, BF16),
            pltpu.VMEM(stacked, BF16),
        ]
        fetched_shapes = [pltpu.VMEM(shape, BF16) for shape in ((D, FF), (FF, D), own)]
        mlp_sources = [in_hbm(array) for array in (w_inner, outer_weight, cotangent)]
        for row in range(count):
            fetch = row == count - 1
            shapes = kept_shapes + (fetched_shapes if fetch else [])
            outs = call(
                functools.partial(attention_kernel, row=row, here=here, seq=seq, fetch=fetch),
                (1,),
                (place, lengths, code),
                [block_input, x1, x2[row], x3[row], observed, x1, x2[0], x3[0]]
                + [gain_attn_row, gain_mlp_row, *resident, *(mlp_sources if fetch else [])],
                [
                    one_row(own, row),
                    pl.BlockSpec(one, lambda *_, row=row: (row, 0)),
                    whole(one),
                    whole(one),
                    whole(observed.shape),
                    pl.BlockSpec((16, D), lambda *_: (tokens // 16, 0)),
                    pl.BlockSpec((16, D), lambda *_: (here // 16, 0)),
                    pl.BlockSpec((16, D), lambda *_: (here // 16, 0)),
                ]
                + [line] * 2
                + [whole(stacked)]
                + [square] * 4
                + [ANYWHERE] * (3 if fetch else 0),
                [pltpu.VMEM(array.shape, array.dtype) for array in resident] + shapes,
                [ANYWHERE] * len(resident) + [whole(shape.shape) for shape in shapes],
                [pltpu.SemaphoreType.DMA((3,))] if fetch else [],
                flops=8 * here * D * PACKED_LENGTH,
                name="attention",
                vmem=12,
                aliases={13 + i: i for i in range(len(resident))},
            )
            resident = outs[: len(resident)]
            kept.append(tuple(outs[len(resident) : len(resident) + len(kept_shapes)]))
            fetched = outs[len(resident) + len(kept_shapes) :]
        _, w_query, w_key, w_value, w_out = resident
        normed_mlp = [part[0] for part in kept]

        flat = (tokens, D)
        part_shape = (HALF, OUTER_ROWS, D)

        def mlp_part(own_half, nm):
            shapes = [pltpu.VMEM(flat, F32)] * 2 + [pltpu.VMEM(part_shape, BF16)] * 2
            return call(
                functools.partial(mlp_kernel, rows=count, own_half=own_half),
                (1,),
                (code,),
                [*nm, cotangent, *fetched],
                [whole(one)] * count + [whole(own), whole((D, FF)), whole((FF, D))],
                shapes,
                [whole(shape.shape) for shape in shapes],
                flops=6 * tokens * D * FF,
                name="mlp",
                vmem=16,
            )

        *fetched, cotangent = fetched
        total_a, back_a, outer_send, inner_send = mlp_part(False, normed_mlp)
        chains = {
            "outer": Reduction(outer_send, part_shape, 3),
            "inner": Reduction(inner_send, part_shape, 3),
        }
        nm = [after(normed_mlp[0], total_a)] + normed_mlp[1:]
        total_b, back_b, outer_keep, inner_keep = mlp_part(True, nm)
        chains["outer"].parts[0] = outer_keep
        chains["inner"].parts[0] = inner_keep

        small_half = (HALF, 4 * SMALL_ROWS, D)
        done = chains["outer"].advance()
        done = chains["inner"].advance(done)
        dx_half = (seq // 2, D, here)
        sum_shapes = [pltpu.VMEM((D, D), F32)] * 4
        sum_shapes += [pltpu.VMEM(stacked, F32), pltpu.VMEM((1, D), F32)]
        sums, block_output = (), ()
        grad_middles, dx_keeps, dx_sends = [], [], []
        for row in range(count):
            end = row == count - 1
            inputs = [*kept[row], cotangent, total_a, total_b, back_a, back_b, gain_mlp_row]
            inputs += [w_out, w_query, w_key, w_value, done, *sums]
            specs = [whole(shape.shape) for shape in kept_shapes] + [whole(own)]
            specs += [whole(flat)] * 4 + [line] + [square] * 4 + [ANYWHERE]
            specs += [whole(shape.shape) for shape in sum_shapes[: len(sums)]]
            if row:
                inputs.append(block_output)
                specs.append(ANYWHERE)
            aliases = {len(inputs) + 1: 0} if row else {}
            outs = [pltpu.HBM(own, BF16), pltpu.VMEM(one, F32)] + [pltpu.VMEM(dx_half, BF16)] * 2
            out_specs = [one_row(own, row), whole(one)] + [whole(dx_half)] * 2
            outs += sum_shapes
            out_specs += [whole(shape.shape) for shape in sum_shapes]
            if row:
                aliases |= {22 + i: 4 + i for i in range(len(sums))}
            if end:
                outs += [pltpu.VMEM(small_half, BF16)] * 2
                out_specs += [whole(small_half)] * 2
            block_output, grad_middle, dx_keep, dx_send, *sums = call(
                functools.partial(back_kernel, row=row, last=end, here=here, seq=seq),
                (1,),
                (place, code),
                inputs,
                specs,
                outs,
                out_specs,
                flops=20 * here * D * PACKED_LENGTH,
                name="attention_back",
                vmem=16,
                aliases=aliases,
            )
            done = grad_middle
            if row == BEFORE_ROW - 1:
                for event in EARLY:
                    done = chains[event].advance(done)
            grad_middles.append(grad_middle)
            dx_keeps.append(dx_keep)
            dx_sends.append(dx_send)
        *sums, small_keep, small_send = sums

        def make_rider(pin):
            _, gq, gk, gv, table_sum, gain_mlp_sum = sums
            return call(
                functools.partial(rider_kernel, here=here, seq=seq),
                (1,),
                (place,),
                (gq, gk, gv, table_sum, after(gain_mlp_sum, pin), gain_attn_row)
                + (w_query, w_key, w_value),
                [square] * 3 + [whole(stacked)] + [line] * 2 + [square] * 3,
                [pltpu.VMEM((16, D), F32)],
                [whole((16, D))],
                [pltpu.VMEM((8 * H, SPAN), F32)],
                name="rider",
                vmem=8,
            )[0]

        dx_arrived = [swap_step(dx_send, 2) for dx_send in dx_sends[:-1]]
        for event in ORDER:
            if event in chains:
                done = chains[event].advance(done)
            elif event == "small_start":
                chains["small"] = Reduction(after(small_send, done), small_half, SMALL_HALVINGS)
                chains["small"].parts[0] = small_keep
            elif event == "rider":
                done = make_rider(done)
                chains["small"].attach(done)
            elif event == "dx_first":
                *dx_arrived, done = lax.optimization_barrier((*dx_arrived, done))
                dx_half = [
                    [add(x[i], y[i]).astype(BF16) for x, y in zip(dx_keeps, dx_arrived)]
                    for i in range(2)
                ]
                *dx_half[0], done = lax.optimization_barrier((*dx_half[0], dx_half[1][-1]))
            elif event == "dx_start":
                dx_arrived = swap_step(after(dx_sends[-1], done), 2)
            elif event == "dx":
                dx_arrived = after(dx_arrived, done)
                half_kept, half_sent = [
                    jnp.stack(dx_half[i] + [add(dx_keeps[-1][i], dx_arrived[i]).astype(BF16)])
                    for i in range(2)
                ]
                dx_last = swap_step(half_sent, 3)
                done = half_sent
            elif event == "post":
                input_grad = call(
                    post_kernel,
                    (1,),
                    (),
                    (half_kept, after(dx_last, done), block_input, gain_attn_row, *grad_middles),
                    [whole(half_kept.shape)] * 2 + [whole(own), line] + [whole(one)] * count,
                    [shaped(own, BF16)],
                    [whole(own)],
                    name="post",
                )[0]
                done = input_grad
            elif event == "finish_outer":
                chain = chains["outer"]
                grad_outer = call(
                    functools.partial(finish_mlp_kernel, turned=False),
                    (FF // FF_TILE,),
                    (code,),
                    (chain.held, after(chain.arrived, done)),
                    [whole(part_shape)] * 2,
                    [shaped((FF, D), F32)],
                    [pl.BlockSpec((FF_TILE, D), lambda i, *_: (i, 0))],
                    [pltpu.VMEM((8, 128), F32)],
                    name="finish_outer",
                )[0]
                done = grad_outer
            elif event == "finish_inner":
                chain = chains["inner"]
                grad_inner = call(
                    functools.partial(finish_mlp_kernel, turned=True),
                    (FF // FF_TILE,),
                    (code,),
                    (chain.held, after(chain.arrived, done)),
                    [whole(part_shape)] * 2,
                    [shaped((D, FF), F32)],
                    [pl.BlockSpec((D, FF_TILE), lambda i, *_: (0, i))],
                    [pltpu.VMEM((FF_TILE, D), F32)],
                    name="finish_inner",
                )[0]
                done = grad_inner
        chain = chains["small"]
        grads = ()
        for own_half in (True, False):
            half = chain.held if own_half else after(chain.arrived, grads[0])

            def half_of(i, code):
                return (code[0] if own_half else 1 - code[0], 0)

            grads = call(
                functools.partial(finish_attention_kernel, own_half=own_half),
                (1,),
                (code,),
                (half, *grads),
                [whole(small_half)] + [ANYWHERE] * len(grads),
                [shaped((D, D), F32)] * 4,
                [pl.BlockSpec((D // 2, D), half_of)] * 4,
                name="finish_attention",
                aliases={2 + i: i for i in range(len(grads))},
            )
        grad_out, grad_query, grad_key, grad_value = grads
        rider = chain.rider

        return (
            block_output,
            input_grad,
            rider[8],
            grad_query,
            grad_key,
            grad_value,
            grad_out,
            rider[9],
            grad_inner,
            grad_outer,
            rider[:H, :BUCKETS].T,
        )

    return body


def solution(mesh):
    split = P("rows", "seq", None)
    placed = (split, split) + (P(),) * 9 + (P("rows", None), P("rows", "seq"))
    return jax.shard_map(
        make_body(mesh.shape["rows"], mesh.shape["seq"]),
        mesh=mesh,
        in_specs=placed,
        out_specs=(split, split) + (P(),) * 9,
        check_vma=False,
    )
```

```python
import functools
import math

import jax
import jax.numpy as jnp
from jax import lax
from jax.experimental import pallas as pl
from jax.experimental.pallas import tpu as pltpu
from jax.sharding import PartitionSpec as P

D = 512
FF = 2048
H = 8
HD = 64
PAIRS = H // 2
BUCKETS = 32
PACKED_LENGTH = 512
EPSILON = 1e-06
BUCKET_EDGES = (12, 16, 23, 32, 46, 64, 91)
SPAN = 2 * PACKED_LENGTH
CHUNKS = 32
HALF = CHUNKS // 2
OUTER_ROWS = FF // CHUNKS
SMALL_ROWS = D // CHUNKS
HALF_FF = FF // 2
MASKED = -1000000000.0
MIB = 1024 * 1024
F32 = jnp.float32
BF16 = jnp.bfloat16


SMALL_HALVINGS = 3
BEFORE_ROW = 2
EARLY = ("outer", "inner", )
ORDER = (
    "outer",
    "small_start",
    "rider",
    "inner",
    "outer",
    "small",
    "dx_first",
    "inner",
    "outer",
    "inner",
    "small",
    "small",
    "dx_start",
    "small",
    "outer",
    "inner",
    "outer",
    "small",
    "inner",
    "dx",
    "outer",
    "small",
    "small",
    "post",
    "inner",
    "own_outer",
    "other_outer",
    "own_inner",
    "other_inner",
    "small",
    "own_small",
    "other_small",
)


def dot(left, right, contract=(1, 0), precision=None):
    return lax.dot_general(
        left,
        right,
        (((contract[0],), (contract[1],)), ((), ())),
        preferred_element_type=F32,
        precision=precision,
    )


def dot_ones(values, ones, contract, swapped=False):
    high = values.astype(BF16)
    low = (values - high.astype(F32)).astype(BF16)
    if swapped:
        return dot(ones, high, contract) + dot(ones, low, contract)
    return dot(high, ones, contract) + dot(low, ones, contract)


def bucket_of(relative):
    distance = jnp.abs(relative)
    beyond = jnp.full(distance.shape, 8, jnp.int32)
    for edge_value in BUCKET_EDGES:
        beyond = beyond + (distance >= edge_value).astype(jnp.int32)
    near = jnp.where(distance < 8, distance, beyond)
    return jnp.where(relative > 0, 16, 0).astype(jnp.int32) + near


def bucket_rows(shape, bucket_axis):
    place_axis = 1 - bucket_axis
    relative = lax.broadcasted_iota(jnp.int32, shape, place_axis) - PACKED_LENGTH
    return (bucket_of(relative) == lax.broadcasted_iota(jnp.int32, shape, bucket_axis)).astype(F32)


def split_heads(pair):
    lane = lax.broadcasted_iota(jnp.int32, pair.shape, 1)
    zero = jnp.zeros_like(pair)
    return jnp.concatenate(
        [jnp.where(lane < HD, pair, zero), jnp.where(lane >= HD, pair, zero)], axis=0
    )


def join_heads(stacked):
    half = stacked.shape[0] // 2
    lane = lax.broadcasted_iota(jnp.int32, (half, stacked.shape[1]), 1)
    return jnp.where(lane < HD, stacked[:half], stacked[half:])


def pack_kernel(x_ref, seen_ref, *out_refs, here, rows, tail):
    count = x_ref.shape[0]
    for out_ref, group in zip(out_refs, rows):
        for place, row in enumerate(group):
            out_ref[place * here : (place + 1) * here] = x_ref[row]
    if tail:
        flags = seen_ref[...].astype(F32)
        flags = jnp.concatenate([flags, jnp.zeros((16 - count, here), F32)], axis=0)
        flags = jnp.concatenate([flags, jnp.zeros((16, D - here), F32)], axis=1)
        out_refs[0][len(rows[0]) * here :] = flags.astype(BF16)


def split_kernel(wire_ref, *out_refs, here):
    for row, out_ref in enumerate(out_refs):
        out_ref[:here] = wire_ref[row * here : (row + 1) * here]
    out_refs[0][here:] = wire_ref[len(out_refs) * here :]


def prepare_kernel(place_ref, table_ref, *refs, here, seq):
    count = (len(refs) - 3) // 2
    sources, bias_ref, targets = refs[:count], refs[count], refs[count + 1 : 2 * count + 1]
    line_ref, sems = refs[2 * count + 1 :]
    copies = [
        pltpu.make_async_copy(source, target, sems.at[i])
        for i, (source, target) in enumerate(zip(sources, targets))
    ]
    for copy in copies:
        copy.start()
    line_ref[...] = dot(
        table_ref[...], bucket_rows((BUCKETS, SPAN), 0), (0, 0), lax.Precision.HIGHEST
    )
    me = place_ref[0]
    for block in range(seq):
        offset = ((me ^ block) - me) * here + PACKED_LENGTH - here
        window = line_ref[:, pl.ds(pl.multiple_of(offset, 128), 2 * here)]
        for head in range(H):
            spread = jnp.broadcast_to(window[head : head + 1], (here, 2 * here))
            skewed = pltpu.roll(spread, here, 1, stride=1, stride_axis=0)
            row = (head % 2) * here
            bias_ref[head // 2, row : row + here, block * here : (block + 1) * here] = skewed[
                :, :here
            ]
    for copy in copies:
        copy.wait()


def attention_kernel(
    place_ref,
    lengths_ref,
    code_ref,
    x0_ref,
    x1_ref,
    x2_ref,
    x3_ref,
    seen_ref,
    x1_tail_ref,
    x2_tail_ref,
    x3_tail_ref,
    gain_ref,
    gain_mlp_ref,
    bias_ref,
    wq_ref,
    wk_ref,
    wv_ref,
    w_out_ref,
    *refs,
    row,
    here,
    seq,
    fetch,
):
    if fetch:
        copies = [
            pltpu.make_async_copy(refs[i], refs[i - 4], refs[-1].at[i]) for i in range(3)
        ]
        for copy in copies:
            copy.start()
        refs = refs[:-4]
    (
        normed_mlp_ref,
        attended_ref,
        middle_ref,
        mixed_ref,
        normed_ref,
        q_ref,
        k_ref,
        v_ref,
        p_ref,
    ) = refs[-9:]
    me = place_ref[0]
    own_x = x0_ref[0].astype(F32)
    x = jnp.concatenate(
        [own_x] + [ref.astype(F32) for ref in (x1_ref[...], x2_ref[...], x3_ref[...])], axis=0
    )
    inv = lax.rsqrt(jnp.mean(x * x, -1, keepdims=True) + EPSILON)
    normed = (x * inv * gain_ref[...]).astype(BF16)
    normed_ref[...] = normed
    q = dot(normed[:here], wq_ref[...]).astype(BF16)
    k = dot(normed, wk_ref[...]).astype(BF16)
    v = dot(normed, wv_ref[...]).astype(BF16)
    q_ref[...] = q
    k_ref[...] = k
    v_ref[...] = v
    ends = [lengths_ref[row, 0]]
    for part in range(1, lengths_ref.shape[1]):
        ends.append(ends[-1] + lengths_ref[row, part])

    def segment(place):
        total = jnp.zeros(place.shape, jnp.int32)
        for end in ends:
            total = total + (end <= place).astype(jnp.int32)
        return total

    query_place = me * here + lax.broadcasted_iota(jnp.int32, (here, 1), 0)
    lane = lax.broadcasted_iota(jnp.int32, (1, here), 1)
    key_place = jnp.concatenate([(me ^ block) * here + lane for block in range(seq)], axis=1)
    seen = jnp.concatenate(
        [seen_ref[row : row + 1].astype(F32)]
        + [
            ref[...].astype(F32)[row : row + 1, :here]
            for ref in (x1_tail_ref, x2_tail_ref, x3_tail_ref)
        ],
        axis=1,
    )
    key_segment = jnp.where(seen == 1.0, segment(key_place), -1)
    allowed = (segment(query_place) == key_segment) | (query_place == key_place)
    allowed = jnp.concatenate([allowed.astype(jnp.int32)] * 2, axis=0) == 1
    attended = []
    for pair in range(PAIRS):
        lanes = slice(pair * 2 * HD, (pair + 1) * 2 * HD)
        scores = dot(split_heads(q[:, lanes]), k[:, lanes], (1, 1)) + bias_ref[pair]
        scores = jnp.where(allowed, scores, MASKED)
        exponent = jnp.exp(scores - jnp.max(scores, -1, keepdims=True))
        ones = jnp.ones((PACKED_LENGTH, 128), BF16)
        both = dot(exponent.astype(BF16), jnp.concatenate([v[:, lanes], ones], axis=1))
        share = 1.0 / both[:, 128:]
        mixed = join_heads(both[:, :128] * share)
        for first in range(0, PACKED_LENGTH, 128):
            part = slice(first, first + 128)
            p_ref[pair, :, part] = (exponent[:, part] * share).astype(BF16)
        mixed_ref[:, lanes] = mixed
        attended.append(mixed.astype(BF16))
    attended = jnp.concatenate(attended, axis=1)
    attended_ref[...] = attended
    middle = own_x + dot(attended, w_out_ref[...])
    middle_ref[...] = middle
    inv = lax.rsqrt(jnp.mean(middle * middle, -1, keepdims=True) + EPSILON)
    normed_mlp_ref[...] = (middle * inv * gain_mlp_ref[...]).astype(BF16)
    if fetch:
        for copy in copies:
            copy.wait()


def gelu_both(u):
    scale = 0.7978845608028654
    square = u * u
    t = jnp.tanh(u * (scale + (scale * 0.044715) * square))
    half_up = 0.5 + 0.5 * t
    slope = half_up + (0.5 * u) * (1.0 - t * t) * (scale + (3.0 * 0.044715 * scale) * square)
    return u * half_up, slope


def mlp_kernel(code_ref, *refs, rows, own_half):
    nm_refs = refs[:rows]
    g_ref, w_inner_ref, w_outer_ref = refs[rows : rows + 3]
    refs = refs[rows + 3 :]
    total_ref, back_ref, outer_ref, inner_ref = refs
    label = code_ref[1] if own_half else code_ref[2]
    normed = jnp.concatenate([ref[...] for ref in nm_refs], axis=0)
    g = g_ref[...].reshape(normed.shape)
    half = code_ref[0] if own_half else 1 - code_ref[0]
    hidden = pl.ds(pl.multiple_of(half * HALF_FF, HALF_FF), HALF_FF)
    w_inner = w_inner_ref[:, hidden]
    w_outer = w_outer_ref[hidden, :]
    active_f, slope = gelu_both(dot(normed, w_inner))
    active = active_f.astype(BF16)
    grad_act = (dot(g, w_outer, (1, 1)) * slope).astype(BF16)
    total_ref[...] = dot(active, w_outer)
    back_ref[...] = dot(grad_act, w_inner, (1, 1))
    outer = dot(active, g, (0, 0)).astype(BF16)
    inner = dot(grad_act, normed, (0, 0)).astype(BF16)
    for part in range(HALF):
        slot = part ^ label
        rows = slice(part * OUTER_ROWS, (part + 1) * OUTER_ROWS)
        outer_ref[slot] = outer[rows]
        inner_ref[slot] = inner[rows]


def back_kernel(place_ref, code_ref, *refs, row, last, here, seq):
    _, attended_ref, middle_ref, mixed_ref, normed_ref, q_ref, k_ref, v_ref, p_ref = refs[:9]
    (
        g_ref,
        total_a_ref,
        total_b_ref,
        back_a_ref,
        back_b_ref,
        gain_mlp_ref,
        w_out_ref,
        wq_ref,
        wk_ref,
        wv_ref,
        _,
    ) = refs[9:20]
    refs = refs[20:]
    old = refs[:6] if row else None
    refs = refs[6:] if row else refs
    if row:
        refs = refs[1:]
    block_output_ref, grad_middle_ref, dx_keep_ref, dx_send_ref = refs[:4]
    sums = refs[4:10]
    if last:
        keep_ref, send_ref = refs[10:12]

    def accumulate(which, value, part=None):
        if part is None:
            sums[which][...] = value + old[which][...] if row else value
        else:
            sums[which][part] = value + old[which][part] if row else value

    index = row
    tokens = slice(index * here, (index + 1) * here)
    middle = middle_ref[...]
    back = back_a_ref[tokens] + back_b_ref[tokens]
    block_output_ref[0] = (middle + total_a_ref[tokens] + total_b_ref[tokens]).astype(BF16)
    inv = lax.rsqrt(jnp.mean(middle * middle, -1, keepdims=True) + EPSILON)
    accumulate(5, jnp.sum(back * middle * inv, axis=0, keepdims=True))
    scaled = back * gain_mlp_ref[...]
    grad_middle = (
        g_ref[row].astype(F32)
        + inv * scaled
        - middle * (inv * inv * inv) * jnp.mean(scaled * middle, -1, keepdims=True)
    )
    grad_middle_ref[...] = grad_middle
    branch = grad_middle.astype(BF16)
    ga = dot(branch, w_out_ref[...], (1, 1)).astype(BF16)

    accumulate(0, dot(attended_ref[...], branch, (0, 0)))
    q = q_ref[...]
    k = k_ref[...]
    v = v_ref[...]
    normed = normed_ref[...]
    dq, dkt, dvt = [], [], []
    for pair in range(PAIRS):
        lanes = slice(pair * 2 * HD, (pair + 1) * 2 * HD)
        ga_split = split_heads(ga[:, lanes])
        q_split = split_heads(q[:, lanes])
        mixed = mixed_ref[:, lanes]
        probs = p_ref[pair]
        delta = jnp.sum(
            ga_split.astype(F32) * jnp.concatenate([mixed, mixed], axis=0), -1, keepdims=True
        )
        grad_probs = dot(ga_split, v[:, lanes], (1, 1))
        grad_scores_f = probs.astype(F32) * (grad_probs - delta)
        accumulate(4, grad_scores_f, pair)
        grad_scores = grad_scores_f.astype(BF16)
        dq.append(join_heads(dot(grad_scores, k[:, lanes])).astype(BF16))
        dkt.append(dot(q_split, grad_scores, (0, 0)).astype(BF16))
        dvt.append(dot(ga_split, probs, (0, 0)).astype(BF16))
    dq = jnp.concatenate(dq, axis=1)
    dkt = jnp.concatenate(dkt, axis=0)
    dvt = jnp.concatenate(dvt, axis=0)
    chunks = [slice(first, first + 128) for first in range(0, D, 128)]
    pieces = [[] for _ in range(seq)]
    for rows in chunks:
        dxt = dot(wk_ref[rows], dkt) + dot(wv_ref[rows], dvt)
        own = dxt[:, :here] + dot(wq_ref[rows], dq, (1, 1))
        pieces[0].append(own.astype(BF16))
        for block in range(1, seq):
            pieces[block].append(dxt[:, block * here : (block + 1) * here].astype(BF16))
    pieces = [jnp.concatenate(piece, axis=0) for piece in pieces]
    dx_keep_ref[0] = pieces[0]
    dx_send_ref[1] = pieces[3]

    @pl.when(code_ref[0] == 0)
    def _():
        dx_keep_ref[1] = pieces[2]
        dx_send_ref[0] = pieces[1]

    @pl.when(code_ref[0] == 1)
    def _():
        dx_keep_ref[1] = pieces[1]
        dx_send_ref[0] = pieces[2]

    accumulate(1, dot(normed[:here], dq, (0, 0)))
    for rows in chunks:
        accumulate(2, dot(dkt[rows], normed), rows)
        accumulate(3, dot(dvt[rows], normed), rows)

    if not last:
        return
    go_ref, gq_ref, gk_ref, gv_ref = sums[:4]
    gk_ref[...] = gk_ref[...].T
    gv_ref[...] = gv_ref[...].T
    core, label, other = code_ref[0], code_ref[1], code_ref[2]
    for index, grad_ref in enumerate((go_ref, gq_ref, gk_ref, gv_ref)):
        for slot in range(HALF):
            chunk = core * HALF + (slot ^ label)
            first = pl.multiple_of(chunk * SMALL_ROWS, SMALL_ROWS)
            rows_to = slice(index * SMALL_ROWS, (index + 1) * SMALL_ROWS)
            keep_ref[slot, rows_to] = grad_ref[pl.ds(first, SMALL_ROWS), :].astype(BF16)
            chunk = (1 - core) * HALF + (slot ^ other)
            first = pl.multiple_of(chunk * SMALL_ROWS, SMALL_ROWS)
            send_ref[slot, rows_to] = grad_ref[pl.ds(first, SMALL_ROWS), :].astype(BF16)


def rider_kernel(
    place_ref,
    gq_ref,
    gk_ref,
    gv_ref,
    table_sum_ref,
    gain_mlp_ref,
    gain_attn_ref,
    wq_ref,
    wk_ref,
    wv_ref,
    rider_ref,
    line_ref,
    *,
    here,
    seq,
):
    me = place_ref[0]
    line_ref[...] = jnp.zeros_like(line_ref)
    for block in range(seq):
        offset = ((me ^ block) - me) * here + PACKED_LENGTH - here
        window = pl.ds(pl.multiple_of(offset, 128), 2 * here)
        for head in range(H):
            row = (head % 2) * here
            tile = table_sum_ref[head // 2, row : row + here, block * here : (block + 1) * here]
            total = jnp.zeros((8, 2 * here), F32)
            empty = jnp.zeros((8, here), F32)
            for group in range(here // 8):
                wide = jnp.concatenate([tile[group * 8 : group * 8 + 8], empty], axis=1)
                total = total + pltpu.roll(wide, here - 8 * group, 1)
            line_ref[head * 8 : head * 8 + 8, window] += total
    lines = line_ref[...]
    sub = lax.broadcasted_iota(jnp.int32, lines.shape, 0)
    for bit in (1, 2, 4):
        lines = jnp.where((sub & bit) != 0, pltpu.roll(lines, SPAN - bit, 1), lines)
    by_head = jnp.concatenate(
        [jnp.sum(lines[h * 8 : h * 8 + 8], axis=0, keepdims=True) for h in range(H)], axis=0
    )
    table = dot_ones(by_head, bucket_rows((SPAN, 128), 1).astype(BF16), (1, 0))
    gain = (
        wq_ref[...].astype(F32) * gq_ref[...]
        + wk_ref[...].astype(F32) * gk_ref[...]
        + wv_ref[...].astype(F32) * gv_ref[...]
    )
    gain_grad = dot_ones(gain, jnp.ones((8, D), BF16), (1, 1), True)
    rider = jnp.concatenate(
        [
            jnp.concatenate([table, jnp.zeros((8, D - 128), F32)], axis=1),
            gain_grad[:1] / gain_attn_ref[...],
            gain_mlp_ref[...],
            jnp.zeros((6, D), F32),
        ],
        axis=0,
    )
    rider_ref[...] = rider


def finish_mlp_kernel(code_ref, half_ref, *refs, own_half, turned):
    out_ref, stage_ref, sems = refs[-3:]
    half = code_ref[0] if own_half else 1 - code_ref[0]
    label = code_ref[1] if own_half else code_ref[2]
    groups = stage_ref.shape[0]
    per_group = HALF // groups
    size = per_group * OUTER_ROWS
    copies = []
    for group in range(groups):
        pieces = [half_ref[(group * per_group + i) ^ label].astype(F32) for i in range(per_group)]
        piece = jnp.concatenate(pieces, axis=0)
        stage_ref[group] = piece.T if turned else piece
        place = pl.ds(pl.multiple_of((half * groups + group) * size, size), size)
        target = out_ref.at[:, place] if turned else out_ref.at[place]
        copies.append(pltpu.make_async_copy(stage_ref.at[group], target, sems.at[group]))
        copies[-1].start()
    for copy in copies:
        copy.wait()


def finish_attention_kernel(code_ref, half_ref, *refs, own_half):
    out_refs, stage_ref, sems = refs[-6:-2], refs[-2], refs[-1]
    half = code_ref[0] if own_half else 1 - code_ref[0]
    label = code_ref[1] if own_half else code_ref[2]
    place = pl.ds(pl.multiple_of(half * (D // 2), D // 2), D // 2)
    copies = []
    for index, out_ref in enumerate(out_refs):
        part = slice(index * SMALL_ROWS, (index + 1) * SMALL_ROWS)
        for slot in range(HALF):
            rows = slice(slot * SMALL_ROWS, (slot + 1) * SMALL_ROWS)
            stage_ref[index, rows] = half_ref[slot ^ label, part].astype(F32)
        copies.append(
            pltpu.make_async_copy(stage_ref.at[index], out_ref.at[place], sems.at[index])
        )
        copies[-1].start()
    for copy in copies:
        copy.wait()


def post_kernel(a_ref, b_ref, x_ref, gain_ref, *refs):
    grad_middle_refs, out_ref = refs[:-1], refs[-1]
    for row, grad_middle_ref in enumerate(grad_middle_refs):
        back = (a_ref[row].astype(F32) + b_ref[row].astype(F32)).T
        x = x_ref[row].astype(F32)
        inv = lax.rsqrt(jnp.mean(x * x, -1, keepdims=True) + EPSILON)
        scaled = back * gain_ref[...]
        grad = inv * scaled - x * (inv * inv * inv) * jnp.mean(scaled * x, -1, keepdims=True)
        out_ref[row] = (grad_middle_ref[...] + grad).astype(BF16)


ANYWHERE = pl.BlockSpec(memory_space=pl.ANY)


def whole(shape):
    return pl.BlockSpec(shape, lambda *_: (0,) * len(shape))


def by_row(shape):
    return pl.BlockSpec((1,) + shape[1:], lambda i, *_: (i,) + (0,) * (len(shape) - 1))


def one_row(shape, row):
    return pl.BlockSpec((1,) + shape[1:], lambda *_: (row,) + (0,) * (len(shape) - 1))


def shaped(shape, dtype):
    return jax.ShapeDtypeStruct(shape, dtype)


def call(
    kernel,
    grid,
    prefetch,
    inputs,
    in_specs,
    outs,
    out_specs,
    scratch=(),
    flops=0,
    name=None,
    aliases=None,
    vmem=16,
):
    return pl.pallas_call(
        kernel,
        out_shape=outs,
        grid_spec=pltpu.PrefetchScalarGridSpec(
            num_scalar_prefetch=len(prefetch),
            grid=grid,
            in_specs=in_specs,
            out_specs=out_specs,
            scratch_shapes=list(scratch),
        ),
        compiler_params=pltpu.CompilerParams(
            dimension_semantics=("arbitrary",) * len(grid), vmem_limit_bytes=vmem * MIB
        ),
        cost_estimate=pl.CostEstimate(flops=flops, bytes_accessed=flops // 256, transcendentals=0),
        input_output_aliases=aliases or {},
        name=name,
    )(*prefetch, *inputs)


def add(*parts):
    total = parts[0].astype(F32)
    for part in parts[1:]:
        total = total + part.astype(F32)
    return total


def make_body(rows, seq):
    both = ("rows", "seq")
    further = [1 << i for i in range(3, rows.bit_length() - 1)]

    def swap_rows(array, bit):
        return lax.ppermute(array, "rows", [(i, i ^ bit) for i in range(rows)])

    def swap_seq(array, bit):
        return lax.ppermute(array, "seq", [(i, i ^ bit) for i in range(seq)])

    def swap_step(array, step):
        def partner(r, z):
            first, second = ((0, 2), (0, 4)), ((1, 1), (1, 2))
            if r & 1:
                first, second = first[::-1], second[::-1]
            axis, bit = (first + second)[step]
            return (r, z ^ bit) if axis else (r ^ bit, z)

        pairs = []
        for r in range(rows):
            for z in range(seq):
                to_r, to_z = partner(r, z)
                pairs.append((r * seq + z, to_r * seq + to_z))
        return lax.ppermute(array, both, pairs)

    def codes():
        r, z = lax.axis_index("rows"), lax.axis_index("seq")
        core = r & 1
        b1, b2, z0, z1 = (r >> 1) & 1, (r >> 2) & 1, z & 1, (z >> 1) & 1
        even = b1 * 8 + b2 * 4 + z0 * 2 + z1
        odd = b2 * 8 + b1 * 4 + z1 * 2 + z0
        label = jnp.where(core == 0, even, odd)
        other = jnp.where(core == 0, odd, even)
        return jnp.stack([core, label, other]).astype(jnp.int32)

    def after(array, *earlier):
        return lax.optimization_barrier((array, *earlier))[0]

    def two_parts(rider):
        high = rider.astype(BF16)
        return [high, (rider - high.astype(F32)).astype(BF16)]

    class Reduction:
        def __init__(self, wire, shape, halvings):
            self.rider = self.side = None
            self.slots, self.rows_each = shape[:2]
            self.halvings = halvings
            self.step = 0
            self.spreading = False
            self.parts = [None]
            self.arrived = swap_rows(wire, 1)

        def attach(self, rider):
            self.rider = rider
            self.side = swap_rows(jnp.concatenate(two_parts(rider), axis=0), 1)

        def send(self, outgoing):
            if self.rider is not None:
                flat = outgoing.reshape(-1, D)
                outgoing = jnp.concatenate([flat] + two_parts(self.rider), axis=0)
            self.slots = outgoing.shape[0] if self.rider is None else flat.shape[0] // self.rows_each
            self.arrived = swap_step(outgoing, self.step)
            self.step += 1

        def receive(self, earlier):
            array = after(self.arrived, *earlier)
            if self.rider is not None:
                size = self.slots * self.rows_each
                extra = (array[size:] if self.side is None else self.side).astype(F32)
                high, low = two_parts(self.rider)
                self.rider = (high.astype(F32) + low.astype(F32)) + (extra[:16] + extra[16:])
                if self.side is None:
                    array = array[:size].reshape(self.slots, self.rows_each, D)
                self.side = None
            return array

        def advance(self, *earlier):
            if self.spreading:
                held = jnp.concatenate([self.held, after(self.arrived, *earlier)])
            else:
                self.parts.append(self.receive(earlier))
                if self.step < self.halvings:
                    size = self.parts[0].shape[0] // 2
                    outgoing = add(*[part[size:] for part in self.parts]).astype(BF16)
                    self.parts = [part[:size] for part in self.parts]
                    self.send(outgoing)
                    return outgoing
                held = add(*self.parts)
                if self.step < 4:
                    held = held.astype(BF16)
                    size = 8 >> self.step
                    order = [slot ^ size for slot in range(held.shape[0])]
                    self.parts = [held]
                    self.send(jnp.concatenate([held[slot : slot + 1] for slot in order]))
                    return held
                for bit in further:
                    held = held + swap_rows(held, bit)
                    if self.rider is not None:
                        self.rider = self.rider + swap_rows(self.rider, bit)
                held = held.astype(BF16)
                self.spreading = True
                self.step = self.halvings
            self.held = held
            self.step -= 1
            if self.step >= 0:
                self.arrived = swap_step(held, self.step)
            else:
                self.arrived = swap_rows(held, 1)
            return held

    def body(
        block_input,
        cotangent,
        gain_attn,
        w_query,
        w_key,
        w_value,
        w_out,
        gain_mlp,
        w_inner,
        outer_weight,
        bias_table,
        lengths,
        observed,
    ):
        count, here = block_input.shape[0], block_input.shape[1]
        tokens = count * here
        last = count - 1
        place = lax.axis_index("seq").astype(jnp.int32).reshape(1)
        code = codes()
        gain_attn_row = gain_attn.reshape(1, D)
        gain_mlp_row = gain_mlp.reshape(1, D)

        def in_hbm(array):
            return pltpu.with_memory_space_constraint(array, pltpu.HBM)

        stacked = (PAIRS, 2 * here, PACKED_LENGTH)
        one = (here, D)
        own = (count, here, D)
        full = (PACKED_LENGTH, D)
        square = whole((D, D))
        line = whole((1, D))

        def pack(rows, tail, *pins):
            shapes = [(len(group) * here + (16 if tail and not i else 0), D) for i, group in enumerate(rows)]
            return call(
                functools.partial(pack_kernel, here=here, rows=rows, tail=tail),
                (1,),
                (),
                (in_hbm(block_input), in_hbm(after(observed, *pins))),
                [whole(own), whole(observed.shape)],
                [shaped(shape, BF16) for shape in shapes],
                [whole(shape) for shape in shapes],
                name="pack",
                vmem=8,
            )

        wire = pack([list(range(count))], True)[0]
        x2 = swap_seq(wire, 2)
        x1 = swap_seq(wire, 1)
        x2 = call(
            functools.partial(split_kernel, here=here),
            (1,),
            (),
            (x2,),
            [whole(wire.shape)],
            [shaped((here + 16, D), BF16)] + [shaped(one, BF16)] * (count - 1),
            [whole((here + 16, D))] + [whole(one)] * (count - 1),
            name="split",
            vmem=4,
        )
        *x2, bias_table = lax.optimization_barrier((*x2, bias_table))
        x3 = [swap_seq(x, 1) for x in x2]
        resident = (w_query, w_key, w_value, w_out)
        resident = call(
            functools.partial(prepare_kernel, here=here, seq=seq),
            (1,),
            (place,),
            (bias_table, *[in_hbm(array) for array in resident]),
            [whole(bias_table.shape)] + [ANYWHERE] * len(resident),
            [pltpu.VMEM(stacked, F32)]
            + [pltpu.VMEM(array.shape, array.dtype) for array in resident],
            [whole(stacked)] + [whole(array.shape) for array in resident],
            [pltpu.VMEM((H, SPAN), F32), pltpu.SemaphoreType.DMA((len(resident),))],
            name="prepare",
            vmem=4,
        )
        kept = []
        kept_shapes = [
            pltpu.VMEM(one, BF16),
            pltpu.VMEM(one, BF16),
            pltpu.VMEM(one, F32),
            pltpu.VMEM(one, F32),
            pltpu.VMEM(full, BF16),
            pltpu.VMEM(one, BF16),
            pltpu.VMEM(full, BF16),
            pltpu.VMEM(full, BF16),
            pltpu.VMEM(stacked, BF16),
        ]
        fetched_shapes = [pltpu.VMEM(shape, BF16) for shape in ((D, FF), (FF, D), own)]
        mlp_sources = [in_hbm(array) for array in (w_inner, outer_weight, cotangent)]
        for row in range(count):
            fetch = row == count - 1
            shapes = kept_shapes + (fetched_shapes if fetch else [])
            outs = call(
                functools.partial(attention_kernel, row=row, here=here, seq=seq, fetch=fetch),
                (1,),
                (place, lengths, code),
                [block_input, x1, x2[row], x3[row], observed, x1, x2[0], x3[0]]
                + [gain_attn_row, gain_mlp_row, *resident, *(mlp_sources if fetch else [])],
                [
                    one_row(own, row),
                    pl.BlockSpec(one, lambda *_, row=row: (row, 0)),
                    whole(one),
                    whole(one),
                    whole(observed.shape),
                    pl.BlockSpec((16, D), lambda *_: (tokens // 16, 0)),
                    pl.BlockSpec((16, D), lambda *_: (here // 16, 0)),
                    pl.BlockSpec((16, D), lambda *_: (here // 16, 0)),
                ]
                + [line] * 2
                + [whole(stacked)]
                + [square] * 4
                + [ANYWHERE] * (3 if fetch else 0),
                [pltpu.VMEM(array.shape, array.dtype) for array in resident] + shapes,
                [ANYWHERE] * len(resident) + [whole(shape.shape) for shape in shapes],
                [pltpu.SemaphoreType.DMA((3,))] if fetch else [],
                flops=8 * here * D * PACKED_LENGTH,
                name="attention",
                vmem=12,
                aliases={13 + i: i for i in range(len(resident))},
            )
            resident = outs[: len(resident)]
            kept.append(tuple(outs[len(resident) : len(resident) + len(kept_shapes)]))
            fetched = outs[len(resident) + len(kept_shapes) :]
        _, w_query, w_key, w_value, w_out = resident
        normed_mlp = [part[0] for part in kept]

        flat = (tokens, D)
        part_shape = (HALF, OUTER_ROWS, D)

        def mlp_part(own_half, nm):
            shapes = [pltpu.VMEM(flat, F32)] * 2 + [pltpu.VMEM(part_shape, BF16)] * 2
            return call(
                functools.partial(mlp_kernel, rows=count, own_half=own_half),
                (1,),
                (code,),
                [*nm, cotangent, *fetched],
                [whole(one)] * count + [whole(own), whole((D, FF)), whole((FF, D))],
                shapes,
                [whole(shape.shape) for shape in shapes],
                flops=6 * tokens * D * FF,
                name="mlp",
                vmem=16,
            )

        *fetched, cotangent = fetched
        total_a, back_a, outer_send, inner_send = mlp_part(False, normed_mlp)
        chains = {
            "outer": Reduction(outer_send, part_shape, 3),
            "inner": Reduction(inner_send, part_shape, 3),
        }
        nm = [after(normed_mlp[0], total_a)] + normed_mlp[1:]
        total_b, back_b, outer_keep, inner_keep = mlp_part(True, nm)
        chains["outer"].parts[0] = outer_keep
        chains["inner"].parts[0] = inner_keep

        small_half = (HALF, 4 * SMALL_ROWS, D)
        done = chains["outer"].advance()
        done = chains["inner"].advance(done)
        dx_half = (seq // 2, D, here)
        sum_shapes = [pltpu.VMEM((D, D), F32)] * 4
        sum_shapes += [pltpu.VMEM(stacked, F32), pltpu.VMEM((1, D), F32)]
        sums, block_output = (), ()
        grad_middles, dx_keeps, dx_sends = [], [], []
        for row in range(count):
            end = row == count - 1
            inputs = [*kept[row], cotangent, total_a, total_b, back_a, back_b, gain_mlp_row]
            inputs += [w_out, w_query, w_key, w_value, done, *sums]
            specs = [whole(shape.shape) for shape in kept_shapes] + [whole(own)]
            specs += [whole(flat)] * 4 + [line] + [square] * 4 + [ANYWHERE]
            specs += [whole(shape.shape) for shape in sum_shapes[: len(sums)]]
            if row:
                inputs.append(block_output)
                specs.append(ANYWHERE)
            aliases = {len(inputs) + 1: 0} if row else {}
            outs = [pltpu.HBM(own, BF16), pltpu.VMEM(one, F32)] + [pltpu.VMEM(dx_half, BF16)] * 2
            out_specs = [one_row(own, row), whole(one)] + [whole(dx_half)] * 2
            outs += sum_shapes
            out_specs += [whole(shape.shape) for shape in sum_shapes]
            if row:
                aliases |= {22 + i: 4 + i for i in range(len(sums))}
            if end:
                outs += [pltpu.VMEM(small_half, BF16)] * 2
                out_specs += [whole(small_half)] * 2
            block_output, grad_middle, dx_keep, dx_send, *sums = call(
                functools.partial(back_kernel, row=row, last=end, here=here, seq=seq),
                (1,),
                (place, code),
                inputs,
                specs,
                outs,
                out_specs,
                flops=20 * here * D * PACKED_LENGTH,
                name="attention_back",
                vmem=16,
                aliases=aliases,
            )
            done = grad_middle
            if row == BEFORE_ROW - 1:
                for event in EARLY:
                    done = chains[event].advance(done)
            grad_middles.append(grad_middle)
            dx_keeps.append(dx_keep)
            dx_sends.append(dx_send)
        *sums, small_keep, small_send = sums

        def make_rider(pin):
            _, gq, gk, gv, table_sum, gain_mlp_sum = sums
            return call(
                functools.partial(rider_kernel, here=here, seq=seq),
                (1,),
                (place,),
                (gq, gk, gv, table_sum, after(gain_mlp_sum, pin), gain_attn_row)
                + (w_query, w_key, w_value),
                [square] * 3 + [whole(stacked)] + [line] * 2 + [square] * 3,
                [pltpu.VMEM((16, D), F32)],
                [whole((16, D))],
                [pltpu.VMEM((8 * H, SPAN), F32)],
                name="rider",
                vmem=8,
            )[0]

        dx_arrived = [swap_step(dx_send, 2) for dx_send in dx_sends[:-1]]

        grads = {}

        def finish(name, own_half, pin):
            chain = chains[name]
            groups = 4
            if name == "small":
                kernel = finish_attention_kernel
                shapes, stage = [(D, D)] * 4, (4, D // 2, D)
            else:
                turned = name == "inner"
                kernel = functools.partial(finish_mlp_kernel, turned=turned)
                size = HALF_FF // groups
                shapes = [(D, FF) if turned else (FF, D)]
                stage = (groups, D, size) if turned else (groups, size, D)
            half = after(chain.held if own_half else chain.arrived, pin)
            before = grads.get(name, ())
            grads[name] = call(
                functools.partial(kernel, own_half=own_half),
                (1,),
                (code,),
                (half, *before),
                [whole(half.shape)] + [ANYWHERE] * len(before),
                [pltpu.HBM(shape, F32) for shape in shapes],
                [ANYWHERE] * len(shapes),
                [pltpu.VMEM(stage, F32), pltpu.SemaphoreType.DMA((stage[0],))],
                name="finish_" + name,
                vmem=10,
                aliases={2 + i: i for i in range(len(before))},
            )
            return grads[name][0]

        for event in ORDER:
            if event in chains:
                done = chains[event].advance(done)
            elif event == "small_start":
                chains["small"] = Reduction(after(small_send, done), small_half, SMALL_HALVINGS)
                chains["small"].parts[0] = small_keep
            elif event == "rider":
                done = make_rider(done)
                chains["small"].attach(done)
            elif event == "dx_first":
                *dx_arrived, done = lax.optimization_barrier((*dx_arrived, done))
                dx_half = [
                    [add(x[i], y[i]).astype(BF16) for x, y in zip(dx_keeps, dx_arrived)]
                    for i in range(2)
                ]
                *dx_half[0], done = lax.optimization_barrier((*dx_half[0], dx_half[1][-1]))
            elif event == "dx_start":
                dx_arrived = swap_step(after(dx_sends[-1], done), 2)
            elif event == "dx":
                dx_arrived = after(dx_arrived, done)
                half_kept, half_sent = [
                    jnp.stack(dx_half[i] + [add(dx_keeps[-1][i], dx_arrived[i]).astype(BF16)])
                    for i in range(2)
                ]
                dx_last = swap_step(half_sent, 3)
                done = half_sent
            elif event == "post":
                input_grad = call(
                    post_kernel,
                    (1,),
                    (),
                    (half_kept, after(dx_last, done), block_input, gain_attn_row, *grad_middles),
                    [whole(half_kept.shape)] * 2 + [whole(own), line] + [whole(one)] * count,
                    [shaped(own, BF16)],
                    [whole(own)],
                    name="post",
                )[0]
                done = input_grad
            else:
                which, name = event.split("_")
                done = finish(name, which == "own", done)
        (grad_outer,), (grad_inner,) = grads["outer"], grads["inner"]
        grad_out, grad_query, grad_key, grad_value = grads["small"]
        rider = chains["small"].rider

        return (
            block_output,
            input_grad,
            rider[8],
            grad_query,
            grad_key,
            grad_value,
            grad_out,
            rider[9],
            grad_inner,
            grad_outer,
            rider[:H, :BUCKETS].T,
        )

    return body


def solution(mesh):
    split = P("rows", "seq", None)
    placed = (split, split) + (P(),) * 9 + (P("rows", None), P("rows", "seq"))
    return jax.shard_map(
        make_body(mesh.shape["rows"], mesh.shape["seq"]),
        mesh=mesh,
        in_specs=placed,
        out_specs=(split, split) + (P(),) * 9,
        check_vma=False,
    )
```

```python
import functools
import math

import jax
import jax.numpy as jnp
from jax import lax
from jax.experimental import pallas as pl
from jax.experimental.pallas import tpu as pltpu
from jax.sharding import PartitionSpec as P

D = 512
FF = 2048
H = 8
HD = 64
PAIRS = H // 2
BUCKETS = 32
PACKED_LENGTH = 512
EPSILON = 1e-06
BUCKET_EDGES = (12, 16, 23, 32, 46, 64, 91)
SPAN = 2 * PACKED_LENGTH
CHUNKS = 32
HALF = CHUNKS // 2
OUTER_ROWS = FF // CHUNKS
SMALL_ROWS = D // CHUNKS
HALF_FF = FF // 2
MASKED = -1000000000.0
MIB = 1024 * 1024
F32 = jnp.float32
BF16 = jnp.bfloat16


SMALL_HALVINGS = 3
BEFORE_ROW = 2
EARLY = ("outer", "inner", )
ORDER = (
    "outer",
    "small_start",
    "rider",
    "inner",
    "outer",
    "small",
    "dx_first",
    "inner",
    "outer",
    "inner",
    "small",
    "small",
    "dx_start",
    "small",
    "outer",
    "inner",
    "outer",
    "small",
    "dx",
    "inner",
    "outer",
    "small",
    "small",
    "post",
    "inner",
    "all_outer",
    "all_inner",
    "small",
    "own_small",
    "other_small",
)


def dot(left, right, contract=(1, 0), precision=None):
    return lax.dot_general(
        left,
        right,
        (((contract[0],), (contract[1],)), ((), ())),
        preferred_element_type=F32,
        precision=precision,
    )


def dot_ones(values, ones, contract, swapped=False):
    high = values.astype(BF16)
    low = (values - high.astype(F32)).astype(BF16)
    if swapped:
        return dot(ones, high, contract) + dot(ones, low, contract)
    return dot(high, ones, contract) + dot(low, ones, contract)


def bucket_of(relative):
    distance = jnp.abs(relative)
    beyond = jnp.full(distance.shape, 8, jnp.int32)
    for edge_value in BUCKET_EDGES:
        beyond = beyond + (distance >= edge_value).astype(jnp.int32)
    near = jnp.where(distance < 8, distance, beyond)
    return jnp.where(relative > 0, 16, 0).astype(jnp.int32) + near


def bucket_rows(shape, bucket_axis):
    place_axis = 1 - bucket_axis
    relative = lax.broadcasted_iota(jnp.int32, shape, place_axis) - PACKED_LENGTH
    return (bucket_of(relative) == lax.broadcasted_iota(jnp.int32, shape, bucket_axis)).astype(F32)


def split_heads(pair):
    lane = lax.broadcasted_iota(jnp.int32, pair.shape, 1)
    zero = jnp.zeros_like(pair)
    return jnp.concatenate(
        [jnp.where(lane < HD, pair, zero), jnp.where(lane >= HD, pair, zero)], axis=0
    )


def join_heads(stacked):
    half = stacked.shape[0] // 2
    lane = lax.broadcasted_iota(jnp.int32, (half, stacked.shape[1]), 1)
    return jnp.where(lane < HD, stacked[:half], stacked[half:])


def pack_kernel(x_ref, seen_ref, *out_refs, here, rows, tail):
    count = x_ref.shape[0]
    for out_ref, group in zip(out_refs, rows):
        for place, row in enumerate(group):
            out_ref[place * here : (place + 1) * here] = x_ref[row]
    if tail:
        flags = seen_ref[...].astype(F32)
        flags = jnp.concatenate([flags, jnp.zeros((16 - count, here), F32)], axis=0)
        flags = jnp.concatenate([flags, jnp.zeros((16, D - here), F32)], axis=1)
        out_refs[0][len(rows[0]) * here :] = flags.astype(BF16)


def split_kernel(wire_ref, *out_refs, here):
    for row, out_ref in enumerate(out_refs):
        out_ref[:here] = wire_ref[row * here : (row + 1) * here]
    out_refs[0][here:] = wire_ref[len(out_refs) * here :]


def prepare_kernel(place_ref, table_ref, *refs, here, seq):
    count = (len(refs) - 3) // 2
    sources, bias_ref, targets = refs[:count], refs[count], refs[count + 1 : 2 * count + 1]
    line_ref, sems = refs[2 * count + 1 :]
    copies = [
        pltpu.make_async_copy(source, target, sems.at[i])
        for i, (source, target) in enumerate(zip(sources, targets))
    ]
    for copy in copies:
        copy.start()
    line_ref[...] = dot(
        table_ref[...], bucket_rows((BUCKETS, SPAN), 0), (0, 0), lax.Precision.HIGHEST
    )
    me = place_ref[0]
    for block in range(seq):
        offset = ((me ^ block) - me) * here + PACKED_LENGTH - here
        window = line_ref[:, pl.ds(pl.multiple_of(offset, 128), 2 * here)]
        for head in range(H):
            spread = jnp.broadcast_to(window[head : head + 1], (here, 2 * here))
            skewed = pltpu.roll(spread, here, 1, stride=1, stride_axis=0)
            row = (head % 2) * here
            bias_ref[head // 2, row : row + here, block * here : (block + 1) * here] = skewed[
                :, :here
            ]
    for copy in copies:
        copy.wait()


def attention_kernel(
    place_ref,
    lengths_ref,
    code_ref,
    x0_ref,
    x1_ref,
    x2_ref,
    x3_ref,
    seen_ref,
    x1_tail_ref,
    x2_tail_ref,
    x3_tail_ref,
    gain_ref,
    gain_mlp_ref,
    bias_ref,
    wq_ref,
    wk_ref,
    wv_ref,
    w_out_ref,
    *refs,
    row,
    here,
    seq,
    fetch,
):
    if fetch:
        copies = [
            pltpu.make_async_copy(refs[i], refs[i - 4], refs[-1].at[i]) for i in range(3)
        ]
        for copy in copies:
            copy.start()
        refs = refs[:-4]
    (
        normed_mlp_ref,
        attended_ref,
        middle_ref,
        mixed_ref,
        normed_ref,
        q_ref,
        k_ref,
        v_ref,
        p_ref,
    ) = refs[-9:]
    me = place_ref[0]
    own_x = x0_ref[0].astype(F32)
    x = jnp.concatenate(
        [own_x] + [ref.astype(F32) for ref in (x1_ref[...], x2_ref[...], x3_ref[...])], axis=0
    )
    inv = lax.rsqrt(jnp.mean(x * x, -1, keepdims=True) + EPSILON)
    normed = (x * inv * gain_ref[...]).astype(BF16)
    normed_ref[...] = normed
    q = dot(normed[:here], wq_ref[...]).astype(BF16)
    k = dot(normed, wk_ref[...]).astype(BF16)
    v = dot(normed, wv_ref[...]).astype(BF16)
    q_ref[...] = q
    k_ref[...] = k
    v_ref[...] = v
    ends = [lengths_ref[row, 0]]
    for part in range(1, lengths_ref.shape[1]):
        ends.append(ends[-1] + lengths_ref[row, part])

    def segment(place):
        total = jnp.zeros(place.shape, jnp.int32)
        for end in ends:
            total = total + (end <= place).astype(jnp.int32)
        return total

    query_place = me * here + lax.broadcasted_iota(jnp.int32, (here, 1), 0)
    lane = lax.broadcasted_iota(jnp.int32, (1, here), 1)
    key_place = jnp.concatenate([(me ^ block) * here + lane for block in range(seq)], axis=1)
    seen = jnp.concatenate(
        [seen_ref[row : row + 1].astype(F32)]
        + [
            ref[...].astype(F32)[row : row + 1, :here]
            for ref in (x1_tail_ref, x2_tail_ref, x3_tail_ref)
        ],
        axis=1,
    )
    key_segment = jnp.where(seen == 1.0, segment(key_place), -1)
    allowed = (segment(query_place) == key_segment) | (query_place == key_place)
    allowed = jnp.concatenate([allowed.astype(jnp.int32)] * 2, axis=0) == 1
    attended = []
    for pair in range(PAIRS):
        lanes = slice(pair * 2 * HD, (pair + 1) * 2 * HD)
        scores = dot(split_heads(q[:, lanes]), k[:, lanes], (1, 1)) + bias_ref[pair]
        scores = jnp.where(allowed, scores, MASKED)
        exponent = jnp.exp(scores - jnp.max(scores, -1, keepdims=True))
        ones = jnp.ones((PACKED_LENGTH, 128), BF16)
        both = dot(exponent.astype(BF16), jnp.concatenate([v[:, lanes], ones], axis=1))
        share = 1.0 / both[:, 128:]
        mixed = join_heads(both[:, :128] * share)
        for first in range(0, PACKED_LENGTH, 128):
            part = slice(first, first + 128)
            p_ref[pair, :, part] = (exponent[:, part] * share).astype(BF16)
        mixed_ref[:, lanes] = mixed
        attended.append(mixed.astype(BF16))
    attended = jnp.concatenate(attended, axis=1)
    attended_ref[...] = attended
    middle = own_x + dot(attended, w_out_ref[...])
    middle_ref[...] = middle
    inv = lax.rsqrt(jnp.mean(middle * middle, -1, keepdims=True) + EPSILON)
    normed_mlp_ref[...] = (middle * inv * gain_mlp_ref[...]).astype(BF16)
    if fetch:
        for copy in copies:
            copy.wait()


def gelu_both(u):
    scale = 0.7978845608028654
    square = u * u
    t = jnp.tanh(u * (scale + (scale * 0.044715) * square))
    half_up = 0.5 + 0.5 * t
    slope = half_up + (0.5 * u) * (1.0 - t * t) * (scale + (3.0 * 0.044715 * scale) * square)
    return u * half_up, slope


def mlp_kernel(code_ref, *refs, rows, own_half):
    nm_refs = refs[:rows]
    g_ref, w_inner_ref, w_outer_ref = refs[rows : rows + 3]
    refs = refs[rows + 3 :]
    total_ref, back_ref, outer_ref, inner_ref = refs
    label = code_ref[1] if own_half else code_ref[2]
    normed = jnp.concatenate([ref[...] for ref in nm_refs], axis=0)
    g = g_ref[...].reshape(normed.shape)
    half = code_ref[0] if own_half else 1 - code_ref[0]
    hidden = pl.ds(pl.multiple_of(half * HALF_FF, HALF_FF), HALF_FF)
    w_inner = w_inner_ref[:, hidden]
    w_outer = w_outer_ref[hidden, :]
    active_f, slope = gelu_both(dot(normed, w_inner))
    active = active_f.astype(BF16)
    grad_act = (dot(g, w_outer, (1, 1)) * slope).astype(BF16)
    total_ref[...] = dot(active, w_outer)
    back_ref[...] = dot(grad_act, w_inner, (1, 1))
    outer = dot(active, g, (0, 0)).astype(BF16)
    inner = dot(grad_act, normed, (0, 0)).astype(BF16)
    for part in range(HALF):
        slot = part ^ label
        rows = slice(part * OUTER_ROWS, (part + 1) * OUTER_ROWS)
        outer_ref[slot] = outer[rows]
        inner_ref[slot] = inner[rows]


def back_kernel(place_ref, code_ref, *refs, row, last, here, seq):
    _, attended_ref, middle_ref, mixed_ref, normed_ref, q_ref, k_ref, v_ref, p_ref = refs[:9]
    (
        g_ref,
        total_a_ref,
        total_b_ref,
        back_a_ref,
        back_b_ref,
        gain_mlp_ref,
        w_out_ref,
        wq_ref,
        wk_ref,
        wv_ref,
        _,
    ) = refs[9:20]
    refs = refs[20:]
    old = refs[:6] if row else None
    refs = refs[6:] if row else refs
    if row:
        refs = refs[1:]
    block_output_ref, grad_middle_ref, dx_keep_ref, dx_send_ref = refs[:4]
    sums = refs[4:10]
    if last:
        keep_ref, send_ref = refs[10:12]

    def accumulate(which, value, part=None):
        if part is None:
            sums[which][...] = value + old[which][...] if row else value
        else:
            sums[which][part] = value + old[which][part] if row else value

    index = row
    tokens = slice(index * here, (index + 1) * here)
    middle = middle_ref[...]
    back = back_a_ref[tokens] + back_b_ref[tokens]
    block_output_ref[0] = (middle + total_a_ref[tokens] + total_b_ref[tokens]).astype(BF16)
    inv = lax.rsqrt(jnp.mean(middle * middle, -1, keepdims=True) + EPSILON)
    accumulate(5, jnp.sum(back * middle * inv, axis=0, keepdims=True))
    scaled = back * gain_mlp_ref[...]
    grad_middle = (
        g_ref[row].astype(F32)
        + inv * scaled
        - middle * (inv * inv * inv) * jnp.mean(scaled * middle, -1, keepdims=True)
    )
    grad_middle_ref[...] = grad_middle
    branch = grad_middle.astype(BF16)
    ga = dot(branch, w_out_ref[...], (1, 1)).astype(BF16)

    accumulate(0, dot(attended_ref[...], branch, (0, 0)))
    q = q_ref[...]
    k = k_ref[...]
    v = v_ref[...]
    normed = normed_ref[...]
    dq, dkt, dvt = [], [], []
    for pair in range(PAIRS):
        lanes = slice(pair * 2 * HD, (pair + 1) * 2 * HD)
        ga_split = split_heads(ga[:, lanes])
        q_split = split_heads(q[:, lanes])
        mixed = mixed_ref[:, lanes]
        probs = p_ref[pair]
        delta = jnp.sum(
            ga_split.astype(F32) * jnp.concatenate([mixed, mixed], axis=0), -1, keepdims=True
        )
        grad_probs = dot(ga_split, v[:, lanes], (1, 1))
        grad_scores_f = probs.astype(F32) * (grad_probs - delta)
        accumulate(4, grad_scores_f, pair)
        grad_scores = grad_scores_f.astype(BF16)
        dq.append(join_heads(dot(grad_scores, k[:, lanes])).astype(BF16))
        dkt.append(dot(q_split, grad_scores, (0, 0)).astype(BF16))
        dvt.append(dot(ga_split, probs, (0, 0)).astype(BF16))
    dq = jnp.concatenate(dq, axis=1)
    dkt = jnp.concatenate(dkt, axis=0)
    dvt = jnp.concatenate(dvt, axis=0)
    chunks = [slice(first, first + 128) for first in range(0, D, 128)]
    pieces = [[] for _ in range(seq)]
    for rows in chunks:
        dxt = dot(wk_ref[rows], dkt) + dot(wv_ref[rows], dvt)
        own = dxt[:, :here] + dot(wq_ref[rows], dq, (1, 1))
        pieces[0].append(own.astype(BF16))
        for block in range(1, seq):
            pieces[block].append(dxt[:, block * here : (block + 1) * here].astype(BF16))
    pieces = [jnp.concatenate(piece, axis=0) for piece in pieces]
    dx_keep_ref[0] = pieces[0]
    dx_send_ref[1] = pieces[3]

    @pl.when(code_ref[0] == 0)
    def _():
        dx_keep_ref[1] = pieces[2]
        dx_send_ref[0] = pieces[1]

    @pl.when(code_ref[0] == 1)
    def _():
        dx_keep_ref[1] = pieces[1]
        dx_send_ref[0] = pieces[2]

    accumulate(1, dot(normed[:here], dq, (0, 0)))
    for rows in chunks:
        accumulate(2, dot(dkt[rows], normed), rows)
        accumulate(3, dot(dvt[rows], normed), rows)

    if not last:
        return
    go_ref, gq_ref, gk_ref, gv_ref = sums[:4]
    gk_ref[...] = gk_ref[...].T
    gv_ref[...] = gv_ref[...].T
    core, label, other = code_ref[0], code_ref[1], code_ref[2]
    for index, grad_ref in enumerate((go_ref, gq_ref, gk_ref, gv_ref)):
        for slot in range(HALF):
            chunk = core * HALF + (slot ^ label)
            first = pl.multiple_of(chunk * SMALL_ROWS, SMALL_ROWS)
            rows_to = slice(index * SMALL_ROWS, (index + 1) * SMALL_ROWS)
            keep_ref[slot, rows_to] = grad_ref[pl.ds(first, SMALL_ROWS), :].astype(BF16)
            chunk = (1 - core) * HALF + (slot ^ other)
            first = pl.multiple_of(chunk * SMALL_ROWS, SMALL_ROWS)
            send_ref[slot, rows_to] = grad_ref[pl.ds(first, SMALL_ROWS), :].astype(BF16)


def rider_kernel(
    place_ref,
    gq_ref,
    gk_ref,
    gv_ref,
    table_sum_ref,
    gain_mlp_ref,
    gain_attn_ref,
    wq_ref,
    wk_ref,
    wv_ref,
    rider_ref,
    line_ref,
    *,
    here,
    seq,
):
    me = place_ref[0]
    line_ref[...] = jnp.zeros_like(line_ref)
    for block in range(seq):
        offset = ((me ^ block) - me) * here + PACKED_LENGTH - here
        window = pl.ds(pl.multiple_of(offset, 128), 2 * here)
        for head in range(H):
            row = (head % 2) * here
            tile = table_sum_ref[head // 2, row : row + here, block * here : (block + 1) * here]
            total = jnp.zeros((8, 2 * here), F32)
            empty = jnp.zeros((8, here), F32)
            for group in range(here // 8):
                wide = jnp.concatenate([tile[group * 8 : group * 8 + 8], empty], axis=1)
                total = total + pltpu.roll(wide, here - 8 * group, 1)
            line_ref[head * 8 : head * 8 + 8, window] += total
    lines = line_ref[...]
    sub = lax.broadcasted_iota(jnp.int32, lines.shape, 0)
    for bit in (1, 2, 4):
        lines = jnp.where((sub & bit) != 0, pltpu.roll(lines, SPAN - bit, 1), lines)
    by_head = jnp.concatenate(
        [jnp.sum(lines[h * 8 : h * 8 + 8], axis=0, keepdims=True) for h in range(H)], axis=0
    )
    table = dot_ones(by_head, bucket_rows((SPAN, 128), 1).astype(BF16), (1, 0))
    gain = (
        wq_ref[...].astype(F32) * gq_ref[...]
        + wk_ref[...].astype(F32) * gk_ref[...]
        + wv_ref[...].astype(F32) * gv_ref[...]
    )
    gain_grad = dot_ones(gain, jnp.ones((8, D), BF16), (1, 1), True)
    rider = jnp.concatenate(
        [
            jnp.concatenate([table, jnp.zeros((8, D - 128), F32)], axis=1),
            gain_grad[:1] / gain_attn_ref[...],
            gain_mlp_ref[...],
            jnp.zeros((6, D), F32),
        ],
        axis=0,
    )
    rider_ref[...] = rider


def finish_mlp_kernel(code_ref, own_ref, other_ref, out_ref, stage_ref, sems, *, turned):
    core, label, other = code_ref[0], code_ref[1], code_ref[2]
    groups = stage_ref.shape[0] // 2
    per_group = HALF // groups
    size = per_group * OUTER_ROWS
    copies = []
    for index, (half, ref, code) in enumerate(((core, own_ref, label), (1 - core, other_ref, other))):
        for group in range(groups):
            slots = [(group * per_group + i) ^ code for i in range(per_group)]
            piece = jnp.concatenate([ref[slot].astype(F32) for slot in slots], axis=0)
            stage = index * groups + group
            stage_ref[stage] = piece.T if turned else piece
            place = pl.ds(pl.multiple_of((half * groups + group) * size, size), size)
            target = out_ref.at[:, place] if turned else out_ref.at[place]
            copies.append(pltpu.make_async_copy(stage_ref.at[stage], target, sems.at[stage]))
            copies[-1].start()
    for copy in copies:
        copy.wait()


def finish_attention_kernel(code_ref, half_ref, *refs, own_half):
    out_refs, stage_ref, sems = refs[-6:-2], refs[-2], refs[-1]
    half = code_ref[0] if own_half else 1 - code_ref[0]
    label = code_ref[1] if own_half else code_ref[2]
    place = pl.ds(pl.multiple_of(half * (D // 2), D // 2), D // 2)
    copies = []
    for index, out_ref in enumerate(out_refs):
        part = slice(index * SMALL_ROWS, (index + 1) * SMALL_ROWS)
        for slot in range(HALF):
            rows = slice(slot * SMALL_ROWS, (slot + 1) * SMALL_ROWS)
            stage_ref[index, rows] = half_ref[slot ^ label, part].astype(F32)
        copies.append(
            pltpu.make_async_copy(stage_ref.at[index], out_ref.at[place], sems.at[index])
        )
        copies[-1].start()
    for copy in copies:
        copy.wait()


def post_kernel(a_ref, b_ref, x_ref, gain_ref, *refs):
    grad_middle_refs, out_ref = refs[:-1], refs[-1]
    for row, grad_middle_ref in enumerate(grad_middle_refs):
        back = (a_ref[row].astype(F32) + b_ref[row].astype(F32)).T
        x = x_ref[row].astype(F32)
        inv = lax.rsqrt(jnp.mean(x * x, -1, keepdims=True) + EPSILON)
        scaled = back * gain_ref[...]
        grad = inv * scaled - x * (inv * inv * inv) * jnp.mean(scaled * x, -1, keepdims=True)
        out_ref[row] = (grad_middle_ref[...] + grad).astype(BF16)


ANYWHERE = pl.BlockSpec(memory_space=pl.ANY)


def whole(shape):
    return pl.BlockSpec(shape, lambda *_: (0,) * len(shape))


def by_row(shape):
    return pl.BlockSpec((1,) + shape[1:], lambda i, *_: (i,) + (0,) * (len(shape) - 1))


def one_row(shape, row):
    return pl.BlockSpec((1,) + shape[1:], lambda *_: (row,) + (0,) * (len(shape) - 1))


def shaped(shape, dtype):
    return jax.ShapeDtypeStruct(shape, dtype)


def call(
    kernel,
    grid,
    prefetch,
    inputs,
    in_specs,
    outs,
    out_specs,
    scratch=(),
    flops=0,
    name=None,
    aliases=None,
    vmem=16,
):
    return pl.pallas_call(
        kernel,
        out_shape=outs,
        grid_spec=pltpu.PrefetchScalarGridSpec(
            num_scalar_prefetch=len(prefetch),
            grid=grid,
            in_specs=in_specs,
            out_specs=out_specs,
            scratch_shapes=list(scratch),
        ),
        compiler_params=pltpu.CompilerParams(
            dimension_semantics=("arbitrary",) * len(grid), vmem_limit_bytes=vmem * MIB
        ),
        cost_estimate=pl.CostEstimate(flops=flops, bytes_accessed=flops // 256, transcendentals=0),
        input_output_aliases=aliases or {},
        name=name,
    )(*prefetch, *inputs)


def add(*parts):
    total = parts[0].astype(F32)
    for part in parts[1:]:
        total = total + part.astype(F32)
    return total


def make_body(rows, seq):
    both = ("rows", "seq")
    further = [1 << i for i in range(3, rows.bit_length() - 1)]

    def swap_rows(array, bit):
        return lax.ppermute(array, "rows", [(i, i ^ bit) for i in range(rows)])

    def swap_seq(array, bit):
        return lax.ppermute(array, "seq", [(i, i ^ bit) for i in range(seq)])

    def swap_step(array, step):
        def partner(r, z):
            first, second = ((0, 2), (0, 4)), ((1, 1), (1, 2))
            if r & 1:
                first, second = first[::-1], second[::-1]
            axis, bit = (first + second)[step]
            return (r, z ^ bit) if axis else (r ^ bit, z)

        pairs = []
        for r in range(rows):
            for z in range(seq):
                to_r, to_z = partner(r, z)
                pairs.append((r * seq + z, to_r * seq + to_z))
        return lax.ppermute(array, both, pairs)

    def codes():
        r, z = lax.axis_index("rows"), lax.axis_index("seq")
        core = r & 1
        b1, b2, z0, z1 = (r >> 1) & 1, (r >> 2) & 1, z & 1, (z >> 1) & 1
        even = b1 * 8 + b2 * 4 + z0 * 2 + z1
        odd = b2 * 8 + b1 * 4 + z1 * 2 + z0
        label = jnp.where(core == 0, even, odd)
        other = jnp.where(core == 0, odd, even)
        return jnp.stack([core, label, other]).astype(jnp.int32)

    def after(array, *earlier):
        return lax.optimization_barrier((array, *earlier))[0]

    def two_parts(rider):
        high = rider.astype(BF16)
        return [high, (rider - high.astype(F32)).astype(BF16)]

    class Reduction:
        def __init__(self, wire, shape, halvings):
            self.rider = self.side = None
            self.slots, self.rows_each = shape[:2]
            self.halvings = halvings
            self.step = 0
            self.spreading = False
            self.parts = [None]
            self.arrived = swap_rows(wire, 1)

        def attach(self, rider):
            self.rider = rider
            self.side = swap_rows(jnp.concatenate(two_parts(rider), axis=0), 1)

        def send(self, outgoing):
            if self.rider is not None:
                flat = outgoing.reshape(-1, D)
                outgoing = jnp.concatenate([flat] + two_parts(self.rider), axis=0)
            self.slots = outgoing.shape[0] if self.rider is None else flat.shape[0] // self.rows_each
            self.arrived = swap_step(outgoing, self.step)
            self.step += 1

        def receive(self, earlier):
            array = after(self.arrived, *earlier)
            if self.rider is not None:
                size = self.slots * self.rows_each
                extra = (array[size:] if self.side is None else self.side).astype(F32)
                high, low = two_parts(self.rider)
                self.rider = (high.astype(F32) + low.astype(F32)) + (extra[:16] + extra[16:])
                if self.side is None:
                    array = array[:size].reshape(self.slots, self.rows_each, D)
                self.side = None
            return array

        def advance(self, *earlier):
            if self.spreading:
                held = jnp.concatenate([self.held, after(self.arrived, *earlier)])
            else:
                self.parts.append(self.receive(earlier))
                if self.step < self.halvings:
                    size = self.parts[0].shape[0] // 2
                    outgoing = add(*[part[size:] for part in self.parts]).astype(BF16)
                    self.parts = [part[:size] for part in self.parts]
                    self.send(outgoing)
                    return outgoing
                held = add(*self.parts)
                if self.step < 4:
                    held = held.astype(BF16)
                    size = 8 >> self.step
                    order = [slot ^ size for slot in range(held.shape[0])]
                    self.parts = [held]
                    self.send(jnp.concatenate([held[slot : slot + 1] for slot in order]))
                    return held
                for bit in further:
                    held = held + swap_rows(held, bit)
                    if self.rider is not None:
                        self.rider = self.rider + swap_rows(self.rider, bit)
                held = held.astype(BF16)
                self.spreading = True
                self.step = self.halvings
            self.held = held
            self.step -= 1
            if self.step >= 0:
                self.arrived = swap_step(held, self.step)
            else:
                self.arrived = swap_rows(held, 1)
            return held

    def body(
        block_input,
        cotangent,
        gain_attn,
        w_query,
        w_key,
        w_value,
        w_out,
        gain_mlp,
        w_inner,
        outer_weight,
        bias_table,
        lengths,
        observed,
    ):
        count, here = block_input.shape[0], block_input.shape[1]
        tokens = count * here
        last = count - 1
        place = lax.axis_index("seq").astype(jnp.int32).reshape(1)
        code = codes()
        gain_attn_row = gain_attn.reshape(1, D)
        gain_mlp_row = gain_mlp.reshape(1, D)

        def in_hbm(array):
            return pltpu.with_memory_space_constraint(array, pltpu.HBM)

        stacked = (PAIRS, 2 * here, PACKED_LENGTH)
        one = (here, D)
        own = (count, here, D)
        full = (PACKED_LENGTH, D)
        square = whole((D, D))
        line = whole((1, D))

        def pack(rows, tail, *pins):
            shapes = [(len(group) * here + (16 if tail and not i else 0), D) for i, group in enumerate(rows)]
            return call(
                functools.partial(pack_kernel, here=here, rows=rows, tail=tail),
                (1,),
                (),
                (in_hbm(block_input), in_hbm(after(observed, *pins))),
                [whole(own), whole(observed.shape)],
                [shaped(shape, BF16) for shape in shapes],
                [whole(shape) for shape in shapes],
                name="pack",
                vmem=8,
            )

        wire = pack([list(range(count))], True)[0]
        x2 = swap_seq(wire, 2)
        x1 = swap_seq(wire, 1)
        x2 = call(
            functools.partial(split_kernel, here=here),
            (1,),
            (),
            (x2,),
            [whole(wire.shape)],
            [shaped((here + 16, D), BF16)] + [shaped(one, BF16)] * (count - 1),
            [whole((here + 16, D))] + [whole(one)] * (count - 1),
            name="split",
            vmem=4,
        )
        *x2, bias_table = lax.optimization_barrier((*x2, bias_table))
        x3 = [swap_seq(x, 1) for x in x2]
        resident = (w_query, w_key, w_value, w_out)
        resident = call(
            functools.partial(prepare_kernel, here=here, seq=seq),
            (1,),
            (place,),
            (bias_table, *[in_hbm(array) for array in resident]),
            [whole(bias_table.shape)] + [ANYWHERE] * len(resident),
            [pltpu.VMEM(stacked, F32)]
            + [pltpu.VMEM(array.shape, array.dtype) for array in resident],
            [whole(stacked)] + [whole(array.shape) for array in resident],
            [pltpu.VMEM((H, SPAN), F32), pltpu.SemaphoreType.DMA((len(resident),))],
            name="prepare",
            vmem=4,
        )
        kept = []
        kept_shapes = [
            pltpu.VMEM(one, BF16),
            pltpu.VMEM(one, BF16),
            pltpu.VMEM(one, F32),
            pltpu.VMEM(one, F32),
            pltpu.VMEM(full, BF16),
            pltpu.VMEM(one, BF16),
            pltpu.VMEM(full, BF16),
            pltpu.VMEM(full, BF16),
            pltpu.VMEM(stacked, BF16),
        ]
        fetched_shapes = [pltpu.VMEM(shape, BF16) for shape in ((D, FF), (FF, D), own)]
        mlp_sources = [in_hbm(array) for array in (w_inner, outer_weight, cotangent)]
        for row in range(count):
            fetch = row == count - 1
            shapes = kept_shapes + (fetched_shapes if fetch else [])
            outs = call(
                functools.partial(attention_kernel, row=row, here=here, seq=seq, fetch=fetch),
                (1,),
                (place, lengths, code),
                [block_input, x1, x2[row], x3[row], observed, x1, x2[0], x3[0]]
                + [gain_attn_row, gain_mlp_row, *resident, *(mlp_sources if fetch else [])],
                [
                    one_row(own, row),
                    pl.BlockSpec(one, lambda *_, row=row: (row, 0)),
                    whole(one),
                    whole(one),
                    whole(observed.shape),
                    pl.BlockSpec((16, D), lambda *_: (tokens // 16, 0)),
                    pl.BlockSpec((16, D), lambda *_: (here // 16, 0)),
                    pl.BlockSpec((16, D), lambda *_: (here // 16, 0)),
                ]
                + [line] * 2
                + [whole(stacked)]
                + [square] * 4
                + [ANYWHERE] * (3 if fetch else 0),
                [pltpu.VMEM(array.shape, array.dtype) for array in resident] + shapes,
                [ANYWHERE] * len(resident) + [whole(shape.shape) for shape in shapes],
                [pltpu.SemaphoreType.DMA((3,))] if fetch else [],
                flops=8 * here * D * PACKED_LENGTH,
                name="attention",
                vmem=12,
                aliases={13 + i: i for i in range(len(resident))},
            )
            resident = outs[: len(resident)]
            kept.append(tuple(outs[len(resident) : len(resident) + len(kept_shapes)]))
            fetched = outs[len(resident) + len(kept_shapes) :]
        _, w_query, w_key, w_value, w_out = resident
        normed_mlp = [part[0] for part in kept]

        flat = (tokens, D)
        part_shape = (HALF, OUTER_ROWS, D)

        def mlp_part(own_half, nm):
            shapes = [pltpu.VMEM(flat, F32)] * 2 + [pltpu.VMEM(part_shape, BF16)] * 2
            return call(
                functools.partial(mlp_kernel, rows=count, own_half=own_half),
                (1,),
                (code,),
                [*nm, cotangent, *fetched],
                [whole(one)] * count + [whole(own), whole((D, FF)), whole((FF, D))],
                shapes,
                [whole(shape.shape) for shape in shapes],
                flops=6 * tokens * D * FF,
                name="mlp",
                vmem=16,
            )

        *fetched, cotangent = fetched
        total_a, back_a, outer_send, inner_send = mlp_part(False, normed_mlp)
        chains = {
            "outer": Reduction(outer_send, part_shape, 3),
            "inner": Reduction(inner_send, part_shape, 3),
        }
        nm = [after(normed_mlp[0], total_a)] + normed_mlp[1:]
        total_b, back_b, outer_keep, inner_keep = mlp_part(True, nm)
        chains["outer"].parts[0] = outer_keep
        chains["inner"].parts[0] = inner_keep

        small_half = (HALF, 4 * SMALL_ROWS, D)
        done = chains["outer"].advance()
        done = chains["inner"].advance(done)
        dx_half = (seq // 2, D, here)
        sum_shapes = [pltpu.VMEM((D, D), F32)] * 4
        sum_shapes += [pltpu.VMEM(stacked, F32), pltpu.VMEM((1, D), F32)]
        sums, block_output = (), ()
        grad_middles, dx_keeps, dx_sends = [], [], []
        for row in range(count):
            end = row == count - 1
            inputs = [*kept[row], cotangent, total_a, total_b, back_a, back_b, gain_mlp_row]
            inputs += [w_out, w_query, w_key, w_value, done, *sums]
            specs = [whole(shape.shape) for shape in kept_shapes] + [whole(own)]
            specs += [whole(flat)] * 4 + [line] + [square] * 4 + [ANYWHERE]
            specs += [whole(shape.shape) for shape in sum_shapes[: len(sums)]]
            if row:
                inputs.append(block_output)
                specs.append(ANYWHERE)
            aliases = {len(inputs) + 1: 0} if row else {}
            outs = [pltpu.HBM(own, BF16), pltpu.VMEM(one, F32)] + [pltpu.VMEM(dx_half, BF16)] * 2
            out_specs = [one_row(own, row), whole(one)] + [whole(dx_half)] * 2
            outs += sum_shapes
            out_specs += [whole(shape.shape) for shape in sum_shapes]
            if row:
                aliases |= {22 + i: 4 + i for i in range(len(sums))}
            if end:
                outs += [pltpu.VMEM(small_half, BF16)] * 2
                out_specs += [whole(small_half)] * 2
            block_output, grad_middle, dx_keep, dx_send, *sums = call(
                functools.partial(back_kernel, row=row, last=end, here=here, seq=seq),
                (1,),
                (place, code),
                inputs,
                specs,
                outs,
                out_specs,
                flops=20 * here * D * PACKED_LENGTH,
                name="attention_back",
                vmem=16,
                aliases=aliases,
            )
            done = grad_middle
            if row == BEFORE_ROW - 1:
                for event in EARLY:
                    done = chains[event].advance(done)
            grad_middles.append(grad_middle)
            dx_keeps.append(dx_keep)
            dx_sends.append(dx_send)
        *sums, small_keep, small_send = sums

        def make_rider(pin):
            _, gq, gk, gv, table_sum, gain_mlp_sum = sums
            return call(
                functools.partial(rider_kernel, here=here, seq=seq),
                (1,),
                (place,),
                (gq, gk, gv, table_sum, after(gain_mlp_sum, pin), gain_attn_row)
                + (w_query, w_key, w_value),
                [square] * 3 + [whole(stacked)] + [line] * 2 + [square] * 3,
                [pltpu.VMEM((16, D), F32)],
                [whole((16, D))],
                [pltpu.VMEM((8 * H, SPAN), F32)],
                name="rider",
                vmem=8,
            )[0]

        dx_arrived = [swap_step(dx_send, 2) for dx_send in dx_sends[:-1]]

        grads = {}

        def finish_mlp(name, pin):
            chain = chains[name]
            turned = name == "inner"
            groups = 2
            size = HALF_FF // groups
            stage = (2 * groups, D, size) if turned else (2 * groups, size, D)
            return call(
                functools.partial(finish_mlp_kernel, turned=turned),
                (1,),
                (code,),
                (chain.held, after(chain.arrived, pin)),
                [whole(part_shape)] * 2,
                [pltpu.HBM((D, FF) if turned else (FF, D), F32)],
                [ANYWHERE],
                [pltpu.VMEM(stage, F32), pltpu.SemaphoreType.DMA((2 * groups,))],
                name="finish_" + name,
                vmem=12,
            )

        def finish_small(own_half, pin):
            chain = chains["small"]
            before = grads.get("small", ())
            half = after(chain.held if own_half else chain.arrived, pin)
            return call(
                functools.partial(finish_attention_kernel, own_half=own_half),
                (1,),
                (code,),
                (half, *before),
                [whole(half.shape)] + [ANYWHERE] * len(before),
                [pltpu.HBM((D, D), F32)] * 4,
                [ANYWHERE] * 4,
                [pltpu.VMEM((4, D // 2, D), F32), pltpu.SemaphoreType.DMA((4,))],
                name="finish_small",
                vmem=10,
                aliases={2 + i: i for i in range(len(before))},
            )

        for event in ORDER:
            if event in chains:
                done = chains[event].advance(done)
            elif event == "small_start":
                chains["small"] = Reduction(after(small_send, done), small_half, SMALL_HALVINGS)
                chains["small"].parts[0] = small_keep
            elif event == "rider":
                done = make_rider(done)
                chains["small"].attach(done)
            elif event == "dx_first":
                *dx_arrived, done = lax.optimization_barrier((*dx_arrived, done))
                dx_half = [
                    [add(x[i], y[i]).astype(BF16) for x, y in zip(dx_keeps, dx_arrived)]
                    for i in range(2)
                ]
                *dx_half[0], done = lax.optimization_barrier((*dx_half[0], dx_half[1][-1]))
            elif event == "dx_start":
                dx_arrived = swap_step(after(dx_sends[-1], done), 2)
            elif event == "dx":
                dx_arrived = after(dx_arrived, done)
                half_kept, half_sent = [
                    jnp.stack(dx_half[i] + [add(dx_keeps[-1][i], dx_arrived[i]).astype(BF16)])
                    for i in range(2)
                ]
                dx_last = swap_step(half_sent, 3)
                done = half_sent
            elif event == "post":
                input_grad = call(
                    post_kernel,
                    (1,),
                    (),
                    (half_kept, after(dx_last, done), block_input, gain_attn_row, *grad_middles),
                    [whole(half_kept.shape)] * 2 + [whole(own), line] + [whole(one)] * count,
                    [shaped(own, BF16)],
                    [whole(own)],
                    name="post",
                )[0]
                done = input_grad
            else:
                which, name = event.split("_")
                if name == "small":
                    grads[name] = finish_small(which == "own", done)
                else:
                    grads[name] = finish_mlp(name, done)
                done = grads[name][0]
        (grad_outer,), (grad_inner,) = grads["outer"], grads["inner"]
        grad_out, grad_query, grad_key, grad_value = grads["small"]
        rider = chains["small"].rider

        return (
            block_output,
            input_grad,
            rider[8],
            grad_query,
            grad_key,
            grad_value,
            grad_out,
            rider[9],
            grad_inner,
            grad_outer,
            rider[:H, :BUCKETS].T,
        )

    return body


def solution(mesh):
    split = P("rows", "seq", None)
    placed = (split, split) + (P(),) * 9 + (P("rows", None), P("rows", "seq"))
    return jax.shard_map(
        make_body(mesh.shape["rows"], mesh.shape["seq"]),
        mesh=mesh,
        in_specs=placed,
        out_specs=(split, split) + (P(),) * 9,
        check_vma=False,
    )
```
